32 devices in a mesh: lon: 8 (over y, x, core), lat: 4 (over z).
Axes of the slice: x: 2, y: 2, z: 4, core: 2. Of those that a mesh axis runs over, the one named last changes fastest.
Arguments:
- tracers: float32 [12, 256, 4096], P(None, 'lat', 'lon'), may hold values from -6 to 6
- lon_shift: int32 [2, 12, 256], P(None, None, 'lat'), may hold values from -127 to 127, as said below
- lon_frac: float32 [2, 12, 256], P(None, None, 'lat'), may hold values from 0 to 1
- lat_shift: int32 [2, 12, 256], P(None, None, 'lat'), may hold values from -1 to 1
- lat_frac: float32 [2, 12, 256], P(None, None, 'lat'), may hold values from 0 to 1
- remap_frac: float32 [2, 12, 256], P(None, None, 'lat'), may hold values from 0 to 1
- diffusivity: float32 [12, 256], P(None, 'lat'), may hold values from 0.1 to 3
Outputs:
- advected: float32 [12, 256, 4096], P(None, 'lat', 'lon')
The draws below stay inside these ranges and needn't reach their ends.
Inputs may be any that keep to these rules, and one draw needn't show every extreme that they name: In latitude row j, with e = |2 * j - 255|, |lon_shift| is at most min(127, 64 * 256 // (257 - e)).
All inputs are finite; a program needn't handle non-finite values.
Results may differ from the reference program's by a relative error of at most 0.00002.
Values sent between devices are 32-bit elements; how exact they have to be, the bound alone decides.
No kernel may reach another device: no remote copies, remote signals or barrier semaphores. Data moves between devices by JAX's collectives and lax.ppermute only.
A program may use at most 64 MiB of HBM per device.

```python
import math
import jax
import jax.numpy as jnp

NTR = 8
LEV = 12
STEPS = 2
CLON = 64
NLON = 512
NLAT = 256


def draw_lon_shift(key, part):
    row_index = jnp.arange(NLAT, dtype=jnp.int32)
    distance = jnp.abs(2 * row_index + 1 - NLAT)
    ceiling = NLON // 4 - 1
    limits = jnp.minimum(ceiling, CLON * NLAT // (NLAT + 1 - distance))
    limits = jnp.broadcast_to(limits[None, None, :], (STEPS, LEV, NLAT)).astype(jnp.int32)
    drawn = jax.random.randint(key, (STEPS, LEV, NLAT), -limits, limits + 1, dtype=jnp.int32)
    drawn = drawn.at[0, 0, 0].set(ceiling)
    drawn = drawn.at[0, 0, NLAT - 1].set(-ceiling)
    return drawn


def with_ends(values, own_key, least, high):
    longest = values.shape.index(max(values.shape))
    spots = []
    for shift in (0, 1):
        where = [jax.random.randint(jax.random.fold_in(own_key, axis), (), 0, length) for axis, length in enumerate(values.shape)]
        where[longest] = (where[longest] + shift) % values.shape[longest]
        spots.append(tuple(where))
    return values.at[spots[0]].set(least).at[spots[1]].set(high)


def block_levels(own_key, shape, pieces, smallest, largest):
    factor_of, own = 1.0, jax.random.fold_in(own_key, 6)
    for dim, blocks in pieces:
        steps = jnp.exp(jax.random.uniform(jax.random.fold_in(own, dim), (blocks,), jnp.float32, smallest / len(pieces), largest / len(pieces)))
        factor_of = factor_of * jnp.repeat(steps, shape[dim] // blocks).reshape([-1 if axis == dim else 1 for axis in range(len(shape))])
    return factor_of


def normal_values(key, shape, spread, most, cuts=(), held_as=jnp.bfloat16):
    loudness = block_levels(key, shape, cuts, -0.22, 0.18) if cuts else 1.0
    array = jax.random.normal(key, shape, jnp.float32) * spread * loudness
    return jnp.minimum(jnp.maximum(array, -most), most).astype(held_as)


def setup_inputs(seed: int = 0) -> dict:
    seeds = jax.random.split(jax.random.key(seed), 8)
    return {
        "tracers": normal_values(seeds[0], (LEV, NLAT, NLON * NTR), 1.0, 6.0, ((1, 4), (2, 8)), jnp.float32),
        "lon_shift": draw_lon_shift(jax.random.fold_in(seeds[7], 71), 0),
        "lon_frac": jnp.clip(1.0 * jax.random.uniform(seeds[2], (STEPS, LEV, NLAT), jnp.float32) ** block_levels(seeds[2], (STEPS, LEV, NLAT), ((2, 4),), -0.2, 0.2), 0.0, 1.0),
        "lat_shift": with_ends(jax.random.randint(seeds[3], (STEPS, LEV, NLAT), -1, 2), jax.random.fold_in(seeds[3], 1), -1, 1).astype(jnp.int32),
        "lat_frac": jnp.clip(1.0 * jax.random.uniform(seeds[4], (STEPS, LEV, NLAT), jnp.float32) ** block_levels(seeds[4], (STEPS, LEV, NLAT), ((2, 4),), -0.2, 0.2), 0.0, 1.0),
        "remap_frac": jnp.clip(1.0 * jax.random.uniform(seeds[5], (STEPS, LEV, NLAT), jnp.float32) ** block_levels(seeds[5], (STEPS, LEV, NLAT), ((2, 4),), -0.2, 0.2), 0.0, 1.0),
        "diffusivity": jnp.clip(jnp.exp(math.log(3.0) - 3.4011974 * jax.random.uniform(seeds[6], (LEV, NLAT), jnp.float32) ** block_levels(seeds[6], (LEV, NLAT), ((1, 4),), -0.2, 0.2)), 0.1, 3.0),
    }


def cubic_weights(fraction):
    w_zero = -fraction * (fraction - 1.0) * (fraction - 2.0) / 6.0
    w_one = (fraction + 1.0) * (fraction - 1.0) * (fraction - 2.0) / 2.0
    w_two = -(fraction + 1.0) * fraction * (fraction - 2.0) / 2.0
    w_three = (fraction + 1.0) * fraction * (fraction - 1.0) / 6.0
    return (w_zero, w_one, w_two, w_three)


def lat_step(padded, offset, fraction, row_count):
    weights = cubic_weights(fraction)
    summed = None
    for place_index in range(6):
        row_delta = place_index - 2
        coeff = jnp.zeros_like(fraction)
        for tap_index in range(4):
            coeff = coeff + jnp.where(offset == (tap_index - 1) - row_delta, weights[tap_index], 0.0)
        addend = coeff[:, :, None] * padded[:, 1 + place_index: 1 + place_index + row_count, :]
        summed = addend if summed is None else summed + addend
    return summed


def lon_step(wrapped, fraction, tracer_count):
    weights = cubic_weights(fraction)
    width_cols = wrapped.shape[2] - 4 * tracer_count
    summed = None
    for tap_index in range(4):
        offset_cols = (1 + tap_index) * tracer_count
        addend = weights[tap_index][:, :, None] * wrapped[:, :, offset_cols: offset_cols + width_cols]
        summed = addend if summed is None else summed + addend
    return summed


def remap(tracer_field, fraction):
    level_above = jnp.concatenate([tracer_field[1:], tracer_field[-1:]], axis=0)
    return (1.0 - fraction)[:, :, None] * tracer_field + fraction[:, :, None] * level_above


def diffuse(tracer_field, kappa):
    levels = tracer_field.shape[0]
    face_kappa = 0.5 * (kappa[:-1] + kappa[1:])
    zero_face = jnp.zeros_like(kappa[:1])
    face_below = jnp.concatenate([zero_face, face_kappa], axis=0)
    face_above = jnp.concatenate([face_kappa, zero_face], axis=0)
    ratio_prev = jnp.zeros_like(kappa[0])
    solved_prev = jnp.zeros_like(tracer_field[0])
    ratios = []
    solveds = []
    for level_index in range(levels):
        below = face_below[level_index]
        above = face_above[level_index]
        pivot_value = 1.0 + below + above + below * ratio_prev
        ratio_now = -above / pivot_value
        solved_now = (tracer_field[level_index] + below[:, None] * solved_prev) / pivot_value[:, None]
        ratios.append(ratio_now)
        solveds.append(solved_now)
        ratio_prev = ratio_now
        solved_prev = solved_now
    results = [None] * levels
    results[levels - 1] = solveds[levels - 1]
    for level_index in range(levels - 2, -1, -1):
        results[level_index] = solveds[level_index] - ratios[level_index][:, None] * results[level_index + 1]
    return jnp.stack(results, axis=0)


def reference(tracers, lon_shift, lon_frac, lat_shift, lat_frac, remap_frac, diffusivity):
    tracer_field = tracers
    for time_step in range(STEPS):
        padded = jnp.pad(tracer_field, ((0, 0), (3, 3), (0, 0)))
        tracer_field = lat_step(padded, lat_shift[time_step], lat_frac[time_step], NLAT)
        split_view = tracer_field.reshape(LEV, NLAT, NLON, NTR)
        cell_index = jnp.arange(NLON, dtype=jnp.int32)
        source = jnp.remainder(cell_index[None, None, :] - lon_shift[time_step][:, :, None], NLON).astype(jnp.int32)
        source = jnp.broadcast_to(source[:, :, :, None], split_view.shape)
        shifted = jnp.take_along_axis(split_view, source, axis=2).reshape(LEV, NLAT, NLON * NTR)
        wrapped = jnp.concatenate([shifted[:, :, -2 * NTR:], shifted, shifted[:, :, :2 * NTR]], axis=2)
        tracer_field = lon_step(wrapped, lon_frac[time_step], NTR)
        tracer_field = remap(tracer_field, remap_frac[time_step])
        tracer_field = diffuse(tracer_field, diffusivity)
    return tracer_field
```

```python
import jax
import jax.numpy as jnp
from jax import lax
from jax.experimental import pallas as pl
from jax.experimental.pallas import tpu as pltpu
from jax.sharding import PartitionSpec as P

NTR = 8
STEPS = 2


def from_behind(x, axis, by):
    peers = lax.axis_size(axis)
    return lax.ppermute(x, axis, [(i, (i + by) % peers) for i in range(peers)])


def with_halo(block, sides, width, periodic):
    for axis, dim in sides:
        count = lax.axis_size(axis)
        forward = [(i, i + 1) for i in range(count - 1)]
        if periodic:
            forward.append((count - 1, 0))
        backward = [(target, source) for source, target in forward]
        low = lax.ppermute(
            lax.slice_in_dim(block, block.shape[dim] - width, None, axis=dim), axis, forward
        )
        high = lax.ppermute(lax.slice_in_dim(block, 0, width, axis=dim), axis, backward)
        block = jnp.concatenate([low, block, high], axis=dim)
    return block


def cubic_weights(fraction):
    w_zero = -fraction * (fraction - 1.0) * (fraction - 2.0) / 6.0
    w_one = (fraction + 1.0) * (fraction - 1.0) * (fraction - 2.0) / 2.0
    w_two = -(fraction + 1.0) * fraction * (fraction - 2.0) / 2.0
    w_three = (fraction + 1.0) * fraction * (fraction - 1.0) / 6.0
    return (w_zero, w_one, w_two, w_three)


def lat_step(padded, offset, fraction, row_count):
    weights = cubic_weights(fraction)
    summed = None
    for place_index in range(6):
        row_delta = place_index - 2
        coeff = jnp.zeros_like(fraction)
        for tap_index in range(4):
            coeff = coeff + jnp.where(offset == tap_index - 1 - row_delta, weights[tap_index], 0.0)
        addend = coeff[:, :, None] * padded[:, 1 + place_index : 1 + place_index + row_count, :]
        summed = addend if summed is None else summed + addend
    return summed


def lon_step(wrapped, fraction, tracer_count):
    weights = cubic_weights(fraction)
    width_cols = wrapped.shape[2] - 4 * tracer_count
    summed = None
    for tap_index in range(4):
        offset_cols = (1 + tap_index) * tracer_count
        addend = (
            weights[tap_index][:, :, None] * wrapped[:, :, offset_cols : offset_cols + width_cols]
        )
        summed = addend if summed is None else summed + addend
    return summed


def remap(tracer_field, fraction):
    level_above = jnp.concatenate([tracer_field[1:], tracer_field[-1:]], axis=0)
    return (1.0 - fraction)[:, :, None] * tracer_field + fraction[:, :, None] * level_above


def diffuse(tracer_field, kappa):
    levels = tracer_field.shape[0]
    face_kappa = 0.5 * (kappa[:-1] + kappa[1:])
    zero_face = jnp.zeros_like(kappa[:1])
    face_below = jnp.concatenate([zero_face, face_kappa], axis=0)
    face_above = jnp.concatenate([face_kappa, zero_face], axis=0)
    ratio_prev = jnp.zeros_like(kappa[0])
    solved_prev = jnp.zeros_like(tracer_field[0])
    ratios = []
    solveds = []
    for level_index in range(levels):
        below = face_below[level_index]
        above = face_above[level_index]
        pivot_value = 1.0 + below + above + below * ratio_prev
        ratio_now = -above / pivot_value
        solved_now = (tracer_field[level_index] + below[:, None] * solved_prev) / pivot_value[
            :, None
        ]
        ratios.append(ratio_now)
        solveds.append(solved_now)
        ratio_prev = ratio_now
        solved_prev = solved_now
    results = [None] * levels
    results[levels - 1] = solveds[levels - 1]
    for level_index in range(levels - 2, -1, -1):
        results[level_index] = (
            solveds[level_index] - ratios[level_index][:, None] * results[level_index + 1]
        )
    return jnp.stack(results, axis=0)


def bit_mask(amount, position):
    return (amount // 2**position % 2 == 1)[:, :, None]


def move_rows(tracer_field, shift_cells):
    tracer_count = NTR
    width_cols = tracer_field.shape[2]
    cell_count = width_cols // tracer_count
    devices = lax.axis_size("lon")
    low_bits = cell_count.bit_length() - 1
    ahead_amount = jnp.remainder(shift_cells, cell_count * devices)
    high_bits = devices.bit_length() - 1
    current = tracer_field
    for position in range(low_bits):
        step_cols = 2**position * tracer_count
        from_west = from_behind(current[:, :, width_cols - step_cols :], "lon", 1)
        forward = jnp.concatenate([from_west, current[:, :, : width_cols - step_cols]], axis=2)
        current = jnp.where(bit_mask(ahead_amount, position), forward, current)
    for position in range(high_bits):
        hops = 2**position
        digit = low_bits + position
        ahead_block = from_behind(current, "lon", hops)
        current = jnp.where(bit_mask(ahead_amount, digit), ahead_block, current)
    return current


def per_device(tracers, lon_shift, lon_frac, lat_shift, lat_frac, remap_frac, diffusivity):
    tracer_field = tracers
    row_count = tracer_field.shape[1]
    for time_step in range(STEPS):
        padded = with_halo(tracer_field, (("lat", 1),), 3, False)
        tracer_field = lat_step(padded, lat_shift[time_step], lat_frac[time_step], row_count)
        shifted = move_rows(tracer_field, lon_shift[time_step])
        wrapped = with_halo(shifted, (("lon", 2),), 2 * NTR, True)
        tracer_field = lon_step(wrapped, lon_frac[time_step], NTR)
        tracer_field = remap(tracer_field, remap_frac[time_step])
        tracer_field = diffuse(tracer_field, diffusivity)
    return tracer_field


LANES = 128
TILE = 8
PLANES = 4
LOW = 2
HIGH = 3


def lane_index():
    return lax.broadcasted_iota(jnp.int32, (TILE, LANES), 1)


def pick(values, index):
    return jnp.take_along_axis(values, index, axis=1)


def swap_blocks(items, masks):
    for bit, mask in enumerate(masks):
        items = [
            jnp.where(mask, items[place ^ (1 << bit)], items[place])
            for place in range(len(items))
        ]
    return items


def lane_masks(lane, first, count):
    return [(lane >> (first + bit)) & 1 == 1 for bit in range(count)]


def pack_kernel(field_ref, *message_refs):
    me = lax.axis_index("lon")
    lane = lane_index()
    cell_masks = lane_masks(lane, 2, 2)
    device_masks = lane_masks(lane, 4, 3)
    base = ((lane & 3) << 5) | (((lane >> 2) & 3) << 3) | ((lane >> 4) ^ me)

    def level(k, carry):
        by_tile = []
        for tile in range(8):
            rows = slice(TILE * tile, TILE * tile + TILE)
            parts = [
                pick(field_ref[k, rows, LANES * q : LANES * q + LANES], base ^ ((q << 3) | tile))
                for q in range(PLANES)
            ]
            by_tile.append(swap_blocks(parts, cell_masks))
        for plane in range(PLANES):
            sent = swap_blocks([parts[plane] for parts in by_tile], device_masks)
            for mate in range(8):
                message_refs[mate][k, plane] = sent[mate]
        return carry

    lax.fori_loop(0, field_ref.shape[0], level, 0)


def unpack_kernel(*refs):
    message_refs, field_ref = refs[:8], refs[8]
    me = lax.axis_index("lon")
    lane = lane_index()
    cell_masks = lane_masks(lane, 2, 2)
    device_masks = lane_masks(lane, 4, 3)
    base = (((lane & 7) ^ me) << 4) | (((lane >> 3) & 3) << 2) | (lane >> 5)

    def level(k, carry):
        by_plane = [
            swap_blocks([ref[k, plane] for ref in message_refs], device_masks)
            for plane in range(PLANES)
        ]
        for tile in range(8):
            rows = slice(TILE * tile, TILE * tile + TILE)
            parts = swap_blocks([planes[tile] for planes in by_plane], cell_masks)
            for q in range(PLANES):
                field_ref[k, rows, LANES * q : LANES * q + LANES] = pick(
                    parts[q], base ^ ((tile << 4) | (q << 2))
                )
        return carry

    lax.fori_loop(0, field_ref.shape[0], level, 0)


def put_edges(k, plane, first, last, up_ref, down_ref):
    up_ref[pl.ds((k * PLANES + plane) * HIGH, HIGH), :] = first[:HIGH]
    down_ref[pl.ds((k * PLANES + plane) * LOW, LOW), :] = last[TILE - LOW :]


def gather_kernel(*refs):
    message_refs, (moved_ref, up_ref, down_ref) = refs[:8], refs[8:]
    me = lax.axis_index("lon")
    lane = lane_index()
    device_masks = lane_masks(lane, 4, 3)
    base = lane ^ (me << 4)

    def level(k, carry):
        for plane in range(PLANES):
            tiles = swap_blocks([ref[k, plane] for ref in message_refs], device_masks)
            tiles = [
                pick(values, base ^ ((tile << 4) | (plane << 2)))
                for tile, values in enumerate(tiles)
            ]
            for tile, values in enumerate(tiles):
                moved_ref[k, plane, TILE * tile : TILE * tile + TILE, :] = values
            put_edges(k, plane, tiles[0], tiles[-1], up_ref, down_ref)
        return carry

    lax.fori_loop(0, moved_ref.shape[0], level, 0)


def advance(field_ref, low_ref, high_ref, coeff_ref, padded, moved, step, put):
    levels, _, rows, _ = field_ref.shape
    tiles = rows // TILE
    lane = lane_index()

    def level(k, carry):
        for plane in range(PLANES):
            place = k * PLANES + plane
            padded[k, plane, TILE - LOW : TILE, :] = low_ref[pl.ds(place * LOW, LOW), :]
            padded[k, plane, TILE : TILE + rows, :] = field_ref[k, plane]
            padded[k, plane, TILE + rows : TILE + rows + HIGH, :] = high_ref[
                pl.ds(place * HIGH, HIGH), :
            ]
        for tile in range(tiles):
            start = TILE * tile
            own = coeff_ref[k, start : start + TILE, :]

            def coeff(which):
                which = which + 16 * step
                return jnp.broadcast_to(own[:, which : which + 1], (TILE, LANES))

            weights = [coeff(which) for which in range(LOW + HIGH + 1)]
            planes = []
            for plane in range(PLANES):
                summed = None
                for which, weight in enumerate(weights):
                    first = TILE + start + which - LOW
                    addend = weight * padded[k, plane, first : first + TILE, :]
                    summed = addend if summed is None else summed + addend
                planes.append(summed)
            shift = coeff(10).astype(jnp.int32)
            bit = shift & 1 == 1
            behind = [pltpu.roll(planes[3], 1, 1)] + planes[:3]
            planes = [jnp.where(bit, a, b) for a, b in zip(behind, planes)]
            bit = shift & 2 == 2
            behind = [pltpu.roll(planes[2], 1, 1), pltpu.roll(planes[3], 1, 1)] + planes[:2]
            planes = [jnp.where(bit, a, b) for a, b in zip(behind, planes)]
            index = (lane - (shift >> 2)) & (LANES - 1)
            planes = [pick(values, index) for values in planes]
            wide = (
                [pltpu.roll(planes[3], 1, 1)]
                + planes
                + [pltpu.roll(planes[0], LANES - 1, 1), pltpu.roll(planes[1], LANES - 1, 1)]
            )
            taps = [coeff(which) for which in range(6, 10)]
            for plane in range(PLANES):
                summed = taps[0] * wide[plane]
                for which in range(1, 4):
                    summed = summed + taps[which] * wide[plane + which]
                moved[k, plane, start : start + TILE, :] = summed
        return carry

    lax.fori_loop(0, levels, level, 0)

    def column(tile, carry):
        rows_of = pl.ds(pl.multiple_of(TILE * tile, TILE), TILE)
        own = [coeff_ref[k, rows_of, :] for k in range(levels)]

        def coeff(k, which):
            which = which + 16 * step
            return jnp.broadcast_to(own[k][:, which : which + 1], (TILE, LANES))

        solved = [[None] * PLANES for _ in range(levels)]
        values = [moved[0, plane, rows_of, :] for plane in range(PLANES)]
        for k in range(levels):
            above = values
            if k + 1 < levels:
                above = [moved[k + 1, plane, rows_of, :] for plane in range(PLANES)]
            c_own, c_above, c_before = coeff(k, 11), coeff(k, 12), coeff(k, 13)
            for plane in range(PLANES):
                now = c_own * values[plane] + c_above * above[plane]
                if k:
                    now = now + c_before * solved[k - 1][plane]
                solved[k][plane] = now
            values = above
        for k in range(levels - 2, -1, -1):
            c_next = coeff(k, 14)
            for plane in range(PLANES):
                solved[k][plane] = solved[k][plane] + c_next * solved[k + 1][plane]
        for k in range(levels):
            for plane in range(PLANES):
                put(k, plane, rows_of, solved[k][plane])
        return carry

    lax.fori_loop(0, tiles, column, 0)


def first_kernel(
    field_ref, low_ref, high_ref, coeff_ref, next_ref, up_ref, down_ref, padded, moved
):
    def put(k, plane, rows_of, values):
        next_ref[k, plane, rows_of, :] = values

    advance(field_ref, low_ref, high_ref, coeff_ref, padded, moved, 0, put)

    def level(k, carry):
        for plane in range(PLANES):
            first = next_ref[k, plane, :TILE, :]
            last = next_ref[k, plane, next_ref.shape[2] - TILE :, :]
            put_edges(k, plane, first, last, up_ref, down_ref)
        return carry

    lax.fori_loop(0, next_ref.shape[0], level, 0)


def second_kernel(field_ref, low_ref, high_ref, coeff_ref, *refs):
    message_refs, (padded, moved) = refs[:8], refs[8:]
    me = lax.axis_index("lon")
    lane = lane_index()
    device_masks = lane_masks(lane, 4, 3)
    base = lane ^ (me << 4)

    def put(k, plane, rows_of, values):
        moved[k, plane, rows_of, :] = values

    advance(field_ref, low_ref, high_ref, coeff_ref, padded, moved, 1, put)

    def level(k, carry):
        for plane in range(PLANES):
            tiles = [
                pick(
                    moved[k, plane, TILE * tile : TILE * tile + TILE, :],
                    base ^ ((tile << 4) | (plane << 2)),
                )
                for tile in range(8)
            ]
            for mate, values in enumerate(swap_blocks(tiles, device_masks)):
                message_refs[mate][k, plane] = values
        return carry

    lax.fori_loop(0, moved.shape[0], level, 0)


def coefficients(lon_shift, lon_frac, lat_shift, lat_frac, remap_frac, diffusivity):
    face = 0.5 * (diffusivity[:-1] + diffusivity[1:])
    zero = jnp.zeros_like(diffusivity[:1])
    below = jnp.concatenate([zero, face], axis=0)
    above = jnp.concatenate([face, zero], axis=0)
    ratio = jnp.zeros_like(diffusivity[0])
    pivots, ratios = [], []
    for k in range(diffusivity.shape[0]):
        pivot = 1.0 + below[k] + above[k] + below[k] * ratio
        ratio = -above[k] / pivot
        pivots.append(pivot)
        ratios.append(ratio)
    pivot = jnp.stack(pivots)
    back = -jnp.stack(ratios)
    lat_weights = cubic_weights(lat_frac)
    columns = []
    for row_delta in range(-LOW, HIGH + 1):
        coeff = jnp.zeros_like(lat_frac)
        for tap in range(4):
            coeff = coeff + jnp.where(lat_shift == tap - 1 - row_delta, lat_weights[tap], 0.0)
        columns.append(coeff)
    columns.extend(cubic_weights(lon_frac))
    columns.append(lon_shift.astype(jnp.float32))
    columns.append((1.0 - remap_frac) / pivot)
    columns.append(remap_frac / pivot)
    columns.append(jnp.broadcast_to(below / pivot, lat_frac.shape))
    columns.append(jnp.broadcast_to(back, lat_frac.shape))
    columns.append(jnp.zeros_like(lat_frac))
    stacked = jnp.stack(columns, axis=-1)
    return jnp.concatenate([stacked[0], stacked[1]], axis=-1)


def call(kernel, out_shapes, scratch=()):
    return pl.pallas_call(
        kernel,
        out_shape=[jax.ShapeDtypeStruct(shape, jnp.float32) for shape in out_shapes],
        scratch_shapes=[pltpu.VMEM(shape, jnp.float32) for shape in scratch],
        compiler_params=pltpu.CompilerParams(vmem_limit_bytes=40 * 2**20),
    )


def exchange(messages):
    peers = lax.axis_size("lon")
    received = [messages[0]]
    for mate in range(1, peers):
        received.append(lax.ppermute(messages[mate], "lon", [(i, i ^ mate) for i in range(peers)]))
    return received


def exchange_rows(up, down):
    count = lax.axis_size("lat")
    high = lax.ppermute(up, "lat", [(i + 1, i) for i in range(count - 1)])
    low = lax.ppermute(down, "lat", [(i, i + 1) for i in range(count - 1)])
    return low, high


def by_tracer(tracers, lon_shift, lon_frac, lat_shift, lat_frac, remap_frac, diffusivity):
    levels, rows, _ = tracers.shape
    block = (levels, PLANES, rows, LANES)
    message = (levels, PLANES, TILE, LANES)
    edges = [(levels * PLANES * HIGH, LANES), (levels * PLANES * LOW, LANES)]
    scratch = [(levels, PLANES, rows + 2 * TILE, LANES), block]
    coeff = coefficients(lon_shift, lon_frac, lat_shift, lat_frac, remap_frac, diffusivity)
    messages = call(pack_kernel, [message] * 8)(tracers)
    field, up, down = call(gather_kernel, [block] + edges)(*exchange(messages))
    low, high = exchange_rows(up, down)
    field, up, down = call(first_kernel, [block] + edges, scratch)(field, low, high, coeff)
    low, high = exchange_rows(up, down)
    messages = call(second_kernel, [message] * 8, scratch)(field, low, high, coeff)
    return call(unpack_kernel, [tracers.shape])(*exchange(messages))[0]


def solution(mesh):
    in_specs = (
        P(None, "lat", "lon"),
        P(None, None, "lat"),
        P(None, None, "lat"),
        P(None, None, "lat"),
        P(None, None, "lat"),
        P(None, None, "lat"),
        P(None, "lat"),
    )
    out_specs = P(None, "lat", "lon")
    def per_part(tracers, *fields):
        _, rows, columns = tracers.shape
        fits = mesh.shape["lon"] == NTR and columns == PLANES * LANES and rows == TILE * NTR
        return (by_tracer if fits else per_device)(tracers, *fields)

    return jax.shard_map(
        per_part, mesh=mesh, in_specs=in_specs, out_specs=out_specs, check_vma=False
    )
```

```python
import functools

import jax
import jax.numpy as jnp
from jax import lax
from jax.experimental import pallas as pl
from jax.experimental.pallas import tpu as pltpu
from jax.sharding import PartitionSpec as P

NTR = 8
STEPS = 2


def from_behind(x, axis, by):
    peers = lax.axis_size(axis)
    return lax.ppermute(x, axis, [(i, (i + by) % peers) for i in range(peers)])


def with_halo(block, sides, width, periodic):
    for axis, dim in sides:
        count = lax.axis_size(axis)
        forward = [(i, i + 1) for i in range(count - 1)]
        if periodic:
            forward.append((count - 1, 0))
        backward = [(target, source) for source, target in forward]
        low = lax.ppermute(
            lax.slice_in_dim(block, block.shape[dim] - width, None, axis=dim), axis, forward
        )
        high = lax.ppermute(lax.slice_in_dim(block, 0, width, axis=dim), axis, backward)
        block = jnp.concatenate([low, block, high], axis=dim)
    return block


def cubic_weights(fraction):
    w_zero = -fraction * (fraction - 1.0) * (fraction - 2.0) / 6.0
    w_one = (fraction + 1.0) * (fraction - 1.0) * (fraction - 2.0) / 2.0
    w_two = -(fraction + 1.0) * fraction * (fraction - 2.0) / 2.0
    w_three = (fraction + 1.0) * fraction * (fraction - 1.0) / 6.0
    return (w_zero, w_one, w_two, w_three)


def lat_step(padded, offset, fraction, row_count):
    weights = cubic_weights(fraction)
    summed = None
    for place_index in range(6):
        row_delta = place_index - 2
        coeff = jnp.zeros_like(fraction)
        for tap_index in range(4):
            coeff = coeff + jnp.where(offset == tap_index - 1 - row_delta, weights[tap_index], 0.0)
        addend = coeff[:, :, None] * padded[:, 1 + place_index : 1 + place_index + row_count, :]
        summed = addend if summed is None else summed + addend
    return summed


def lon_step(wrapped, fraction, tracer_count):
    weights = cubic_weights(fraction)
    width_cols = wrapped.shape[2] - 4 * tracer_count
    summed = None
    for tap_index in range(4):
        offset_cols = (1 + tap_index) * tracer_count
        addend = (
            weights[tap_index][:, :, None] * wrapped[:, :, offset_cols : offset_cols + width_cols]
        )
        summed = addend if summed is None else summed + addend
    return summed


def remap(tracer_field, fraction):
    level_above = jnp.concatenate([tracer_field[1:], tracer_field[-1:]], axis=0)
    return (1.0 - fraction)[:, :, None] * tracer_field + fraction[:, :, None] * level_above


def diffuse(tracer_field, kappa):
    levels = tracer_field.shape[0]
    face_kappa = 0.5 * (kappa[:-1] + kappa[1:])
    zero_face = jnp.zeros_like(kappa[:1])
    face_below = jnp.concatenate([zero_face, face_kappa], axis=0)
    face_above = jnp.concatenate([face_kappa, zero_face], axis=0)
    ratio_prev = jnp.zeros_like(kappa[0])
    solved_prev = jnp.zeros_like(tracer_field[0])
    ratios = []
    solveds = []
    for level_index in range(levels):
        below = face_below[level_index]
        above = face_above[level_index]
        pivot_value = 1.0 + below + above + below * ratio_prev
        ratio_now = -above / pivot_value
        solved_now = (tracer_field[level_index] + below[:, None] * solved_prev) / pivot_value[
            :, None
        ]
        ratios.append(ratio_now)
        solveds.append(solved_now)
        ratio_prev = ratio_now
        solved_prev = solved_now
    results = [None] * levels
    results[levels - 1] = solveds[levels - 1]
    for level_index in range(levels - 2, -1, -1):
        results[level_index] = (
            solveds[level_index] - ratios[level_index][:, None] * results[level_index + 1]
        )
    return jnp.stack(results, axis=0)


def bit_mask(amount, position):
    return (amount // 2**position % 2 == 1)[:, :, None]


def move_rows(tracer_field, shift_cells):
    tracer_count = NTR
    width_cols = tracer_field.shape[2]
    cell_count = width_cols // tracer_count
    devices = lax.axis_size("lon")
    low_bits = cell_count.bit_length() - 1
    ahead_amount = jnp.remainder(shift_cells, cell_count * devices)
    high_bits = devices.bit_length() - 1
    current = tracer_field
    for position in range(low_bits):
        step_cols = 2**position * tracer_count
        from_west = from_behind(current[:, :, width_cols - step_cols :], "lon", 1)
        forward = jnp.concatenate([from_west, current[:, :, : width_cols - step_cols]], axis=2)
        current = jnp.where(bit_mask(ahead_amount, position), forward, current)
    for position in range(high_bits):
        hops = 2**position
        digit = low_bits + position
        ahead_block = from_behind(current, "lon", hops)
        current = jnp.where(bit_mask(ahead_amount, digit), ahead_block, current)
    return current


def per_device(tracers, lon_shift, lon_frac, lat_shift, lat_frac, remap_frac, diffusivity):
    tracer_field = tracers
    row_count = tracer_field.shape[1]
    for time_step in range(STEPS):
        padded = with_halo(tracer_field, (("lat", 1),), 3, False)
        tracer_field = lat_step(padded, lat_shift[time_step], lat_frac[time_step], row_count)
        shifted = move_rows(tracer_field, lon_shift[time_step])
        wrapped = with_halo(shifted, (("lon", 2),), 2 * NTR, True)
        tracer_field = lon_step(wrapped, lon_frac[time_step], NTR)
        tracer_field = remap(tracer_field, remap_frac[time_step])
        tracer_field = diffuse(tracer_field, diffusivity)
    return tracer_field


LANES = 128
TILE = 8
PLANES = 4
LOW = 2
HIGH = 3
TAPS = LOW + HIGH + 1
OUTER = (0, 1, 6, 7)
INNER = (2, 3, 4, 5)
PAD = TILE
COEFFS = 14
MESH_LON = "lon"


def lane_index():
    return lax.broadcasted_iota(jnp.int32, (TILE, LANES), 1)


def pick(values, index):
    return jnp.take_along_axis(values, index, axis=1)


def swap_blocks(items, masks):
    for bit, mask in enumerate(masks):
        items = [
            jnp.where(mask, items[place ^ (1 << bit)], items[place])
            for place in range(len(items))
        ]
    return items


def lane_masks(lane, first, count):
    return [(lane >> (first + bit)) & 1 == 1 for bit in range(count)]


def at(tile, offset=0):
    return slice(TILE * tile + offset, TILE * tile + offset + TILE)


def row_runs(tiles):
    runs = []
    for place, tile in enumerate(tiles):
        if runs and tiles[place - 1] + 1 == tile:
            runs[-1][2] += 1
        else:
            runs.append([tile, place, 1])
    return [(TILE * tile, TILE * place, TILE * count) for tile, place, count in runs]


def pack_kernel(tiles, field_ref, *refs):
    message_refs, (held, sems) = refs[:8], refs[8:]
    levels = held.shape[0]
    runs = row_runs(tiles)

    def copies(k):
        return [
            pltpu.make_async_copy(
                field_ref.at[k, pl.ds(source, count), :],
                held.at[k, pl.ds(target, count), :],
                sems.at[k, which],
            )
            for which, (source, target, count) in enumerate(runs)
        ]

    def begin(k, carry):
        for copy in copies(k):
            copy.start()
        return carry

    lax.fori_loop(0, levels, begin, 0)
    me = lax.axis_index(MESH_LON)
    lane = lane_index()
    cell_masks = lane_masks(lane, 2, 2)
    device_masks = lane_masks(lane, 4, 3)
    base = ((lane & 3) << 5) | (((lane >> 2) & 3) << 3) | ((lane >> 4) ^ me)

    def unit(u, carry):
        by_group = []
        for group in range(8):
            k = 2 * u + group // 4
            if group % 4 == 0:
                for copy in copies(k):
                    copy.wait()
            parts = [
                pick(
                    held[k, at(group % 4), LANES * q : LANES * q + LANES],
                    base ^ ((q << 3) | group),
                )
                for q in range(PLANES)
            ]
            by_group.append(swap_blocks(parts, cell_masks))
        for plane in range(PLANES):
            sent = swap_blocks([parts[plane] for parts in by_group], device_masks)
            for mate in range(8):
                message_refs[mate][u, plane] = sent[mate]
        return carry

    lax.fori_loop(0, levels // 2, unit, 0)


def unpack_kernel(tiles, *refs):
    message_refs, (field_ref, held, sems) = refs[:8], refs[-3:]
    levels = held.shape[0]
    runs = row_runs(tiles)

    def copies(k):
        return [
            pltpu.make_async_copy(
                held.at[k, pl.ds(source, count), :],
                field_ref.at[k, pl.ds(target, count), :],
                sems.at[k, which],
            )
            for which, (target, source, count) in enumerate(runs)
        ]

    me = lax.axis_index(MESH_LON)
    lane = lane_index()
    cell_masks = lane_masks(lane, 2, 2)
    device_masks = lane_masks(lane, 4, 3)
    base = (((lane & 7) ^ me) << 4) | (((lane >> 3) & 3) << 2) | (lane >> 5)

    def unit(u, carry):
        by_plane = [
            swap_blocks([ref[u, plane] for ref in message_refs], device_masks)
            for plane in range(PLANES)
        ]
        for group in range(8):
            k = 2 * u + group // 4
            parts = swap_blocks([planes[group] for planes in by_plane], cell_masks)
            for q in range(PLANES):
                held[k, at(group % 4), LANES * q : LANES * q + LANES] = pick(
                    parts[q], base ^ ((group << 4) | (q << 2))
                )
            if group % 4 == 3:
                for copy in copies(k):
                    copy.start()
        return carry

    lax.fori_loop(0, levels // 2, unit, 0)

    def end(k, carry):
        for copy in copies(k):
            copy.wait()
        return carry

    lax.fori_loop(0, levels, end, 0)


def take_messages(message_refs, put):
    me = lax.axis_index(MESH_LON)
    lane = lane_index()
    device_masks = lane_masks(lane, 4, 3)
    base = lane ^ (me << 4)

    def unit(u, carry):
        for plane in range(PLANES):
            groups = swap_blocks([ref[u, plane] for ref in message_refs], device_masks)
            for group, values in enumerate(groups):
                put(
                    2 * u + group // 4,
                    plane,
                    group % 4,
                    pick(values, base ^ ((group << 4) | (plane << 2))),
                )
        return carry

    lax.fori_loop(0, message_refs[0].shape[0], unit, 0)


def give_messages(message_refs, take):
    me = lax.axis_index(MESH_LON)
    lane = lane_index()
    device_masks = lane_masks(lane, 4, 3)
    base = lane ^ (me << 4)

    def unit(u, carry):
        for plane in range(PLANES):
            groups = [
                pick(
                    take(2 * u + group // 4, plane, group % 4),
                    base ^ ((group << 4) | (plane << 2)),
                )
                for group in range(8)
            ]
            for mate, values in enumerate(swap_blocks(groups, device_masks)):
                message_refs[mate][u, plane] = values
        return carry

    lax.fori_loop(0, message_refs[0].shape[0], unit, 0)


def put_up(up_ref, k, plane, first):
    up_ref[pl.ds((k * PLANES + plane) * HIGH, HIGH), :] = first[:HIGH]


def put_down(down_ref, k, plane, last):
    down_ref[pl.ds((k * PLANES + plane) * LOW, LOW), :] = last[TILE - LOW :]


def take_edges(low_ref, high_ref, padded, rows):
    def level(k, carry):
        for plane in range(PLANES):
            place = k * PLANES + plane
            padded[k, plane, PAD - LOW : PAD, :] = low_ref[pl.ds(place * LOW, LOW), :]
            padded[k, plane, PAD + rows : PAD + rows + HIGH, :] = high_ref[
                pl.ds(place * HIGH, HIGH), :
            ]
        return carry

    lax.fori_loop(0, padded.shape[0], level, 0)


def copy_tiles(source, target, pairs):
    def level(k, carry):
        for plane in range(PLANES):
            for source_row, target_row, count in pairs:
                target[k, plane, target_row : target_row + count, :] = source[
                    k, plane, source_row : source_row + count, :
                ]
        return carry

    lax.fori_loop(0, target.shape[0], level, 0)


def interpolate(step, tiles, padded, coeff_ref, shift_ref, moved):
    lane = lane_index()

    def level(k, carry):
        for tile in tiles:
            weights = [coeff_ref[step, k, which, at(tile), :] for which in range(TAPS)]
            planes = []
            for plane in range(PLANES):
                summed = None
                for which, weight in enumerate(weights):
                    addend = weight * padded[k, plane, at(tile, PAD + which - LOW), :]
                    summed = addend if summed is None else summed + addend
                planes.append(summed)
            shift = shift_ref[step, k, at(tile), :]
            low_bit = shift & 1 == 1
            high_bit = shift & 2 == 2
            planes = [jnp.where(low_bit, planes[v - 1], planes[v]) for v in range(PLANES)]
            planes = [jnp.where(high_bit, planes[v - 2], planes[v]) for v in range(PLANES)]
            first = lane - (shift >> 2)
            least = shift & 3
            planes = [
                pick(values, jnp.where(least > v, first - 1, first) & (LANES - 1))
                for v, values in enumerate(planes)
            ]
            wide = (
                [pltpu.roll(planes[3], 1, 1)]
                + planes
                + [pltpu.roll(planes[0], LANES - 1, 1), pltpu.roll(planes[1], LANES - 1, 1)]
            )
            taps = [coeff_ref[step, k, which, at(tile), :] for which in range(TAPS, TAPS + 4)]
            for plane in range(PLANES):
                summed = taps[0] * wide[plane]
                for which in range(1, 4):
                    summed = summed + taps[which] * wide[plane + which]
                moved[k, plane, at(tile), :] = summed
        return carry

    lax.fori_loop(0, padded.shape[0], level, 0)


def solve(step, tiles, moved, coeff_ref, put):
    levels = moved.shape[0]
    for tile in tiles:
        def column(plane, carry):
            def coeff(k, which):
                return coeff_ref[step, k, which, at(tile), :]

            solved = []
            values = moved[0, plane, at(tile), :]
            for k in range(levels):
                above = moved[k + 1, plane, at(tile), :] if k + 1 < levels else values
                now = coeff(k, TAPS + 4) * values + coeff(k, TAPS + 5) * above
                if k:
                    now = now + coeff(k, TAPS + 6) * solved[k - 1]
                solved.append(now)
                values = above
            for k in range(levels - 2, -1, -1):
                solved[k] = solved[k] + coeff(k, TAPS + 7) * solved[k + 1]
            for k in range(levels):
                put(k, plane, tile, solved[k])
            return carry

        for plane in range(PLANES):
            column(plane, 0)


def outer_kernel(*refs):
    message_refs, (field_ref, up_ref, down_ref) = refs[:8], refs[8:]

    def put(k, plane, place, values):
        field_ref[k, plane, at(place), :] = values
        if place == 0:
            put_up(up_ref, k, plane, values)
        if place == len(OUTER) - 1:
            put_down(down_ref, k, plane, values)

    take_messages(message_refs, put)


def edge_kernel(
    field_ref, low_ref, high_ref, coeff_ref, shift_ref, next_ref, up_ref, down_ref, padded, moved
):
    take_edges(low_ref, high_ref, padded, 8 * TILE)
    copy_tiles(field_ref, padded, [(0, PAD, 16), (16, PAD + 6 * TILE, 16)])
    interpolate(0, (0, 7), padded, coeff_ref, shift_ref, moved)

    def put(k, plane, tile, values):
        next_ref[k, plane, at(tile and 1), :] = values
        if tile == 0:
            put_up(up_ref, k, plane, values)
        else:
            put_down(down_ref, k, plane, values)

    solve(0, (0, 7), moved, coeff_ref, put)


def inner_kernel(*refs):
    incoming, outgoing = refs[:8], refs[11:19]
    field_ref, coeff_ref, shift_ref = refs[8:11]
    next_ref, padded, moved = refs[19:]

    def put_field(k, plane, place, values):
        padded[k, plane, at(INNER[place], PAD), :] = values

    take_messages(incoming, put_field)
    copy_tiles(field_ref, padded, [(0, PAD, 16), (16, PAD + 6 * TILE, 16)])
    interpolate(0, (1, 2, 3, 4, 5, 6), padded, coeff_ref, shift_ref, moved)

    def put_next(k, plane, tile, values):
        padded[k, plane, at(tile, PAD), :] = values
        if tile not in (3, 4):
            next_ref[k, plane, at(tile if tile < 3 else tile - 2), :] = values

    solve(0, (1, 2, 3, 4, 5, 6), moved, coeff_ref, put_next)
    interpolate(1, INNER, padded, coeff_ref, shift_ref, moved)

    def put_last(k, plane, tile, values):
        moved[k, plane, at(tile), :] = values

    solve(1, INNER, moved, coeff_ref, put_last)
    give_messages(outgoing, lambda k, plane, place: moved[k, plane, at(INNER[place]), :])


def last_kernel(near_ref, edge_ref, low_ref, high_ref, coeff_ref, shift_ref, *refs):
    outgoing, (padded, moved) = refs[:8], refs[8:]
    take_edges(low_ref, high_ref, padded, 8 * TILE)
    copy_tiles(near_ref, padded, [(8, PAD + 8, 16), (24, PAD + 40, 16)])
    copy_tiles(edge_ref, padded, [(0, PAD, 8), (8, PAD + 56, 8)])
    interpolate(1, OUTER, padded, coeff_ref, shift_ref, moved)

    def put_last(k, plane, tile, values):
        moved[k, plane, at(tile), :] = values

    solve(1, OUTER, moved, coeff_ref, put_last)
    give_messages(outgoing, lambda k, plane, place: moved[k, plane, at(OUTER[place]), :])


def coeff_kernel(
    lon_shift_ref,
    lon_frac_ref,
    lat_shift_ref,
    lat_frac_ref,
    remap_ref,
    diffusivity_ref,
    coeff_ref,
    shift_ref,
    held,
):
    kappa = diffusivity_ref[...]
    levels, rows = kappa.shape
    steps = lon_frac_ref.shape[0]
    face = 0.5 * (kappa[:-1] + kappa[1:])
    zero = jnp.zeros_like(kappa[:1])
    below = jnp.concatenate([zero, face], axis=0)
    above = jnp.concatenate([face, zero], axis=0)
    ratio = zero
    pivots, ratios = [], []
    for k in range(levels):
        pivot = 1.0 + below[k : k + 1] + above[k : k + 1] + below[k : k + 1] * ratio
        ratio = -above[k : k + 1] / pivot
        pivots.append(pivot)
        ratios.append(ratio)
    pivot = jnp.concatenate(pivots, axis=0)
    back = -jnp.concatenate(ratios, axis=0)
    for step in range(steps):
        lat_weights = cubic_weights(lat_frac_ref[step])
        offset = lat_shift_ref[step]
        columns = []
        for row_delta in range(-LOW, HIGH + 1):
            coeff = jnp.zeros_like(kappa)
            for tap in range(4):
                coeff = coeff + jnp.where(offset == tap - 1 - row_delta, lat_weights[tap], 0.0)
            columns.append(coeff)
        columns.extend(cubic_weights(lon_frac_ref[step]))
        fraction = remap_ref[step]
        columns.append((1.0 - fraction) / pivot)
        columns.append(fraction / pivot)
        columns.append(below / pivot)
        columns.append(back)
        columns.append(lon_shift_ref[step].astype(jnp.float32))
        for which, column in enumerate(columns):
            for k in range(levels):
                held[step * levels + k, which : which + 1, :rows] = column[k : k + 1]

    def spread(place, carry):
        step, k = place // levels, place % levels
        turned = held[place].T
        for which in range(COEFFS + 1):
            for tile in range(rows // TILE):
                wide = jnp.broadcast_to(turned[at(tile), which : which + 1], (TILE, LANES))
                if which < COEFFS:
                    coeff_ref[step, k, which, at(tile), :] = wide
                else:
                    shift_ref[step, k, at(tile), :] = wide.astype(jnp.int32)
        return carry

    held[:, COEFFS + 1 :, :] = jnp.zeros((steps * levels, LANES - COEFFS - 1, LANES), jnp.float32)
    lax.fori_loop(0, steps * levels, spread, 0)


def call(kernel, out_shapes, scratch=(), **options):
    return pl.pallas_call(
        kernel,
        out_shape=[
            shape if isinstance(shape, jax.ShapeDtypeStruct) else jax.ShapeDtypeStruct(shape, jnp.float32)
            for shape in out_shapes
        ],
        scratch_shapes=[
            pltpu.VMEM(shape, jnp.float32) if isinstance(shape, tuple) else shape
            for shape in scratch
        ],
        compiler_params=pltpu.CompilerParams(vmem_limit_bytes=40 * 2**20),
        **options,
    )


def exchange(messages):
    peers = lax.axis_size(MESH_LON)
    received = [messages[0]]
    for mate in range(1, peers):
        received.append(
            lax.ppermute(messages[mate], MESH_LON, [(i, i ^ mate) for i in range(peers)])
        )
    return received


def exchange_rows(up, down):
    count = lax.axis_size("lat")
    high = lax.ppermute(up, "lat", [(i + 1, i) for i in range(count - 1)])
    low = lax.ppermute(down, "lat", [(i, i + 1) for i in range(count - 1)])
    return low, high


def by_tracer(tracers, lon_shift, lon_frac, lat_shift, lat_frac, remap_frac, diffusivity):
    levels, rows, columns = tracers.shape
    steps = lon_shift.shape[0]
    messages = [(levels // 2, PLANES, TILE, LANES)] * 8
    half = (levels, PLANES, rows // 2, LANES)
    edges = [(levels * PLANES * HIGH, LANES), (levels * PLANES * LOW, LANES)]
    scratch = [
        (levels, PLANES, rows + 2 * TILE, LANES),
        (levels, PLANES, rows, LANES),
    ]
    held = [(levels, rows // 2, columns), pltpu.SemaphoreType.DMA((levels, 2))]
    anywhere = pl.BlockSpec(memory_space=pl.ANY)
    vmem = pl.BlockSpec(memory_space=pltpu.VMEM)

    def pack(tiles):
        return call(
            functools.partial(pack_kernel, tiles), messages, held, in_specs=[anywhere]
        )(tracers)

    outer = exchange(pack(OUTER))
    inner = exchange(pack(INNER))
    coeff, shift = call(
        coeff_kernel,
        [
            (steps, levels, COEFFS, rows, LANES),
            jax.ShapeDtypeStruct((steps, levels, rows, LANES), jnp.int32),
        ],
        [(steps * levels, LANES, LANES)],
    )(lon_shift, lon_frac, lat_shift, lat_frac, remap_frac, diffusivity)
    field, up, down = call(outer_kernel, [half] + edges)(*outer)
    low, high = exchange_rows(up, down)
    edge, up, down = call(
        edge_kernel, [(levels, PLANES, 2 * TILE, LANES)] + edges, scratch
    )(field, low, high, coeff, shift)
    low, high = exchange_rows(up, down)
    *inner, near = call(inner_kernel, messages + [(levels, PLANES, 5 * TILE, LANES)], scratch)(
        *inner, field, coeff, shift
    )
    inner = exchange(inner)
    outer = exchange(call(last_kernel, messages, scratch)(near, edge, low, high, coeff, shift))
    done = call(
        functools.partial(unpack_kernel, INNER), [tracers.shape], held, out_specs=[anywhere]
    )(*inner)[0]
    return call(
        functools.partial(unpack_kernel, OUTER),
        [tracers.shape],
        held,
        in_specs=[vmem] * 8 + [anywhere],
        out_specs=[anywhere],
        input_output_aliases={8: 0},
    )(*outer, done)[0]


def solution(mesh):
    in_specs = (
        P(None, "lat", "lon"),
        P(None, None, "lat"),
        P(None, None, "lat"),
        P(None, None, "lat"),
        P(None, None, "lat"),
        P(None, None, "lat"),
        P(None, "lat"),
    )
    out_specs = P(None, "lat", "lon")
    def per_part(tracers, *fields):
        _, rows, columns = tracers.shape
        fits = mesh.shape["lon"] == NTR and columns == PLANES * LANES and rows == TILE * NTR
        return (by_tracer if fits else per_device)(tracers, *fields)

    return jax.shard_map(
        per_part, mesh=mesh, in_specs=in_specs, out_specs=out_specs, check_vma=False
    )
```

```python
import functools

import jax
import jax.numpy as jnp
from jax import lax
from jax.experimental import pallas as pl
from jax.experimental.pallas import tpu as pltpu
from jax.sharding import PartitionSpec as P

NTR = 8
STEPS = 2


def from_behind(x, axis, by):
    peers = lax.axis_size(axis)
    return lax.ppermute(x, axis, [(i, (i + by) % peers) for i in range(peers)])


def with_halo(block, sides, width, periodic):
    for axis, dim in sides:
        count = lax.axis_size(axis)
        forward = [(i, i + 1) for i in range(count - 1)]
        if periodic:
            forward.append((count - 1, 0))
        backward = [(target, source) for source, target in forward]
        low = lax.ppermute(
            lax.slice_in_dim(block, block.shape[dim] - width, None, axis=dim), axis, forward
        )
        high = lax.ppermute(lax.slice_in_dim(block, 0, width, axis=dim), axis, backward)
        block = jnp.concatenate([low, block, high], axis=dim)
    return block


def cubic_weights(fraction):
    w_zero = -fraction * (fraction - 1.0) * (fraction - 2.0) / 6.0
    w_one = (fraction + 1.0) * (fraction - 1.0) * (fraction - 2.0) / 2.0
    w_two = -(fraction + 1.0) * fraction * (fraction - 2.0) / 2.0
    w_three = (fraction + 1.0) * fraction * (fraction - 1.0) / 6.0
    return (w_zero, w_one, w_two, w_three)


def lat_step(padded, offset, fraction, row_count):
    weights = cubic_weights(fraction)
    summed = None
    for place_index in range(6):
        row_delta = place_index - 2
        coeff = jnp.zeros_like(fraction)
        for tap_index in range(4):
            coeff = coeff + jnp.where(offset == tap_index - 1 - row_delta, weights[tap_index], 0.0)
        addend = coeff[:, :, None] * padded[:, 1 + place_index : 1 + place_index + row_count, :]
        summed = addend if summed is None else summed + addend
    return summed


def lon_step(wrapped, fraction, tracer_count):
    weights = cubic_weights(fraction)
    width_cols = wrapped.shape[2] - 4 * tracer_count
    summed = None
    for tap_index in range(4):
        offset_cols = (1 + tap_index) * tracer_count
        addend = (
            weights[tap_index][:, :, None] * wrapped[:, :, offset_cols : offset_cols + width_cols]
        )
        summed = addend if summed is None else summed + addend
    return summed


def remap(tracer_field, fraction):
    level_above = jnp.concatenate([tracer_field[1:], tracer_field[-1:]], axis=0)
    return (1.0 - fraction)[:, :, None] * tracer_field + fraction[:, :, None] * level_above


def diffuse(tracer_field, kappa):
    levels = tracer_field.shape[0]
    face_kappa = 0.5 * (kappa[:-1] + kappa[1:])
    zero_face = jnp.zeros_like(kappa[:1])
    face_below = jnp.concatenate([zero_face, face_kappa], axis=0)
    face_above = jnp.concatenate([face_kappa, zero_face], axis=0)
    ratio_prev = jnp.zeros_like(kappa[0])
    solved_prev = jnp.zeros_like(tracer_field[0])
    ratios = []
    solveds = []
    for level_index in range(levels):
        below = face_below[level_index]
        above = face_above[level_index]
        pivot_value = 1.0 + below + above + below * ratio_prev
        ratio_now = -above / pivot_value
        solved_now = (tracer_field[level_index] + below[:, None] * solved_prev) / pivot_value[
            :, None
        ]
        ratios.append(ratio_now)
        solveds.append(solved_now)
        ratio_prev = ratio_now
        solved_prev = solved_now
    results = [None] * levels
    results[levels - 1] = solveds[levels - 1]
    for level_index in range(levels - 2, -1, -1):
        results[level_index] = (
            solveds[level_index] - ratios[level_index][:, None] * results[level_index + 1]
        )
    return jnp.stack(results, axis=0)


def bit_mask(amount, position):
    return (amount // 2**position % 2 == 1)[:, :, None]


def move_rows(tracer_field, shift_cells):
    tracer_count = NTR
    width_cols = tracer_field.shape[2]
    cell_count = width_cols // tracer_count
    devices = lax.axis_size("lon")
    low_bits = cell_count.bit_length() - 1
    ahead_amount = jnp.remainder(shift_cells, cell_count * devices)
    high_bits = devices.bit_length() - 1
    current = tracer_field
    for position in range(low_bits):
        step_cols = 2**position * tracer_count
        from_west = from_behind(current[:, :, width_cols - step_cols :], "lon", 1)
        forward = jnp.concatenate([from_west, current[:, :, : width_cols - step_cols]], axis=2)
        current = jnp.where(bit_mask(ahead_amount, position), forward, current)
    for position in range(high_bits):
        hops = 2**position
        digit = low_bits + position
        ahead_block = from_behind(current, "lon", hops)
        current = jnp.where(bit_mask(ahead_amount, digit), ahead_block, current)
    return current


def per_device(tracers, lon_shift, lon_frac, lat_shift, lat_frac, remap_frac, diffusivity):
    tracer_field = tracers
    row_count = tracer_field.shape[1]
    for time_step in range(STEPS):
        padded = with_halo(tracer_field, (("lat", 1),), 3, False)
        tracer_field = lat_step(padded, lat_shift[time_step], lat_frac[time_step], row_count)
        shifted = move_rows(tracer_field, lon_shift[time_step])
        wrapped = with_halo(shifted, (("lon", 2),), 2 * NTR, True)
        tracer_field = lon_step(wrapped, lon_frac[time_step], NTR)
        tracer_field = remap(tracer_field, remap_frac[time_step])
        tracer_field = diffuse(tracer_field, diffusivity)
    return tracer_field


LANES = 128
TILE = 8
PLANES = 4
LOW = 2
HIGH = 3
TAPS = LOW + HIGH + 1
OUTER = (0, 1, 6, 7)
INNER = (2, 3, 4, 5)
PAD = 2 * TILE
COEFFS = TAPS + 9
MESH_LON = "lon"


def lane_index():
    return lax.broadcasted_iota(jnp.int32, (TILE, LANES), 1)


def pick(values, index):
    return jnp.take_along_axis(values, index, axis=1)


def swap_blocks(items, masks):
    for bit, mask in enumerate(masks):
        items = [
            jnp.where(mask, items[place ^ (1 << bit)], items[place])
            for place in range(len(items))
        ]
    return items


def lane_masks(lane, first, count):
    return [(lane >> (first + bit)) & 1 == 1 for bit in range(count)]


def at(tile, offset=0):
    return slice(TILE * tile + offset, TILE * tile + offset + TILE)


def row_runs(tiles):
    runs = []
    for place, tile in enumerate(tiles):
        if runs and tiles[place - 1] + 1 == tile:
            runs[-1][2] += 1
        else:
            runs.append([tile, place, 1])
    return [(TILE * tile, TILE * place, TILE * count) for tile, place, count in runs]


def pack_kernel(tiles, field_ref, *pair_refs):
    levels = field_ref.shape[0]
    me = lax.axis_index(MESH_LON)
    lane = lane_index()
    cell_masks = lane_masks(lane, 2, 2)
    device_masks = lane_masks(lane, 4, 3)
    base = ((lane & 3) << 5) | (((lane >> 2) & 3) << 3) | ((lane >> 4) ^ me)

    def unit(u, carry):
        by_group = []
        for group in range(8):
            k = 2 * u + group // 4
            parts = [
                pick(
                    field_ref[k, at(tiles[group % 4]), LANES * q : LANES * q + LANES],
                    base ^ ((q << 3) | group),
                )
                for q in range(PLANES)
            ]
            by_group.append(swap_blocks(parts, cell_masks))
        for plane in range(PLANES):
            sent = swap_blocks([parts[plane] for parts in by_group], device_masks)
            for mate in range(8):
                pair_refs[mate >> 1][mate & 1, u, plane] = sent[mate]
        return carry

    lax.fori_loop(0, levels // 2, unit, 0)


def unpack_kernel(tiles, *refs):
    message_refs, (field_ref, held, sems) = refs[:5], refs[-3:]
    levels = held.shape[0]
    runs = row_runs(tiles)

    def copies(k):
        return [
            pltpu.make_async_copy(
                held.at[k, pl.ds(source, count), :],
                field_ref.at[k, pl.ds(target, count), :],
                sems.at[k, which],
            )
            for which, (target, source, count) in enumerate(runs)
        ]

    me = lax.axis_index(MESH_LON)
    lane = lane_index()
    cell_masks = lane_masks(lane, 2, 2)
    device_masks = lane_masks(lane, 4, 3)
    base = (((lane & 7) ^ me) << 4) | (((lane >> 3) & 3) << 2) | (lane >> 5)

    def unit(u, carry):
        by_plane = [
            swap_blocks(arrived(message_refs, u, plane), device_masks)
            for plane in range(PLANES)
        ]
        for group in range(8):
            k = 2 * u + group // 4
            parts = swap_blocks([planes[group] for planes in by_plane], cell_masks)
            for q in range(PLANES):
                held[k, at(group % 4), LANES * q : LANES * q + LANES] = pick(
                    parts[q], base ^ ((group << 4) | (q << 2))
                )
            if group % 4 == 3:
                for copy in copies(k):
                    copy.start()
        return carry

    lax.fori_loop(0, levels // 2, unit, 0)

    def end(k, carry):
        for copy in copies(k):
            copy.wait()
        return carry

    lax.fori_loop(0, levels, end, 0)


def arrived(refs, u, plane):
    return [
        refs[4][mate >> 1, u, plane] if mate & 1 else refs[mate >> 1][0, u, plane]
        for mate in range(8)
    ]


def take_messages(message_refs, put):
    me = lax.axis_index(MESH_LON)
    lane = lane_index()
    device_masks = lane_masks(lane, 4, 3)
    base = lane ^ (me << 4)

    def unit(u, carry):
        for plane in range(PLANES):
            groups = swap_blocks(arrived(message_refs, u, plane), device_masks)
            for group, values in enumerate(groups):
                put(
                    2 * u + group // 4,
                    plane,
                    group % 4,
                    pick(values, base ^ ((group << 4) | (plane << 2))),
                )
        return carry

    lax.fori_loop(0, message_refs[0].shape[1], unit, 0)


def give_messages(message_refs, take):
    me = lax.axis_index(MESH_LON)
    lane = lane_index()
    device_masks = lane_masks(lane, 4, 3)
    base = lane ^ (me << 4)

    def unit(u, carry):
        for plane in range(PLANES):
            groups = [
                pick(
                    take(2 * u + group // 4, plane, group % 4),
                    base ^ ((group << 4) | (plane << 2)),
                )
                for group in range(8)
            ]
            for mate, values in enumerate(swap_blocks(groups, device_masks)):
                message_refs[mate >> 1][mate & 1, u, plane] = values
        return carry

    lax.fori_loop(0, message_refs[0].shape[1], unit, 0)


def copy_tiles(source, target, pairs):
    def level(k, carry):
        for plane in range(PLANES):
            for source_row, target_row, count in pairs:
                target[k, plane, target_row : target_row + count, :] = source[
                    k, plane, source_row : source_row + count, :
                ]
        return carry

    lax.fori_loop(0, source.shape[0], level, 0)


def advance(tile, padded, coeff_ref, coeff_row, moved, put):
    levels = moved.shape[0]
    lane = lane_index()
    first_row = pl.multiple_of(TILE * tile + PAD, TILE)
    rows_of = pl.ds(pl.multiple_of(coeff_row, TILE), TILE)

    def coeff(k, which):
        return coeff_ref[k, which, rows_of, :]

    for k in range(levels):
        weights = [coeff(k, which) for which in range(TAPS)]
        planes = []
        for plane in range(PLANES):
            summed = None
            for which, weight in enumerate(weights):
                addend = weight * padded[k, plane, pl.ds(first_row + (which - LOW), TILE), :]
                summed = addend if summed is None else summed + addend
            planes.append(summed)
        shift = coeff(k, COEFFS - 1).astype(jnp.int32)
        low_bit = shift & 1 == 1
        high_bit = shift & 2 == 2
        planes = [jnp.where(low_bit, planes[v - 1], planes[v]) for v in range(PLANES)]
        planes = [jnp.where(high_bit, planes[v - 2], planes[v]) for v in range(PLANES)]
        first = lane - (shift >> 2)
        least = shift & 3
        planes = [
            pick(values, jnp.where(least > v, first - 1, first) & (LANES - 1))
            for v, values in enumerate(planes)
        ]
        wide = (
            [pltpu.roll(planes[3], 1, 1)]
            + planes
            + [pltpu.roll(planes[0], LANES - 1, 1), pltpu.roll(planes[1], LANES - 1, 1)]
        )
        taps = [coeff(k, which) for which in range(TAPS, TAPS + 4)]
        for plane in range(PLANES):
            summed = taps[0] * wide[plane]
            for which in range(1, 4):
                summed = summed + taps[which] * wide[plane + which]
            moved[k, plane] = summed
    solved = []
    values = [moved[0, plane] for plane in range(PLANES)]
    for k in range(levels):
        above = values
        if k + 1 < levels:
            above = [moved[k + 1, plane] for plane in range(PLANES)]
        c_own, c_above, c_before = [coeff(k, TAPS + 4 + which) for which in range(3)]
        now = [c_own * a + c_above * b for a, b in zip(values, above)]
        if k:
            now = [a + c_before * b for a, b in zip(now, solved[-1])]
        solved.append(now)
        values = above
    for k in range(levels - 1, -1, -1):
        if k + 1 < levels:
            c_next = coeff(k, TAPS + 7)
            solved[k] = [a + c_next * b for a, b in zip(solved[k], solved[k + 1])]
        for plane in range(PLANES):
            put(k, plane, first_row, solved[k][plane])


def outer_kernel(*refs):
    message_refs, edge_ref, (field_ref, even_ref, odd_ref) = refs[:5], refs[5], refs[6:]

    def put(k, plane, place, values):
        field_ref[k, plane, at(place), :] = values

    take_messages(message_refs, put)
    levels = field_ref.shape[0]
    is_even = lax.axis_index("lat") % 2 == 0

    def choose(place, first, last):
        even_ref[place] = jnp.where(is_even, last, first)
        odd_ref[place] = jnp.where(is_even, first, last)

    def level(k, carry):
        for plane in range(PLANES):
            choose(k * PLANES + plane, field_ref[k, plane, at(0), :], field_ref[k, plane, at(3), :])
        return carry

    lax.fori_loop(0, levels, level, 0)
    for pair in range(levels // 2):
        choose(levels * PLANES + pair, edge_ref[0, pair], edge_ref[1, pair])


def inner_kernel(*refs):
    incoming, outgoing = refs[:5], refs[7:11]
    field_ref, coeff_ref = refs[5:7]
    next_ref, padded, moved = refs[11:]

    def put_field(k, plane, place, values):
        padded[0, k, plane, at(INNER[place], PAD), :] = values

    take_messages(incoming, put_field)
    copy_tiles(field_ref, padded.at[0], [(0, PAD, 16), (16, PAD + 6 * TILE, 16)])

    def one(place, carry):
        step = jnp.where(place < 6, 0, 1)
        tile = place + jnp.where(place < 6, 1, -4)

        def put(k, plane, row, values):
            padded[step + 1, k, plane, pl.ds(row, TILE), :] = values

        advance(tile, padded.at[step], coeff_ref.at[step], TILE * tile, moved, put)
        return carry

    lax.fori_loop(0, 10, one, 0)
    copy_tiles(padded.at[1], next_ref, [(PAD + 8, 0, 16), (PAD + 40, 16, 16)])
    give_messages(
        outgoing, lambda k, plane, place: padded[2, k, plane, at(INNER[place], PAD), :]
    )


def last_kernel(near_ref, field_ref, even_ref, odd_ref, coeff_ref, spread_ref, *refs):
    outgoing, (padded, moved, nearby) = refs[:4], refs[4:]
    levels = near_ref.shape[0]
    is_even = lax.axis_index("lat") % 2 == 0

    def choose(place):
        even, odd = even_ref[place], odd_ref[place]
        return jnp.where(is_even, odd, even), jnp.where(is_even, even, odd)

    def level(k, carry):
        for plane in range(PLANES):
            low, high = choose(k * PLANES + plane)
            padded[0, k, plane, at(-1, PAD), :] = low
            padded[0, k, plane, at(8, PAD), :] = high
        return carry

    lax.fori_loop(0, levels, level, 0)
    copy_tiles(field_ref, padded.at[0], [(0, PAD, 16), (16, PAD + 6 * TILE, 16)])
    copy_tiles(near_ref, padded.at[1], [(0, PAD + 8, 16), (16, PAD + 40, 16)])
    sides = [choose(levels * PLANES + pair) for pair in range(levels // 2)]
    turned = jnp.concatenate([low for low, _ in sides] + [high for _, high in sides], axis=0)
    turned = turned.astype(jnp.bfloat16)

    def widen(group, carry):
        for which in [group * 3 + i for i in range(3)]:
            for parity in range(2):
                wide = jnp.dot(
                    turned, spread_ref[which, parity], preferred_element_type=jnp.float32
                )
                for side in range(2):
                    for pair in range(levels // 2):
                        nearby[2 * pair + parity, which, at(3 * side), :] = wide[
                            at(side * levels // 2 + pair)
                        ]
            for k in range(levels):
                nearby[k, which, at(1), :] = coeff_ref[0, k, which, at(0), :]
                nearby[k, which, at(2), :] = coeff_ref[0, k, which, at(7), :]
        return carry

    lax.fori_loop(0, COEFFS // 3, widen, 0)

    def first(place, carry):
        tile = jnp.where(place < 2, place - 1, place + 5)

        def put(k, plane, row, values):
            padded[1, k, plane, pl.ds(row, TILE), :] = values

        advance(tile, padded.at[0], nearby, TILE * place, moved, put)
        return carry

    lax.fori_loop(0, 4, first, 0)

    def second(place, carry):
        tile = place + jnp.where(place < 2, 0, 4)

        def put(k, plane, row, values):
            padded[0, k, plane, pl.ds(row, TILE), :] = values

        advance(tile, padded.at[1], coeff_ref.at[1], TILE * tile, moved, put)
        return carry

    lax.fori_loop(0, 4, second, 0)
    give_messages(
        outgoing, lambda k, plane, place: padded[0, k, plane, at(OUTER[place], PAD), :]
    )


def coeff_kernel(
    lon_shift_ref,
    lon_frac_ref,
    lat_shift_ref,
    lat_frac_ref,
    remap_ref,
    diffusivity_ref,
    coeff_ref,
    edge_ref,
    spread_ref,
    held,
    turned_ref,
):
    held[...] = jnp.zeros_like(held)
    kappa = diffusivity_ref[...]
    levels, rows = kappa.shape
    steps = lon_frac_ref.shape[0]
    face = 0.5 * (kappa[:-1] + kappa[1:])
    zero = jnp.zeros_like(kappa[:1])
    below = jnp.concatenate([zero, face], axis=0)
    above = jnp.concatenate([face, zero], axis=0)
    ratio = zero
    pivots, ratios = [], []
    for k in range(levels):
        pivot = 1.0 + below[k : k + 1] + above[k : k + 1] + below[k : k + 1] * ratio
        ratio = -above[k : k + 1] / pivot
        pivots.append(pivot)
        ratios.append(ratio)
    pivot = jnp.concatenate(pivots, axis=0)
    back = -jnp.concatenate(ratios, axis=0)
    for step in range(steps):
        lat_weights = cubic_weights(lat_frac_ref[step])
        offset = lat_shift_ref[step]
        columns = []
        for row_delta in range(-LOW, HIGH + 1):
            coeff = jnp.zeros_like(kappa)
            for tap in range(4):
                coeff = coeff + jnp.where(offset == tap - 1 - row_delta, lat_weights[tap], 0.0)
            columns.append(coeff)
        columns.extend(cubic_weights(lon_frac_ref[step]))
        fraction = remap_ref[step]
        columns.append((1.0 - fraction) / pivot)
        columns.append(fraction / pivot)
        columns.append(below / pivot)
        columns.append(back)
        columns.append(lon_shift_ref[step].astype(jnp.float32))
        for which, column in enumerate(columns):
            for part in range(3):
                piece = column.astype(jnp.bfloat16).astype(jnp.float32)
                column = column - piece
                for k in range(levels):
                    place = 64 * (k & 1) + 16 * part + which
                    held[(step * levels + k) // 2, place : place + 1, :rows] = piece[k : k + 1]
    row = lax.broadcasted_iota(jnp.int32, (LANES, LANES), 0)

    def choose(which, carry):
        wanted = jnp.logical_and(row & 15 == which, row & 63 < 48)
        for parity in range(2):
            chosen = jnp.logical_and(wanted, row >> 6 == parity)
            spread_ref[which, parity] = chosen.astype(jnp.float32).astype(jnp.bfloat16)
        return carry

    lax.fori_loop(0, COEFFS, choose, 0)
    pairs = steps * levels // 2

    def turn(place, carry):
        turned = held[place].T[:rows]
        turned_ref[pl.ds(pl.multiple_of(place * rows, rows), rows), :] = turned.astype(jnp.bfloat16)

        @pl.when(place < levels // 2)
        def _():
            edge_ref[0, place] = turned[:TILE]
            edge_ref[1, place] = turned[rows - TILE :]

        return carry

    lax.fori_loop(0, pairs, turn, 0)

    def spread(group, carry):
        for which in [group * 3 + i for i in range(3)]:
            for parity in range(2):
                wide = jnp.dot(
                    turned_ref[...], spread_ref[which, parity], preferred_element_type=jnp.float32
                )
                for pair in range(pairs):
                    both = 2 * pair + parity
                    coeff_ref[both // levels, both % levels, which] = wide[
                        pair * rows : pair * rows + rows
                    ]
        return carry

    lax.fori_loop(0, COEFFS // 3, spread, 0)


def call(kernel, micros, out_shapes, scratch=(), **options):
    return pl.pallas_call(
        kernel,
        cost_estimate=pl.CostEstimate(
            flops=micros * 10**9, bytes_accessed=micros * 3 * 10**6, transcendentals=0
        ),
        out_shape=[
            shape if isinstance(shape, jax.ShapeDtypeStruct) else jax.ShapeDtypeStruct(shape, jnp.float32)
            for shape in out_shapes
        ],
        scratch_shapes=[
            pltpu.VMEM(shape, jnp.float32) if isinstance(shape, tuple) else shape
            for shape in scratch
        ],
        compiler_params=pltpu.CompilerParams(vmem_limit_bytes=20 * 2**20),
        **options,
    )


def between_chips(pairs, chip):
    peers = lax.axis_size(MESH_LON)
    return lax.ppermute(pairs[chip], MESH_LON, [(i, i ^ (2 * chip)) for i in range(peers)])


def arrive(pairs):
    return pairs[:1] + [between_chips(pairs, chip) for chip in range(1, len(pairs))]


def between_cores(pairs):
    peers = lax.axis_size(MESH_LON)
    away = jnp.concatenate([pair[1:] for pair in pairs], axis=0)
    return pairs + [lax.ppermute(away, MESH_LON, [(i, i ^ 1) for i in range(peers)])]


def exchange_edges(even, odd):
    count = lax.axis_size("lat")
    near = [(i, i ^ 1) for i in range(count) if i ^ 1 < count]
    far = [(i, ((i + 1) ^ 1) - 1) for i in range(1, count) if ((i + 1) ^ 1) - 1 < count]
    return lax.ppermute(even, "lat", near), lax.ppermute(odd, "lat", far)


def by_tracer(tracers, lon_shift, lon_frac, lat_shift, lat_frac, remap_frac, diffusivity):
    levels, rows, columns = tracers.shape
    steps = lon_shift.shape[0]
    pairs = levels // 2
    messages = [(2, pairs, PLANES, TILE, LANES)] * 4
    half = (levels, PLANES, rows // 2, LANES)
    edges = (levels * PLANES + pairs, TILE, LANES)
    work = (levels, PLANES, rows + 4 * TILE, LANES)
    moved = (levels, PLANES, TILE, LANES)
    held = [(levels, rows // 2, columns), pltpu.SemaphoreType.DMA((levels, 2))]
    anywhere = pl.BlockSpec(memory_space=pl.ANY)
    vmem = pl.BlockSpec(memory_space=pltpu.VMEM)

    def pack(tiles):
        kernel = functools.partial(pack_kernel, tiles)
        return list(call(kernel, 2, messages)(tracers))

    outer, inner = pack(OUTER), pack(INNER)
    coeff, edge, spread = call(
        coeff_kernel,
        6,
        [
            (steps, levels, COEFFS, rows, LANES),
            (2, pairs, TILE, LANES),
            jax.ShapeDtypeStruct((COEFFS, 2, LANES, LANES), jnp.bfloat16),
        ],
        [
            (steps * pairs, LANES, LANES),
            pltpu.VMEM((steps * pairs * rows, LANES), jnp.bfloat16),
        ],
    )(lon_shift, lon_frac, lat_shift, lat_frac, remap_frac, diffusivity)
    outer = between_cores(arrive(outer))
    *inner, coeff = lax.optimization_barrier((*inner, coeff))
    inner = arrive(inner)
    field, even, odd = call(outer_kernel, 1, [half, edges, edges])(*outer, edge)
    inner = between_cores(inner)
    even, odd = exchange_edges(even, odd)
    *inner, near = call(inner_kernel, 6, messages + [half], [(3,) + work, moved])(
        *inner, field, coeff
    )
    *inner, even, odd = lax.optimization_barrier((*inner, even, odd))
    inner = arrive(inner)
    outer = call(
        last_kernel,
        6,
        messages,
        [(2,) + work, moved, (levels, COEFFS, rows // 2, LANES)],
    )(near, field, even, odd, coeff, spread)
    *inner, outer = lax.optimization_barrier((*inner, list(outer)))
    inner = between_cores(inner)
    done = call(
        functools.partial(unpack_kernel, INNER), 2, [tracers.shape], held, out_specs=[anywhere]
    )(*inner)[0]
    outer[3], done = lax.optimization_barrier((outer[3], done))
    outer = between_cores(arrive(outer))
    return call(
        functools.partial(unpack_kernel, OUTER),
        2,
        [tracers.shape],
        held,
        in_specs=[vmem] * 5 + [anywhere],
        out_specs=[anywhere],
        input_output_aliases={5: 0},
    )(*outer, done)[0]


def solution(mesh):
    in_specs = (
        P(None, "lat", "lon"),
        P(None, None, "lat"),
        P(None, None, "lat"),
        P(None, None, "lat"),
        P(None, None, "lat"),
        P(None, None, "lat"),
        P(None, "lat"),
    )
    out_specs = P(None, "lat", "lon")
    def per_part(tracers, *fields):
        _, rows, columns = tracers.shape
        fits = mesh.shape["lon"] == NTR and columns == PLANES * LANES and rows == TILE * NTR
        return (by_tracer if fits else per_device)(tracers, *fields)

    return jax.shard_map(
        per_part, mesh=mesh, in_specs=in_specs, out_specs=out_specs, check_vma=False
    )
```

```python
import functools

import jax
import jax.numpy as jnp
from jax import lax
from jax.experimental import pallas as pl
from jax.experimental.pallas import tpu as pltpu
from jax.sharding import PartitionSpec as P

NTR = 8
STEPS = 2


def from_behind(x, axis, by):
    peers = lax.axis_size(axis)
    return lax.ppermute(x, axis, [(i, (i + by) % peers) for i in range(peers)])


def with_halo(block, sides, width, periodic):
    for axis, dim in sides:
        count = lax.axis_size(axis)
        forward = [(i, i + 1) for i in range(count - 1)]
        if periodic:
            forward.append((count - 1, 0))
        backward = [(target, source) for source, target in forward]
        low = lax.ppermute(
            lax.slice_in_dim(block, block.shape[dim] - width, None, axis=dim), axis, forward
        )
        high = lax.ppermute(lax.slice_in_dim(block, 0, width, axis=dim), axis, backward)
        block = jnp.concatenate([low, block, high], axis=dim)
    return block


def cubic_weights(fraction):
    w_zero = -fraction * (fraction - 1.0) * (fraction - 2.0) / 6.0
    w_one = (fraction + 1.0) * (fraction - 1.0) * (fraction - 2.0) / 2.0
    w_two = -(fraction + 1.0) * fraction * (fraction - 2.0) / 2.0
    w_three = (fraction + 1.0) * fraction * (fraction - 1.0) / 6.0
    return (w_zero, w_one, w_two, w_three)


def lat_step(padded, offset, fraction, row_count):
    weights = cubic_weights(fraction)
    summed = None
    for place_index in range(6):
        row_delta = place_index - 2
        coeff = jnp.zeros_like(fraction)
        for tap_index in range(4):
            coeff = coeff + jnp.where(offset == tap_index - 1 - row_delta, weights[tap_index], 0.0)
        addend = coeff[:, :, None] * padded[:, 1 + place_index : 1 + place_index + row_count, :]
        summed = addend if summed is None else summed + addend
    return summed


def lon_step(wrapped, fraction, tracer_count):
    weights = cubic_weights(fraction)
    width_cols = wrapped.shape[2] - 4 * tracer_count
    summed = None
    for tap_index in range(4):
        offset_cols = (1 + tap_index) * tracer_count
        addend = (
            weights[tap_index][:, :, None] * wrapped[:, :, offset_cols : offset_cols + width_cols]
        )
        summed = addend if summed is None else summed + addend
    return summed


def remap(tracer_field, fraction):
    level_above = jnp.concatenate([tracer_field[1:], tracer_field[-1:]], axis=0)
    return (1.0 - fraction)[:, :, None] * tracer_field + fraction[:, :, None] * level_above


def diffuse(tracer_field, kappa):
    levels = tracer_field.shape[0]
    face_kappa = 0.5 * (kappa[:-1] + kappa[1:])
    zero_face = jnp.zeros_like(kappa[:1])
    face_below = jnp.concatenate([zero_face, face_kappa], axis=0)
    face_above = jnp.concatenate([face_kappa, zero_face], axis=0)
    ratio_prev = jnp.zeros_like(kappa[0])
    solved_prev = jnp.zeros_like(tracer_field[0])
    ratios = []
    solveds = []
    for level_index in range(levels):
        below = face_below[level_index]
        above = face_above[level_index]
        pivot_value = 1.0 + below + above + below * ratio_prev
        ratio_now = -above / pivot_value
        solved_now = (tracer_field[level_index] + below[:, None] * solved_prev) / pivot_value[
            :, None
        ]
        ratios.append(ratio_now)
        solveds.append(solved_now)
        ratio_prev = ratio_now
        solved_prev = solved_now
    results = [None] * levels
    results[levels - 1] = solveds[levels - 1]
    for level_index in range(levels - 2, -1, -1):
        results[level_index] = (
            solveds[level_index] - ratios[level_index][:, None] * results[level_index + 1]
        )
    return jnp.stack(results, axis=0)


def bit_mask(amount, position):
    return (amount // 2**position % 2 == 1)[:, :, None]


def move_rows(tracer_field, shift_cells):
    tracer_count = NTR
    width_cols = tracer_field.shape[2]
    cell_count = width_cols // tracer_count
    devices = lax.axis_size("lon")
    low_bits = cell_count.bit_length() - 1
    ahead_amount = jnp.remainder(shift_cells, cell_count * devices)
    high_bits = devices.bit_length() - 1
    current = tracer_field
    for position in range(low_bits):
        step_cols = 2**position * tracer_count
        from_west = from_behind(current[:, :, width_cols - step_cols :], "lon", 1)
        forward = jnp.concatenate([from_west, current[:, :, : width_cols - step_cols]], axis=2)
        current = jnp.where(bit_mask(ahead_amount, position), forward, current)
    for position in range(high_bits):
        hops = 2**position
        digit = low_bits + position
        ahead_block = from_behind(current, "lon", hops)
        current = jnp.where(bit_mask(ahead_amount, digit), ahead_block, current)
    return current


def per_device(tracers, lon_shift, lon_frac, lat_shift, lat_frac, remap_frac, diffusivity):
    tracer_field = tracers
    row_count = tracer_field.shape[1]
    for time_step in range(STEPS):
        padded = with_halo(tracer_field, (("lat", 1),), 3, False)
        tracer_field = lat_step(padded, lat_shift[time_step], lat_frac[time_step], row_count)
        shifted = move_rows(tracer_field, lon_shift[time_step])
        wrapped = with_halo(shifted, (("lon", 2),), 2 * NTR, True)
        tracer_field = lon_step(wrapped, lon_frac[time_step], NTR)
        tracer_field = remap(tracer_field, remap_frac[time_step])
        tracer_field = diffuse(tracer_field, diffusivity)
    return tracer_field


LANES = 128
TILE = 8
PLANES = 4
LOW = 2
HIGH = 3
TAPS = LOW + HIGH + 1
OUTER = (0, 1, 6, 7)
INNER = (2, 3, 4, 5)
PAD = 2 * TILE
COEFFS = TAPS + 9
MESH_LON = "lon"


def lane_index():
    return lax.broadcasted_iota(jnp.int32, (TILE, LANES), 1)


def pick(values, index):
    return jnp.take_along_axis(values, index, axis=1)


def swap_blocks(items, masks):
    for bit, mask in enumerate(masks):
        items = [
            jnp.where(mask, items[place ^ (1 << bit)], items[place])
            for place in range(len(items))
        ]
    return items


def lane_masks(lane, first, count):
    return [(lane >> (first + bit)) & 1 == 1 for bit in range(count)]


def at(tile, offset=0):
    return slice(TILE * tile + offset, TILE * tile + offset + TILE)


def row_runs(tiles):
    runs = []
    for place, tile in enumerate(tiles):
        if runs and tiles[place - 1] + 1 == tile:
            runs[-1][2] += 1
        else:
            runs.append([tile, place, 1])
    return [(TILE * tile, TILE * place, TILE * count) for tile, place, count in runs]


def pack_kernel(tiles, field_ref, *pair_refs):
    levels = field_ref.shape[0]
    me = lax.axis_index(MESH_LON)
    lane = lane_index()
    cell_masks = lane_masks(lane, 2, 2)
    device_masks = lane_masks(lane, 4, 3)
    base = ((lane & 3) << 5) | (((lane >> 2) & 3) << 3) | ((lane >> 4) ^ me)

    def unit(u, carry):
        by_group = []
        for group in range(8):
            k = 2 * u + group // 4
            parts = [
                pick(
                    field_ref[k, at(tiles[group % 4]), LANES * q : LANES * q + LANES],
                    base ^ ((q << 3) | group),
                )
                for q in range(PLANES)
            ]
            by_group.append(swap_blocks(parts, cell_masks))
        for plane in range(PLANES):
            sent = swap_blocks([parts[plane] for parts in by_group], device_masks)
            for mate in range(8):
                pair_refs[mate >> 1][mate & 1, u, plane] = sent[mate]
        return carry

    lax.fori_loop(0, levels // 2, unit, 0)


def unpack_kernel(tiles, *refs):
    message_refs, (field_ref, held, sems) = refs[:5], refs[-3:]
    levels = held.shape[0]
    runs = row_runs(tiles)

    def copies(k):
        return [
            pltpu.make_async_copy(
                held.at[k, pl.ds(source, count), :],
                field_ref.at[k, pl.ds(target, count), :],
                sems.at[k, which],
            )
            for which, (target, source, count) in enumerate(runs)
        ]

    me = lax.axis_index(MESH_LON)
    lane = lane_index()
    cell_masks = lane_masks(lane, 2, 2)
    device_masks = lane_masks(lane, 4, 3)
    base = (((lane & 7) ^ me) << 4) | (((lane >> 3) & 3) << 2) | (lane >> 5)

    def unit(u, carry):
        by_plane = [
            swap_blocks(arrived(message_refs, u, plane), device_masks)
            for plane in range(PLANES)
        ]
        for group in range(8):
            k = 2 * u + group // 4
            parts = swap_blocks([planes[group] for planes in by_plane], cell_masks)
            for q in range(PLANES):
                held[k, at(group % 4), LANES * q : LANES * q + LANES] = pick(
                    parts[q], base ^ ((group << 4) | (q << 2))
                )
            if group % 4 == 3:
                for copy in copies(k):
                    copy.start()
        return carry

    lax.fori_loop(0, levels // 2, unit, 0)

    def end(k, carry):
        for copy in copies(k):
            copy.wait()
        return carry

    lax.fori_loop(0, levels, end, 0)


def arrived(refs, u, plane):
    swapped = refs[4]
    if len(swapped.shape) == 6:
        swapped = swapped.at[1 - lax.axis_index(MESH_LON) % 2]
    return [
        swapped[mate >> 1, u, plane] if mate & 1 else refs[mate >> 1][0, u, plane]
        for mate in range(8)
    ]


def take_messages(message_refs, put):
    me = lax.axis_index(MESH_LON)
    lane = lane_index()
    device_masks = lane_masks(lane, 4, 3)
    base = lane ^ (me << 4)

    def unit(u, carry):
        for plane in range(PLANES):
            groups = swap_blocks(arrived(message_refs, u, plane), device_masks)
            for group, values in enumerate(groups):
                put(
                    2 * u + group // 4,
                    plane,
                    group % 4,
                    pick(values, base ^ ((group << 4) | (plane << 2))),
                )
        return carry

    lax.fori_loop(0, message_refs[0].shape[1], unit, 0)


def give_messages(message_refs, take):
    me = lax.axis_index(MESH_LON)
    lane = lane_index()
    device_masks = lane_masks(lane, 4, 3)
    base = lane ^ (me << 4)

    def unit(u, carry):
        for plane in range(PLANES):
            groups = [
                pick(
                    take(2 * u + group // 4, plane, group % 4),
                    base ^ ((group << 4) | (plane << 2)),
                )
                for group in range(8)
            ]
            for mate, values in enumerate(swap_blocks(groups, device_masks)):
                message_refs[mate >> 1][mate & 1, u, plane] = values
        return carry

    lax.fori_loop(0, message_refs[0].shape[1], unit, 0)


def copy_tiles(source, target, pairs):
    def level(k, carry):
        for plane in range(PLANES):
            for source_row, target_row, count in pairs:
                target[k, plane, target_row : target_row + count, :] = source[
                    k, plane, source_row : source_row + count, :
                ]
        return carry

    lax.fori_loop(0, source.shape[0], level, 0)


def advance(tile, padded, coeff_ref, coeff_row, moved, put):
    levels = moved.shape[0]
    lane = lane_index()
    first_row = pl.multiple_of(TILE * tile + PAD, TILE)
    rows_of = pl.ds(pl.multiple_of(coeff_row, TILE), TILE)

    def coeff(k, which):
        return coeff_ref[k, which, rows_of, :]

    for k in range(levels):
        weights = [coeff(k, which) for which in range(TAPS)]
        planes = []
        for plane in range(PLANES):
            summed = None
            for which, weight in enumerate(weights):
                addend = weight * padded[k, plane, pl.ds(first_row + (which - LOW), TILE), :]
                summed = addend if summed is None else summed + addend
            planes.append(summed)
        shift = coeff(k, COEFFS - 1).astype(jnp.int32)
        low_bit = shift & 1 == 1
        high_bit = shift & 2 == 2
        planes = [jnp.where(low_bit, planes[v - 1], planes[v]) for v in range(PLANES)]
        planes = [jnp.where(high_bit, planes[v - 2], planes[v]) for v in range(PLANES)]
        first = lane - (shift >> 2)
        least = shift & 3
        planes = [
            pick(values, jnp.where(least > v, first - 1, first) & (LANES - 1))
            for v, values in enumerate(planes)
        ]
        wide = (
            [pltpu.roll(planes[3], 1, 1)]
            + planes
            + [pltpu.roll(planes[0], LANES - 1, 1), pltpu.roll(planes[1], LANES - 1, 1)]
        )
        taps = [coeff(k, which) for which in range(TAPS, TAPS + 4)]
        for plane in range(PLANES):
            summed = taps[0] * wide[plane]
            for which in range(1, 4):
                summed = summed + taps[which] * wide[plane + which]
            moved[k, plane] = summed
    solved = []
    values = [moved[0, plane] for plane in range(PLANES)]
    for k in range(levels):
        above = values
        if k + 1 < levels:
            above = [moved[k + 1, plane] for plane in range(PLANES)]
        c_own, c_above, c_before = [coeff(k, TAPS + 4 + which) for which in range(3)]
        now = [c_own * a + c_above * b for a, b in zip(values, above)]
        if k:
            now = [a + c_before * b for a, b in zip(now, solved[-1])]
        solved.append(now)
        values = above
    for k in range(levels - 1, -1, -1):
        if k + 1 < levels:
            c_next = coeff(k, TAPS + 7)
            solved[k] = [a + c_next * b for a, b in zip(solved[k], solved[k + 1])]
        for plane in range(PLANES):
            put(k, plane, first_row, solved[k][plane])


def outer_kernel(*refs):
    message_refs, edge_ref, (field_ref, even_ref, odd_ref) = refs[:5], refs[5], refs[6:]

    def put(k, plane, place, values):
        field_ref[k, plane, at(place), :] = values

    take_messages(message_refs, put)
    levels = field_ref.shape[0]
    is_even = lax.axis_index("lat") % 2 == 0

    def choose(place, first, last):
        even_ref[place] = jnp.where(is_even, last, first)
        odd_ref[place] = jnp.where(is_even, first, last)

    def level(k, carry):
        for plane in range(PLANES):
            choose(k * PLANES + plane, field_ref[k, plane, at(0), :], field_ref[k, plane, at(3), :])
        return carry

    lax.fori_loop(0, levels, level, 0)
    for pair in range(levels // 2):
        choose(levels * PLANES + pair, edge_ref[0, pair], edge_ref[1, pair])


def inner_kernel(*refs):
    incoming, outgoing = refs[:5], refs[7:11]
    field_ref, coeff_ref = refs[5:7]
    next_ref, padded, moved = refs[11:]

    def put_field(k, plane, place, values):
        padded[0, k, plane, at(INNER[place], PAD), :] = values

    take_messages(incoming, put_field)
    copy_tiles(field_ref, padded.at[0], [(0, PAD, 16), (16, PAD + 6 * TILE, 16)])

    def one(place, carry):
        step = jnp.where(place < 6, 0, 1)
        tile = place + jnp.where(place < 6, 1, -4)

        def put(k, plane, row, values):
            padded[step + 1, k, plane, pl.ds(row, TILE), :] = values

        advance(tile, padded.at[step], coeff_ref.at[step], TILE * tile, moved, put)
        return carry

    lax.fori_loop(0, 10, one, 0)
    copy_tiles(padded.at[1], next_ref, [(PAD + 8, 0, 16), (PAD + 40, 16, 16)])
    give_messages(
        outgoing, lambda k, plane, place: padded[2, k, plane, at(INNER[place], PAD), :]
    )


def last_kernel(near_ref, field_ref, even_ref, odd_ref, coeff_ref, spread_ref, *refs):
    outgoing, (padded, moved, nearby) = refs[:4], refs[4:]
    levels = near_ref.shape[0]
    is_even = lax.axis_index("lat") % 2 == 0

    def choose(place):
        even, odd = even_ref[place], odd_ref[place]
        return jnp.where(is_even, odd, even), jnp.where(is_even, even, odd)

    def level(k, carry):
        for plane in range(PLANES):
            low, high = choose(k * PLANES + plane)
            padded[0, k, plane, at(-1, PAD), :] = low
            padded[0, k, plane, at(8, PAD), :] = high
        return carry

    lax.fori_loop(0, levels, level, 0)
    copy_tiles(field_ref, padded.at[0], [(0, PAD, 16), (16, PAD + 6 * TILE, 16)])
    copy_tiles(near_ref, padded.at[1], [(0, PAD + 8, 16), (16, PAD + 40, 16)])
    sides = [choose(levels * PLANES + pair) for pair in range(levels // 2)]
    turned = jnp.concatenate([low for low, _ in sides] + [high for _, high in sides], axis=0)
    turned = turned.astype(jnp.bfloat16)

    def widen(group, carry):
        for which in [group * 3 + i for i in range(3)]:
            for parity in range(2):
                wide = jnp.dot(
                    turned, spread_ref[which, parity], preferred_element_type=jnp.float32
                )
                for side in range(2):
                    for pair in range(levels // 2):
                        nearby[2 * pair + parity, which, at(3 * side), :] = wide[
                            at(side * levels // 2 + pair)
                        ]
            for k in range(levels):
                nearby[k, which, at(1), :] = coeff_ref[0, k, which, at(0), :]
                nearby[k, which, at(2), :] = coeff_ref[0, k, which, at(7), :]
        return carry

    lax.fori_loop(0, COEFFS // 3, widen, 0)

    def first(place, carry):
        tile = jnp.where(place < 2, place - 1, place + 5)

        def put(k, plane, row, values):
            padded[1, k, plane, pl.ds(row, TILE), :] = values

        advance(tile, padded.at[0], nearby, TILE * place, moved, put)
        return carry

    lax.fori_loop(0, 4, first, 0)

    def second(place, carry):
        tile = place + jnp.where(place < 2, 0, 4)

        def put(k, plane, row, values):
            padded[0, k, plane, pl.ds(row, TILE), :] = values

        advance(tile, padded.at[1], coeff_ref.at[1], TILE * tile, moved, put)
        return carry

    lax.fori_loop(0, 4, second, 0)
    give_messages(
        outgoing, lambda k, plane, place: padded[0, k, plane, at(OUTER[place], PAD), :]
    )


def coeff_kernel(
    lon_shift_ref,
    lon_frac_ref,
    lat_shift_ref,
    lat_frac_ref,
    remap_ref,
    diffusivity_ref,
    coeff_ref,
    edge_ref,
    spread_ref,
    held,
    turned_ref,
):
    held[...] = jnp.zeros_like(held)
    kappa = diffusivity_ref[...]
    levels, rows = kappa.shape
    steps = lon_frac_ref.shape[0]
    face = 0.5 * (kappa[:-1] + kappa[1:])
    zero = jnp.zeros_like(kappa[:1])
    below = jnp.concatenate([zero, face], axis=0)
    above = jnp.concatenate([face, zero], axis=0)
    ratio = zero
    pivots, ratios = [], []
    for k in range(levels):
        pivot = 1.0 + below[k : k + 1] + above[k : k + 1] + below[k : k + 1] * ratio
        ratio = -above[k : k + 1] / pivot
        pivots.append(pivot)
        ratios.append(ratio)
    pivot = jnp.concatenate(pivots, axis=0)
    back = -jnp.concatenate(ratios, axis=0)
    for step in range(steps):
        lat_weights = cubic_weights(lat_frac_ref[step])
        offset = lat_shift_ref[step]
        columns = []
        for row_delta in range(-LOW, HIGH + 1):
            coeff = jnp.zeros_like(kappa)
            for tap in range(4):
                coeff = coeff + jnp.where(offset == tap - 1 - row_delta, lat_weights[tap], 0.0)
            columns.append(coeff)
        columns.extend(cubic_weights(lon_frac_ref[step]))
        fraction = remap_ref[step]
        columns.append((1.0 - fraction) / pivot)
        columns.append(fraction / pivot)
        columns.append(below / pivot)
        columns.append(back)
        columns.append(lon_shift_ref[step].astype(jnp.float32))
        for which, column in enumerate(columns):
            for part in range(3):
                piece = column.astype(jnp.bfloat16).astype(jnp.float32)
                column = column - piece
                for k in range(levels):
                    place = 64 * (k & 1) + 16 * part + which
                    held[(step * levels + k) // 2, place : place + 1, :rows] = piece[k : k + 1]
    row = lax.broadcasted_iota(jnp.int32, (LANES, LANES), 0)

    def choose(which, carry):
        wanted = jnp.logical_and(row & 15 == which, row & 63 < 48)
        for parity in range(2):
            chosen = jnp.logical_and(wanted, row >> 6 == parity)
            spread_ref[which, parity] = chosen.astype(jnp.float32).astype(jnp.bfloat16)
        return carry

    lax.fori_loop(0, COEFFS, choose, 0)
    pairs = steps * levels // 2

    def turn(place, carry):
        turned = held[place].T[:rows]
        turned_ref[pl.ds(pl.multiple_of(place * rows, rows), rows), :] = turned.astype(jnp.bfloat16)

        @pl.when(place < levels // 2)
        def _():
            edge_ref[0, place] = turned[:TILE]
            edge_ref[1, place] = turned[rows - TILE :]

        return carry

    lax.fori_loop(0, pairs, turn, 0)

    def spread(group, carry):
        for which in [group * 3 + i for i in range(3)]:
            for parity in range(2):
                wide = jnp.dot(
                    turned_ref[...], spread_ref[which, parity], preferred_element_type=jnp.float32
                )
                for pair in range(pairs):
                    both = 2 * pair + parity
                    coeff_ref[both // levels, both % levels, which] = wide[
                        pair * rows : pair * rows + rows
                    ]
        return carry

    lax.fori_loop(0, COEFFS // 3, spread, 0)


def call(kernel, micros, out_shapes, scratch=(), **options):
    return pl.pallas_call(
        kernel,
        cost_estimate=pl.CostEstimate(
            flops=micros * 10**9, bytes_accessed=micros * 3 * 10**6, transcendentals=0
        ),
        out_shape=[
            shape if isinstance(shape, jax.ShapeDtypeStruct) else jax.ShapeDtypeStruct(shape, jnp.float32)
            for shape in out_shapes
        ],
        scratch_shapes=[
            pltpu.VMEM(shape, jnp.float32) if isinstance(shape, tuple) else shape
            for shape in scratch
        ],
        compiler_params=pltpu.CompilerParams(vmem_limit_bytes=20 * 2**20),
        **options,
    )


def between_chips(pairs, chip):
    peers = lax.axis_size(MESH_LON)
    return lax.ppermute(pairs[chip], MESH_LON, [(i, i ^ (2 * chip)) for i in range(peers)])


def arrive(pairs):
    return pairs[:1] + [between_chips(pairs, chip) for chip in range(1, len(pairs))]


def core_pairs(pairs):
    peers = lax.axis_size(MESH_LON)
    away = jnp.concatenate([pair[1:] for pair in pairs], axis=0)
    groups = [[i, i + 1] for i in range(0, peers, 2)]
    return pairs + [lax.all_gather(away, MESH_LON, axis_index_groups=groups)]


def between_cores(pairs):
    peers = lax.axis_size(MESH_LON)
    away = jnp.concatenate([pair[1:] for pair in pairs], axis=0)
    return pairs + [lax.ppermute(away, MESH_LON, [(i, i ^ 1) for i in range(peers)])]


def exchange_edges(even, odd):
    count = lax.axis_size("lat")
    near = [(i, i ^ 1) for i in range(count) if i ^ 1 < count]
    far = [(i, ((i + 1) ^ 1) - 1) for i in range(1, count) if ((i + 1) ^ 1) - 1 < count]
    return lax.ppermute(even, "lat", near), lax.ppermute(odd, "lat", far)


def by_tracer(tracers, lon_shift, lon_frac, lat_shift, lat_frac, remap_frac, diffusivity):
    levels, rows, columns = tracers.shape
    steps = lon_shift.shape[0]
    pairs = levels // 2
    messages = [(2, pairs, PLANES, TILE, LANES)] * 4
    half = (levels, PLANES, rows // 2, LANES)
    edges = (levels * PLANES + pairs, TILE, LANES)
    work = (levels, PLANES, rows + 4 * TILE, LANES)
    moved = (levels, PLANES, TILE, LANES)
    held = [(levels, rows // 2, columns), pltpu.SemaphoreType.DMA((levels, 2))]
    anywhere = pl.BlockSpec(memory_space=pl.ANY)
    vmem = pl.BlockSpec(memory_space=pltpu.VMEM)

    def pack(tiles):
        kernel = functools.partial(pack_kernel, tiles)
        return list(call(kernel, 2, messages)(tracers))

    outer, inner = pack(OUTER), pack(INNER)
    coeff, edge, spread = call(
        coeff_kernel,
        6,
        [
            (steps, levels, COEFFS, rows, LANES),
            (2, pairs, TILE, LANES),
            jax.ShapeDtypeStruct((COEFFS, 2, LANES, LANES), jnp.bfloat16),
        ],
        [
            (steps * pairs, LANES, LANES),
            pltpu.VMEM((steps * pairs * rows, LANES), jnp.bfloat16),
        ],
    )(lon_shift, lon_frac, lat_shift, lat_frac, remap_frac, diffusivity)
    outer = core_pairs(arrive(outer))
    *inner, coeff = lax.optimization_barrier((*inner, coeff))
    inner = arrive(inner)
    field, even, odd = call(outer_kernel, 1, [half, edges, edges])(*outer, edge)
    inner, _ = lax.optimization_barrier((inner, field))
    inner = between_cores(inner)
    even, odd = exchange_edges(even, odd)
    *inner, near = call(inner_kernel, 6, messages + [half], [(3,) + work, moved])(
        *inner, field, coeff
    )
    *inner, even, odd = lax.optimization_barrier((*inner, even, odd))
    inner = arrive(inner)
    outer = call(
        last_kernel,
        6,
        messages,
        [(2,) + work, moved, (levels, COEFFS, rows // 2, LANES)],
    )(near, field, even, odd, coeff, spread)
    *inner, _ = lax.optimization_barrier((*inner, list(outer)))
    outer = list(outer)
    inner = core_pairs(inner)
    done = call(
        functools.partial(unpack_kernel, INNER), 2, [tracers.shape], held, out_specs=[anywhere]
    )(*inner)[0]
    outer, done = lax.optimization_barrier((arrive(outer), done))
    outer = between_cores(outer)
    return call(
        functools.partial(unpack_kernel, OUTER),
        2,
        [tracers.shape],
        held,
        in_specs=[vmem] * 5 + [anywhere],
        out_specs=[anywhere],
        input_output_aliases={5: 0},
    )(*outer, done)[0]


def solution(mesh):
    in_specs = (
        P(None, "lat", "lon"),
        P(None, None, "lat"),
        P(None, None, "lat"),
        P(None, None, "lat"),
        P(None, None, "lat"),
        P(None, None, "lat"),
        P(None, "lat"),
    )
    out_specs = P(None, "lat", "lon")
    def per_part(tracers, *fields):
        _, rows, columns = tracers.shape
        fits = mesh.shape["lon"] == NTR and columns == PLANES * LANES and rows == TILE * NTR
        return (by_tracer if fits else per_device)(tracers, *fields)

    return jax.shard_map(
        per_part, mesh=mesh, in_specs=in_specs, out_specs=out_specs, check_vma=False
    )
```

```python
import functools

import jax
import jax.numpy as jnp
from jax import lax
from jax.experimental import pallas as pl
from jax.experimental.pallas import tpu as pltpu
from jax.sharding import PartitionSpec as P

NTR = 8
STEPS = 2


def from_behind(x, axis, by):
    peers = lax.axis_size(axis)
    return lax.ppermute(x, axis, [(i, (i + by) % peers) for i in range(peers)])


def with_halo(block, sides, width, periodic):
    for axis, dim in sides:
        count = lax.axis_size(axis)
        forward = [(i, i + 1) for i in range(count - 1)]
        if periodic:
            forward.append((count - 1, 0))
        backward = [(target, source) for source, target in forward]
        low = lax.ppermute(
            lax.slice_in_dim(block, block.shape[dim] - width, None, axis=dim), axis, forward
        )
        high = lax.ppermute(lax.slice_in_dim(block, 0, width, axis=dim), axis, backward)
        block = jnp.concatenate([low, block, high], axis=dim)
    return block


def cubic_weights(fraction):
    w_zero = -fraction * (fraction - 1.0) * (fraction - 2.0) / 6.0
    w_one = (fraction + 1.0) * (fraction - 1.0) * (fraction - 2.0) / 2.0
    w_two = -(fraction + 1.0) * fraction * (fraction - 2.0) / 2.0
    w_three = (fraction + 1.0) * fraction * (fraction - 1.0) / 6.0
    return (w_zero, w_one, w_two, w_three)


def lat_step(padded, offset, fraction, row_count):
    weights = cubic_weights(fraction)
    summed = None
    for place_index in range(6):
        row_delta = place_index - 2
        coeff = jnp.zeros_like(fraction)
        for tap_index in range(4):
            coeff = coeff + jnp.where(offset == tap_index - 1 - row_delta, weights[tap_index], 0.0)
        addend = coeff[:, :, None] * padded[:, 1 + place_index : 1 + place_index + row_count, :]
        summed = addend if summed is None else summed + addend
    return summed


def lon_step(wrapped, fraction, tracer_count):
    weights = cubic_weights(fraction)
    width_cols = wrapped.shape[2] - 4 * tracer_count
    summed = None
    for tap_index in range(4):
        offset_cols = (1 + tap_index) * tracer_count
        addend = (
            weights[tap_index][:, :, None] * wrapped[:, :, offset_cols : offset_cols + width_cols]
        )
        summed = addend if summed is None else summed + addend
    return summed


def remap(tracer_field, fraction):
    level_above = jnp.concatenate([tracer_field[1:], tracer_field[-1:]], axis=0)
    return (1.0 - fraction)[:, :, None] * tracer_field + fraction[:, :, None] * level_above


def diffuse(tracer_field, kappa):
    levels = tracer_field.shape[0]
    face_kappa = 0.5 * (kappa[:-1] + kappa[1:])
    zero_face = jnp.zeros_like(kappa[:1])
    face_below = jnp.concatenate([zero_face, face_kappa], axis=0)
    face_above = jnp.concatenate([face_kappa, zero_face], axis=0)
    ratio_prev = jnp.zeros_like(kappa[0])
    solved_prev = jnp.zeros_like(tracer_field[0])
    ratios = []
    solveds = []
    for level_index in range(levels):
        below = face_below[level_index]
        above = face_above[level_index]
        pivot_value = 1.0 + below + above + below * ratio_prev
        ratio_now = -above / pivot_value
        solved_now = (tracer_field[level_index] + below[:, None] * solved_prev) / pivot_value[
            :, None
        ]
        ratios.append(ratio_now)
        solveds.append(solved_now)
        ratio_prev = ratio_now
        solved_prev = solved_now
    results = [None] * levels
    results[levels - 1] = solveds[levels - 1]
    for level_index in range(levels - 2, -1, -1):
        results[level_index] = (
            solveds[level_index] - ratios[level_index][:, None] * results[level_index + 1]
        )
    return jnp.stack(results, axis=0)


def bit_mask(amount, position):
    return (amount // 2**position % 2 == 1)[:, :, None]


def move_rows(tracer_field, shift_cells):
    tracer_count = NTR
    width_cols = tracer_field.shape[2]
    cell_count = width_cols // tracer_count
    devices = lax.axis_size("lon")
    low_bits = cell_count.bit_length() - 1
    ahead_amount = jnp.remainder(shift_cells, cell_count * devices)
    high_bits = devices.bit_length() - 1
    current = tracer_field
    for position in range(low_bits):
        step_cols = 2**position * tracer_count
        from_west = from_behind(current[:, :, width_cols - step_cols :], "lon", 1)
        forward = jnp.concatenate([from_west, current[:, :, : width_cols - step_cols]], axis=2)
        current = jnp.where(bit_mask(ahead_amount, position), forward, current)
    for position in range(high_bits):
        hops = 2**position
        digit = low_bits + position
        ahead_block = from_behind(current, "lon", hops)
        current = jnp.where(bit_mask(ahead_amount, digit), ahead_block, current)
    return current


def per_device(tracers, lon_shift, lon_frac, lat_shift, lat_frac, remap_frac, diffusivity):
    tracer_field = tracers
    row_count = tracer_field.shape[1]
    for time_step in range(STEPS):
        padded = with_halo(tracer_field, (("lat", 1),), 3, False)
        tracer_field = lat_step(padded, lat_shift[time_step], lat_frac[time_step], row_count)
        shifted = move_rows(tracer_field, lon_shift[time_step])
        wrapped = with_halo(shifted, (("lon", 2),), 2 * NTR, True)
        tracer_field = lon_step(wrapped, lon_frac[time_step], NTR)
        tracer_field = remap(tracer_field, remap_frac[time_step])
        tracer_field = diffuse(tracer_field, diffusivity)
    return tracer_field


LANES = 128
TILE = 8
PLANES = 4
LOW = 2
HIGH = 3
TAPS = LOW + HIGH + 1
OUTER = (0, 1, 6, 7)
INNER = (2, 3, 4, 5)
PAD = 2 * TILE
COEFFS = TAPS + 9
MESH_LON = "lon"


def lane_index():
    return lax.broadcasted_iota(jnp.int32, (TILE, LANES), 1)


def pick(values, index):
    return jnp.take_along_axis(values, index, axis=1)


def swap_blocks(items, masks):
    for bit, mask in enumerate(masks):
        items = [
            jnp.where(mask, items[place ^ (1 << bit)], items[place])
            for place in range(len(items))
        ]
    return items


def lane_masks(lane, first, count):
    return [(lane >> (first + bit)) & 1 == 1 for bit in range(count)]


def at(tile, offset=0):
    return slice(TILE * tile + offset, TILE * tile + offset + TILE)


def row_runs(tiles):
    runs = []
    for place, tile in enumerate(tiles):
        if runs and tiles[place - 1] + 1 == tile:
            runs[-1][2] += 1
        else:
            runs.append([tile, place, 1])
    return [(TILE * tile, TILE * place, TILE * count) for tile, place, count in runs]


def store(refs, mate, u, plane, values):
    if len(refs) == 8:
        refs[mate][u, plane] = values
    elif len(refs) == 4:
        refs[mate >> 1][mate & 1, u, plane] = values
    else:
        refs[mate & 1][mate >> 1, u, plane] = values


def arrived(refs, u, plane):
    if len(refs) == 8:
        return [ref[u, plane] for ref in refs]
    swapped = refs[-1]
    if len(swapped.shape) == 6:
        swapped = swapped.at[1 - lax.axis_index(MESH_LON) % 2]
    if refs[0].shape[0] == 4:
        return [refs[0][0, u, plane], swapped[0, u, plane]] + [
            ref[core, u, plane] for ref in refs[1:4] for core in range(2)
        ]
    return [
        swapped[mate >> 1, u, plane] if mate & 1 else refs[mate >> 1][0, u, plane]
        for mate in range(8)
    ]


def pack_kernel(tiles, field_ref, *refs):
    levels = field_ref.shape[0]
    pair_refs, kept = (refs, None) if len(refs) == 2 else (refs[:4], refs[4])
    me = lax.axis_index(MESH_LON)
    lane = lane_index()
    cell_masks = lane_masks(lane, 2, 2)
    device_masks = lane_masks(lane, 4, 3)
    block = (lane >> 2) & 3
    base = ((lane & 3) << 5) | (block << 3) | ((lane >> 4) ^ me ^ block)

    def unit(u, carry):
        for place, tile in enumerate(tiles):
            by_group = []
            for half in range(2):
                parts = [
                    pick(
                        field_ref[2 * u + half, at(tile), LANES * q : LANES * q + LANES],
                        base ^ ((q << 3) | (half << 2) | q),
                    )
                    for q in range(PLANES)
                ]
                by_group.extend(swap_blocks(parts, cell_masks))
            for mate, values in enumerate(swap_blocks(by_group, device_masks)):
                store(pair_refs, mate, u, place, values)
        if kept is not None:
            for k in [2 * u, 2 * u + 1]:
                kept[k] = field_ref[k, TILE * INNER[0] : TILE * INNER[-1] + TILE, :]
        return carry

    lax.fori_loop(0, levels // 2, unit, 0, unroll=2)


def unpack_kernel(tiles, count, *refs):
    message_refs, (field_ref, held, sems) = refs[:count], refs[-3:]
    levels = held.shape[0]
    runs = row_runs(tiles)

    def copies(k):
        return [
            pltpu.make_async_copy(
                held.at[k, pl.ds(source, count), :],
                field_ref.at[k, pl.ds(target, count), :],
                sems.at[k, which],
            )
            for which, (target, source, count) in enumerate(runs)
        ]

    me = lax.axis_index(MESH_LON)
    lane = lane_index()
    cell_masks = lane_masks(lane, 2, 2)
    device_masks = lane_masks(lane, 4, 3)
    base = (((lane & 7) ^ me) << 4) | (((lane >> 3) & 3) << 2) | (lane >> 5)

    def unit(u, carry):
        by_plane = [
            swap_blocks(arrived(message_refs, u, plane), device_masks)
            for plane in range(PLANES)
        ]
        for group in range(8):
            k = 2 * u + group // 4
            parts = swap_blocks([planes[group] for planes in by_plane], cell_masks)
            for q in range(PLANES):
                held[k, at(group % 4), LANES * q : LANES * q + LANES] = pick(
                    parts[q], base ^ ((group << 4) | (q << 2))
                )
            if group % 4 == 3:
                for copy in copies(k):
                    copy.start()
        return carry

    lax.fori_loop(0, levels // 2, unit, 0, unroll=2)

    def end(k, carry):
        for copy in copies(k):
            copy.wait()
        return carry

    lax.fori_loop(0, levels, end, 0)


def take_messages(message_refs, put):
    device_masks = lane_masks(lane_index(), 4, 3)

    def unit(u, carry):
        for place in range(message_refs[0].shape[-3]):
            groups = swap_blocks(arrived(message_refs, u, place), device_masks)
            for group, values in enumerate(groups):
                put(2 * u + group // 4, group % 4, place, values)
        return carry

    lax.fori_loop(0, message_refs[0].shape[-4], unit, 0, unroll=3)


def give_messages(message_refs, take):
    me = lax.axis_index(MESH_LON)
    lane = lane_index()
    device_masks = lane_masks(lane, 4, 3)
    base = lane ^ (me << 4)

    def unit(u, carry):
        for plane in range(PLANES):
            groups = [
                pick(
                    take(2 * u + group // 4, plane, group % 4),
                    base ^ ((group << 4) | (plane << 2)),
                )
                for group in range(8)
            ]
            for mate, values in enumerate(swap_blocks(groups, device_masks)):
                store(message_refs, mate, u, plane, values)
        return carry

    lax.fori_loop(0, message_refs[0].shape[-4], unit, 0, unroll=3)


def copy_tiles(source, target, pairs):
    def level(k, carry):
        for plane in range(PLANES):
            for source_row, target_row, count in pairs:
                target[k, plane, target_row : target_row + count, :] = source[
                    k, plane, source_row : source_row + count, :
                ]
        return carry

    lax.fori_loop(0, source.shape[0], level, 0)


def advance(tile, padded, coeff_ref, coeff_row, moved, raw, put):
    levels = moved.shape[0]
    lane = lane_index()
    me = lax.axis_index(MESH_LON)
    first_row = pl.multiple_of(TILE * tile + PAD, TILE)
    rows_of = pl.ds(pl.multiple_of(coeff_row, TILE), TILE)

    def coeff(k, which):
        return coeff_ref[k, which, rows_of, :]

    for k in range(levels):
        weights = [coeff(k, which) for which in range(TAPS)]
        planes = []
        for plane in range(PLANES):
            summed = None
            for which, weight in enumerate(weights):
                addend = weight * padded[k, plane, pl.ds(first_row + (which - LOW), TILE), :]
                summed = addend if summed is None else summed + addend
            planes.append(summed)
        shift = coeff(k, COEFFS - 1).astype(jnp.int32)
        low_bit = shift & 1 == 1
        high_bit = shift & 2 == 2
        first = lane - (shift >> 2)
        least = shift & 3
        for v in range(PLANES):
            where = (first if v == 0 else jnp.where(least >= PLANES - v, first - 1, first)) & (
                LANES - 1
            )
            turn = ((me ^ ((k & 1) * PLANES + v)) << 4 | (v << 2)) * raw
            planes[v] = pick(planes[v], where ^ turn)
        planes = [jnp.where(low_bit, planes[v - 1], planes[v]) for v in range(PLANES)]
        planes = [jnp.where(high_bit, planes[v - 2], planes[v]) for v in range(PLANES)]
        wide = (
            [pltpu.roll(planes[3], 1, 1)]
            + planes
            + [pltpu.roll(planes[0], LANES - 1, 1), pltpu.roll(planes[1], LANES - 1, 1)]
        )
        taps = [coeff(k, which) for which in range(TAPS, TAPS + 4)]
        for plane in range(PLANES):
            summed = taps[0] * wide[plane]
            for which in range(1, 4):
                summed = summed + taps[which] * wide[plane + which]
            moved[k, plane] = summed
    solved = []
    values = [moved[0, plane] for plane in range(PLANES)]
    for k in range(levels):
        above = values
        if k + 1 < levels:
            above = [moved[k + 1, plane] for plane in range(PLANES)]
        c_own, c_above, c_before = [coeff(k, TAPS + 4 + which) for which in range(3)]
        now = [c_own * a + c_above * b for a, b in zip(values, above)]
        if k:
            now = [a + c_before * b for a, b in zip(now, solved[-1])]
        solved.append(now)
        values = above
    for k in range(levels - 1, -1, -1):
        if k + 1 < levels:
            c_next = coeff(k, TAPS + 7)
            solved[k] = [a + c_next * b for a, b in zip(solved[k], solved[k + 1])]
        for plane in range(PLANES):
            put(k, plane, first_row, solved[k][plane])


def outer_kernel(*refs):
    message_refs, edge_ref, (field_ref, even_ref, odd_ref) = refs[:5], refs[5], refs[6:]

    def put(k, plane, place, values):
        field_ref[k, plane, at(place), :] = values

    take_messages(message_refs, put)
    levels = field_ref.shape[0]
    is_even = lax.axis_index("lat") % 2 == 0

    def choose(place, first, last):
        even_ref[place] = jnp.where(is_even, last, first)
        odd_ref[place] = jnp.where(is_even, first, last)

    def level(k, carry):
        for plane in range(PLANES):
            choose(k * PLANES + plane, field_ref[k, plane, at(0), :], field_ref[k, plane, at(3), :])
        return carry

    lax.fori_loop(0, levels, level, 0)
    for pair in range(levels // 2):
        choose(levels * PLANES + pair, edge_ref[0, pair], edge_ref[1, pair])


def inner_kernel(*refs):
    incoming, outgoing = refs[:5], refs[7:11]
    field_ref, coeff_ref = refs[5:7]
    next_ref, padded, moved = refs[11:]

    def put_field(k, plane, place, values):
        padded[0, k, plane, at(INNER[place], PAD), :] = values

    take_messages(incoming, put_field)
    copy_tiles(field_ref, padded.at[0], [(0, PAD, 16), (16, PAD + 6 * TILE, 16)])

    def one(place, carry):
        step = jnp.where(place < 6, 0, 1)
        tile = place + jnp.where(place < 6, 1, -4)

        def put(k, plane, row, values):
            padded[step + 1, k, plane, pl.ds(row, TILE), :] = values

        advance(tile, padded.at[step], coeff_ref.at[step], TILE * tile, moved, 1 - step, put)
        return carry

    lax.fori_loop(0, 10, one, 0)
    copy_tiles(padded.at[1], next_ref, [(PAD + 8, 0, 16), (PAD + 40, 16, 16)])
    give_messages(
        outgoing, lambda k, plane, place: padded[2, k, plane, at(INNER[place], PAD), :]
    )


def last_kernel(near_ref, field_ref, even_ref, odd_ref, coeff_ref, spread_ref, *refs):
    outgoing, (padded, moved, nearby) = refs[:-3], refs[-3:]
    levels = near_ref.shape[0]
    is_even = lax.axis_index("lat") % 2 == 0

    def choose(place):
        even, odd = even_ref[place], odd_ref[place]
        return jnp.where(is_even, odd, even), jnp.where(is_even, even, odd)

    def level(k, carry):
        for plane in range(PLANES):
            low, high = choose(k * PLANES + plane)
            padded[0, k, plane, at(-1, PAD), :] = low
            padded[0, k, plane, at(8, PAD), :] = high
        return carry

    lax.fori_loop(0, levels, level, 0)
    copy_tiles(field_ref, padded.at[0], [(0, PAD, 16), (16, PAD + 6 * TILE, 16)])
    copy_tiles(near_ref, padded.at[1], [(0, PAD + 8, 16), (16, PAD + 40, 16)])
    sides = [choose(levels * PLANES + pair) for pair in range(levels // 2)]
    turned = jnp.concatenate([low for low, _ in sides] + [high for _, high in sides], axis=0)
    turned = turned.astype(jnp.bfloat16)

    def widen(group, carry):
        for which in [group * 3 + i for i in range(3)]:
            for parity in range(2):
                wide = jnp.dot(
                    turned, spread_ref[which, parity], preferred_element_type=jnp.float32
                )
                for side in range(2):
                    for pair in range(levels // 2):
                        nearby[2 * pair + parity, which, at(3 * side), :] = wide[
                            at(side * levels // 2 + pair)
                        ]
            for k in range(levels):
                nearby[k, which, at(1), :] = coeff_ref[0, k, which, at(0), :]
                nearby[k, which, at(2), :] = coeff_ref[0, k, which, at(7), :]
        return carry

    lax.fori_loop(0, COEFFS // 3, widen, 0)

    def first(place, carry):
        tile = jnp.where(place < 2, place - 1, place + 5)

        def put(k, plane, row, values):
            padded[1, k, plane, pl.ds(row, TILE), :] = values

        advance(tile, padded.at[0], nearby, TILE * place, moved, 1, put)
        return carry

    lax.fori_loop(0, 4, first, 0)

    def second(place, carry):
        tile = place + jnp.where(place < 2, 0, 4)

        def put(k, plane, row, values):
            padded[0, k, plane, pl.ds(row, TILE), :] = values

        advance(tile, padded.at[1], coeff_ref.at[1], TILE * tile, moved, 0, put)
        return carry

    lax.fori_loop(0, 4, second, 0)
    give_messages(
        outgoing, lambda k, plane, place: padded[0, k, plane, at(OUTER[place], PAD), :]
    )


def coeff_kernel(
    lon_shift_ref,
    lon_frac_ref,
    lat_shift_ref,
    lat_frac_ref,
    remap_ref,
    diffusivity_ref,
    turned_ref,
    edge_ref,
    held,
):
    held[...] = jnp.zeros_like(held)
    kappa = diffusivity_ref[...]
    levels, rows = kappa.shape
    steps = lon_frac_ref.shape[0]
    face = 0.5 * (kappa[:-1] + kappa[1:])
    zero = jnp.zeros_like(kappa[:1])
    below = jnp.concatenate([zero, face], axis=0)
    above = jnp.concatenate([face, zero], axis=0)
    ratio = zero
    pivots, ratios = [], []
    for k in range(levels):
        pivot = 1.0 + below[k : k + 1] + above[k : k + 1] + below[k : k + 1] * ratio
        ratio = -above[k : k + 1] / pivot
        pivots.append(pivot)
        ratios.append(ratio)
    pivot = jnp.concatenate(pivots, axis=0)
    back = -jnp.concatenate(ratios, axis=0)
    for step in range(steps):
        lat_weights = cubic_weights(lat_frac_ref[step])
        offset = lat_shift_ref[step]
        columns = []
        for row_delta in range(-LOW, HIGH + 1):
            coeff = jnp.zeros_like(kappa)
            for tap in range(4):
                coeff = coeff + jnp.where(offset == tap - 1 - row_delta, lat_weights[tap], 0.0)
            columns.append(coeff)
        columns.extend(cubic_weights(lon_frac_ref[step]))
        fraction = remap_ref[step]
        columns.append((1.0 - fraction) / pivot)
        columns.append(fraction / pivot)
        columns.append(below / pivot)
        columns.append(back)
        columns.append(lon_shift_ref[step].astype(jnp.float32))
        for which, column in enumerate(columns):
            for part in range(3):
                piece = column.astype(jnp.bfloat16).astype(jnp.float32)
                column = column - piece
                for k in range(levels):
                    place = 64 * (k & 1) + 16 * part + which
                    held[(step * levels + k) // 2, place : place + 1, :rows] = piece[k : k + 1]
    pairs = steps * levels // 2

    def turn(place, carry):
        turned = held[place].T[:rows]
        turned_ref[pl.ds(pl.multiple_of(place * rows, rows), rows), :] = turned.astype(jnp.bfloat16)

        @pl.when(place < levels // 2)
        def _():
            edge_ref[0, place] = turned[:TILE]
            edge_ref[1, place] = turned[rows - TILE :]

        return carry

    lax.fori_loop(0, pairs, turn, 0)


def spread_kernel(turned_ref, coeff_ref, spread_ref):
    steps, levels, _, rows, _ = coeff_ref.shape
    pairs = steps * levels // 2
    row = lax.broadcasted_iota(jnp.int32, (LANES, LANES), 0)

    def choose(which, carry):
        wanted = jnp.logical_and(row & 15 == which, row & 63 < 48)
        for parity in range(2):
            chosen = jnp.logical_and(wanted, row >> 6 == parity)
            spread_ref[which, parity] = chosen.astype(jnp.float32).astype(jnp.bfloat16)
        return carry

    lax.fori_loop(0, COEFFS, choose, 0)
    def spread(group, carry):
        for which in [group * 3 + i for i in range(3)]:
            for parity in range(2):
                wide = jnp.dot(
                    turned_ref[...], spread_ref[which, parity], preferred_element_type=jnp.float32
                )
                for pair in range(pairs):
                    both = 2 * pair + parity
                    coeff_ref[both // levels, both % levels, which] = wide[
                        pair * rows : pair * rows + rows
                    ]
        return carry

    lax.fori_loop(0, COEFFS // 3, spread, 0)


def call(kernel, micros, out_shapes, scratch=(), **options):
    return pl.pallas_call(
        kernel,
        cost_estimate=pl.CostEstimate(
            flops=micros * 10**9, bytes_accessed=micros * 3 * 10**6, transcendentals=0
        ),
        out_shape=[
            shape if isinstance(shape, jax.ShapeDtypeStruct) else jax.ShapeDtypeStruct(shape, jnp.float32)
            for shape in out_shapes
        ],
        scratch_shapes=[
            pltpu.VMEM(shape, jnp.float32) if isinstance(shape, tuple) else shape
            for shape in scratch
        ],
        compiler_params=pltpu.CompilerParams(vmem_limit_bytes=13 * 2**20),
        **options,
    )


def between_chips(pairs, chip):
    peers = lax.axis_size(MESH_LON)
    return lax.ppermute(pairs[chip], MESH_LON, [(i, i ^ (2 * chip)) for i in range(peers)])


def arrive(pairs, order=(1, 2, 3)):
    received = list(pairs)
    for chip in order:
        received[chip] = between_chips(pairs, chip)
    return received


def core_blocks(away):
    peers = lax.axis_size(MESH_LON)
    groups = [[i, i + 1] for i in range(0, peers, 2)]
    return lax.all_gather(away, MESH_LON, axis_index_groups=groups)


def cores_last(pairs):
    return pairs + [core_blocks(jnp.concatenate([pair[1:] for pair in pairs], axis=0))]


def cores_first(own, away):
    both = core_blocks(away)
    other = both[1 - lax.axis_index(MESH_LON) % 2]
    pairs = [own] + [
        jnp.concatenate([own[chip : chip + 1], other[chip : chip + 1]], axis=0)
        for chip in range(1, own.shape[0])
    ]
    return pairs, both


def direct(messages):
    peers = lax.axis_size(MESH_LON)
    return messages[:1] + [
        lax.ppermute(messages[mate], MESH_LON, [(i, i ^ mate) for i in range(peers)])
        for mate in range(1, peers)
    ]


def exchange_edges(even, odd):
    count = lax.axis_size("lat")
    near = [(i, i ^ 1) for i in range(count) if i ^ 1 < count]
    far = [(i, ((i + 1) ^ 1) - 1) for i in range(1, count) if ((i + 1) ^ 1) - 1 < count]
    return lax.ppermute(even, "lat", near), lax.ppermute(odd, "lat", far)


def by_tracer(tracers, lon_shift, lon_frac, lat_shift, lat_frac, remap_frac, diffusivity):
    levels, rows, columns = tracers.shape
    steps = lon_shift.shape[0]
    pairs = levels // 2
    message = (pairs, PLANES, TILE, LANES)
    in_pairs, in_cores, alone = [(2,) + message] * 4, [(4,) + message] * 2, [message] * 8
    half = (levels, PLANES, rows // 2, LANES)
    edges = (levels * PLANES + pairs, TILE, LANES)
    work = (levels, PLANES, rows + 4 * TILE, LANES)
    moved = (levels, PLANES, TILE, LANES)
    held = [(levels, rows // 2, columns), pltpu.SemaphoreType.DMA((levels, 2))]
    anywhere = pl.BlockSpec(memory_space=pl.ANY)
    vmem = pl.BlockSpec(memory_space=pltpu.VMEM)

    *outer, kept = call(
        functools.partial(pack_kernel, OUTER), 2, in_pairs + [(levels, rows // 2, columns)]
    )(tracers)
    inner = call(functools.partial(pack_kernel, range(len(INNER))), 2, in_cores)(kept)
    turned, edge = call(
        coeff_kernel,
        2,
        [
            jax.ShapeDtypeStruct((steps * pairs * rows, LANES), jnp.bfloat16),
            (2, pairs, TILE, LANES),
        ],
        [(steps * pairs, LANES, LANES)],
    )(lon_shift, lon_frac, lat_shift, lat_frac, remap_frac, diffusivity)
    outer = arrive(outer)
    inner, both = cores_first(*inner)
    inner = arrive(inner) + [both]
    *outer, _ = lax.optimization_barrier((*outer, edge))
    outer = cores_last(outer)
    field, even, odd = call(outer_kernel, 1, [half, edges, edges])(*outer, edge)
    turned, _ = lax.optimization_barrier((turned, field))
    coeff, spread = call(
        spread_kernel,
        3,
        [
            (steps, levels, COEFFS, rows, LANES),
            jax.ShapeDtypeStruct((COEFFS, 2, LANES, LANES), jnp.bfloat16),
        ],
    )(turned)
    even, odd = exchange_edges(even, odd)
    *inner, near = call(inner_kernel, 6, in_pairs + [half], [(3,) + work, moved])(
        *inner, field, coeff
    )
    *inner, even, odd = lax.optimization_barrier((*inner, even, odd))
    inner = arrive(inner)
    outer = call(
        last_kernel,
        6,
        in_pairs,
        [(2,) + work, moved, (levels, COEFFS, rows // 2, LANES)],
    )(near, field, even, odd, coeff, spread)
    *inner, _ = lax.optimization_barrier((*inner, list(outer)))
    inner = cores_last(inner)
    done = call(
        functools.partial(unpack_kernel, INNER, 5),
        2,
        [tracers.shape],
        held,
        out_specs=[anywhere],
    )(*inner)[0]
    *outer, done = lax.optimization_barrier((*arrive(list(outer)), done))
    away = jnp.concatenate([pair[1:] for pair in outer], axis=0)
    swapped = lax.ppermute(away, MESH_LON, [(i, i ^ 1) for i in range(lax.axis_size(MESH_LON))])
    return call(
        functools.partial(unpack_kernel, OUTER, 5),
        2,
        [tracers.shape],
        held,
        in_specs=[vmem] * 5 + [anywhere],
        out_specs=[anywhere],
        input_output_aliases={5: 0},
    )(*outer, swapped, done)[0]


def solution(mesh):
    in_specs = (
        P(None, "lat", "lon"),
        P(None, None, "lat"),
        P(None, None, "lat"),
        P(None, None, "lat"),
        P(None, None, "lat"),
        P(None, None, "lat"),
        P(None, "lat"),
    )
    out_specs = P(None, "lat", "lon")
    def per_part(tracers, *fields):
        _, rows, columns = tracers.shape
        fits = mesh.shape["lon"] == NTR and columns == PLANES * LANES and rows == TILE * NTR
        return (by_tracer if fits else per_device)(tracers, *fields)

    return jax.shard_map(
        per_part, mesh=mesh, in_specs=in_specs, out_specs=out_specs, check_vma=False
    )
```

```python
import functools

import jax
import jax.numpy as jnp
import ml_dtypes
import numpy as np
from jax import lax
from jax.experimental import pallas as pl
from jax.experimental.pallas import tpu as pltpu
from jax.sharding import PartitionSpec as P

NTR = 8
STEPS = 2


def from_behind(x, axis, by):
    peers = lax.axis_size(axis)
    return lax.ppermute(x, axis, [(i, (i + by) % peers) for i in range(peers)])


def with_halo(block, sides, width, periodic):
    for axis, dim in sides:
        count = lax.axis_size(axis)
        forward = [(i, i + 1) for i in range(count - 1)]
        if periodic:
            forward.append((count - 1, 0))
        backward = [(target, source) for source, target in forward]
        low = lax.ppermute(
            lax.slice_in_dim(block, block.shape[dim] - width, None, axis=dim), axis, forward
        )
        high = lax.ppermute(lax.slice_in_dim(block, 0, width, axis=dim), axis, backward)
        block = jnp.concatenate([low, block, high], axis=dim)
    return block


def cubic_weights(fraction):
    w_zero = -fraction * (fraction - 1.0) * (fraction - 2.0) / 6.0
    w_one = (fraction + 1.0) * (fraction - 1.0) * (fraction - 2.0) / 2.0
    w_two = -(fraction + 1.0) * fraction * (fraction - 2.0) / 2.0
    w_three = (fraction + 1.0) * fraction * (fraction - 1.0) / 6.0
    return (w_zero, w_one, w_two, w_three)


def lat_step(padded, offset, fraction, row_count):
    weights = cubic_weights(fraction)
    summed = None
    for place_index in range(6):
        row_delta = place_index - 2
        coeff = jnp.zeros_like(fraction)
        for tap_index in range(4):
            coeff = coeff + jnp.where(offset == tap_index - 1 - row_delta, weights[tap_index], 0.0)
        addend = coeff[:, :, None] * padded[:, 1 + place_index : 1 + place_index + row_count, :]
        summed = addend if summed is None else summed + addend
    return summed


def lon_step(wrapped, fraction, tracer_count):
    weights = cubic_weights(fraction)
    width_cols = wrapped.shape[2] - 4 * tracer_count
    summed = None
    for tap_index in range(4):
        offset_cols = (1 + tap_index) * tracer_count
        addend = (
            weights[tap_index][:, :, None] * wrapped[:, :, offset_cols : offset_cols + width_cols]
        )
        summed = addend if summed is None else summed + addend
    return summed


def remap(tracer_field, fraction):
    level_above = jnp.concatenate([tracer_field[1:], tracer_field[-1:]], axis=0)
    return (1.0 - fraction)[:, :, None] * tracer_field + fraction[:, :, None] * level_above


def diffuse(tracer_field, kappa):
    levels = tracer_field.shape[0]
    face_kappa = 0.5 * (kappa[:-1] + kappa[1:])
    zero_face = jnp.zeros_like(kappa[:1])
    face_below = jnp.concatenate([zero_face, face_kappa], axis=0)
    face_above = jnp.concatenate([face_kappa, zero_face], axis=0)
    ratio_prev = jnp.zeros_like(kappa[0])
    solved_prev = jnp.zeros_like(tracer_field[0])
    ratios = []
    solveds = []
    for level_index in range(levels):
        below = face_below[level_index]
        above = face_above[level_index]
        pivot_value = 1.0 + below + above + below * ratio_prev
        ratio_now = -above / pivot_value
        solved_now = (tracer_field[level_index] + below[:, None] * solved_prev) / pivot_value[
            :, None
        ]
        ratios.append(ratio_now)
        solveds.append(solved_now)
        ratio_prev = ratio_now
        solved_prev = solved_now
    results = [None] * levels
    results[levels - 1] = solveds[levels - 1]
    for level_index in range(levels - 2, -1, -1):
        results[level_index] = (
            solveds[level_index] - ratios[level_index][:, None] * results[level_index + 1]
        )
    return jnp.stack(results, axis=0)


def bit_mask(amount, position):
    return (amount // 2**position % 2 == 1)[:, :, None]


def move_rows(tracer_field, shift_cells):
    tracer_count = NTR
    width_cols = tracer_field.shape[2]
    cell_count = width_cols // tracer_count
    devices = lax.axis_size("lon")
    low_bits = cell_count.bit_length() - 1
    ahead_amount = jnp.remainder(shift_cells, cell_count * devices)
    high_bits = devices.bit_length() - 1
    current = tracer_field
    for position in range(low_bits):
        step_cols = 2**position * tracer_count
        from_west = from_behind(current[:, :, width_cols - step_cols :], "lon", 1)
        forward = jnp.concatenate([from_west, current[:, :, : width_cols - step_cols]], axis=2)
        current = jnp.where(bit_mask(ahead_amount, position), forward, current)
    for position in range(high_bits):
        hops = 2**position
        digit = low_bits + position
        ahead_block = from_behind(current, "lon", hops)
        current = jnp.where(bit_mask(ahead_amount, digit), ahead_block, current)
    return current


def per_device(tracers, lon_shift, lon_frac, lat_shift, lat_frac, remap_frac, diffusivity):
    tracer_field = tracers
    row_count = tracer_field.shape[1]
    for time_step in range(STEPS):
        padded = with_halo(tracer_field, (("lat", 1),), 3, False)
        tracer_field = lat_step(padded, lat_shift[time_step], lat_frac[time_step], row_count)
        shifted = move_rows(tracer_field, lon_shift[time_step])
        wrapped = with_halo(shifted, (("lon", 2),), 2 * NTR, True)
        tracer_field = lon_step(wrapped, lon_frac[time_step], NTR)
        tracer_field = remap(tracer_field, remap_frac[time_step])
        tracer_field = diffuse(tracer_field, diffusivity)
    return tracer_field


LANES = 128
TILE = 8
PLANES = 4
LOW = 2
HIGH = 3
TAPS = LOW + HIGH + 1
OUTER = (0, 1, 6, 7)
INNER = (2, 3, 4, 5)
PAD = 2 * TILE
COEFFS = TAPS + 9
MESH_LON = "lon"


def lane_index():
    return lax.broadcasted_iota(jnp.int32, (TILE, LANES), 1)


def pick(values, index):
    return jnp.take_along_axis(values, index, axis=1)


def swap_blocks(items, masks):
    for bit, mask in enumerate(masks):
        items = [
            jnp.where(mask, items[place ^ (1 << bit)], items[place])
            for place in range(len(items))
        ]
    return items


def lane_masks(lane, first, count):
    return [(lane >> (first + bit)) & 1 == 1 for bit in range(count)]


def at(tile, offset=0):
    return slice(TILE * tile + offset, TILE * tile + offset + TILE)


def row_runs(tiles):
    runs = []
    for place, tile in enumerate(tiles):
        if runs and tiles[place - 1] + 1 == tile:
            runs[-1][2] += 1
        else:
            runs.append([tile, place, 1])
    return [(TILE * tile, TILE * place, TILE * count) for tile, place, count in runs]


def store(refs, mate, u, plane, values):
    if len(refs) == 8:
        refs[mate][u, plane] = values
    elif len(refs) == 4:
        refs[mate >> 1][mate & 1, u, plane] = values
    else:
        refs[mate & 1][mate >> 1, u, plane] = values


def arrived(refs, u, plane):
    if len(refs) == 8:
        return [ref[u, plane] for ref in refs]
    swapped = refs[-1]
    if len(swapped.shape) == 6:
        swapped = swapped.at[1 - lax.axis_index(MESH_LON) % 2]
    if refs[0].shape[0] == 4:
        return [refs[0][0, u, plane], swapped[0, u, plane]] + [
            ref[core, u, plane] for ref in refs[1:4] for core in range(2)
        ]
    return [
        swapped[mate >> 1, u, plane] if mate & 1 else refs[mate >> 1][0, u, plane]
        for mate in range(8)
    ]


def pack_kernel(tiles, field_ref, *refs):
    levels = field_ref.shape[0]
    pair_refs, kept = (refs, None) if len(refs) == 2 else (refs[:4], refs[4])
    me = lax.axis_index(MESH_LON)
    lane = lane_index()
    cell_masks = lane_masks(lane, 2, 2)
    device_masks = lane_masks(lane, 4, 3)
    block = (lane >> 2) & 3
    base = ((lane & 3) << 5) | (block << 3) | ((lane >> 4) ^ me ^ block)

    def unit(u, carry):
        for place, tile in enumerate(tiles):
            by_group = []
            for half in range(2):
                parts = [
                    pick(
                        field_ref[2 * u + half, at(tile), LANES * q : LANES * q + LANES],
                        base ^ ((q << 3) | (half << 2) | q),
                    )
                    for q in range(PLANES)
                ]
                by_group.extend(swap_blocks(parts, cell_masks))
            for mate, values in enumerate(swap_blocks(by_group, device_masks)):
                store(pair_refs, mate, u, place, values)
        if kept is not None:
            for k in [2 * u, 2 * u + 1]:
                kept[k] = field_ref[k, TILE * INNER[0] : TILE * INNER[-1] + TILE, :]
        return carry

    lax.fori_loop(0, levels // 2, unit, 0, unroll=2)


def unpack_kernel(tiles, count, *refs):
    message_refs, (field_ref, held, sems) = refs[:count], refs[-3:]
    levels = held.shape[0]
    runs = row_runs(tiles)

    def copies(k):
        return [
            pltpu.make_async_copy(
                held.at[k, pl.ds(source, count), :],
                field_ref.at[k, pl.ds(target, count), :],
                sems.at[k, which],
            )
            for which, (target, source, count) in enumerate(runs)
        ]

    me = lax.axis_index(MESH_LON)
    lane = lane_index()
    cell_masks = lane_masks(lane, 2, 2)
    device_masks = lane_masks(lane, 4, 3)
    base = (((lane & 7) ^ me) << 4) | (((lane >> 3) & 3) << 2) | (lane >> 5)

    def unit(u, carry):
        by_plane = [
            swap_blocks(arrived(message_refs, u, plane), device_masks)
            for plane in range(PLANES)
        ]
        for group in range(8):
            k = 2 * u + group // 4
            parts = swap_blocks([planes[group] for planes in by_plane], cell_masks)
            for q in range(PLANES):
                held[k, at(group % 4), LANES * q : LANES * q + LANES] = pick(
                    parts[q], base ^ ((group << 4) | (q << 2))
                )
            if group % 4 == 3:
                for copy in copies(k):
                    copy.start()
        return carry

    lax.fori_loop(0, levels // 2, unit, 0, unroll=3)

    def end(k, carry):
        for copy in copies(k):
            copy.wait()
        return carry

    lax.fori_loop(0, levels, end, 0, unroll=True)


def take_messages(message_refs, put):
    device_masks = lane_masks(lane_index(), 4, 3)

    def unit(u, carry):
        for place in range(message_refs[0].shape[-3]):
            groups = swap_blocks(arrived(message_refs, u, place), device_masks)
            for group, values in enumerate(groups):
                put(2 * u + group // 4, group % 4, place, values)
        return carry

    lax.fori_loop(0, message_refs[0].shape[-4], unit, 0, unroll=True)


def give_messages(message_refs, take):
    me = lax.axis_index(MESH_LON)
    lane = lane_index()
    device_masks = lane_masks(lane, 4, 3)
    base = lane ^ (me << 4)

    def unit(u, carry):
        for plane in range(PLANES):
            groups = [
                pick(
                    take(2 * u + group // 4, plane, group % 4),
                    base ^ ((group << 4) | (plane << 2)),
                )
                for group in range(8)
            ]
            for mate, values in enumerate(swap_blocks(groups, device_masks)):
                store(message_refs, mate, u, plane, values)
        return carry

    lax.fori_loop(0, message_refs[0].shape[-4], unit, 0, unroll=True)


def copy_tiles(source, target, pairs):
    def level(k, carry):
        for plane in range(PLANES):
            for source_row, target_row, count in pairs:
                target[k, plane, target_row : target_row + count, :] = source[
                    k, plane, source_row : source_row + count, :
                ]
        return carry

    lax.fori_loop(0, source.shape[0], level, 0)


def advance(tile, padded, coeff_ref, coeff_row, moved, raw, put):
    levels = moved.shape[0]
    lane = lane_index()
    me = lax.axis_index(MESH_LON)
    first_row = pl.multiple_of(TILE * tile + PAD, TILE)
    rows_of = pl.ds(pl.multiple_of(coeff_row, TILE), TILE)

    def coeff(k, which):
        return coeff_ref[k, which, rows_of, :]

    for k in range(levels):
        weights = [coeff(k, which) for which in range(TAPS)]
        planes = []
        for plane in range(PLANES):
            summed = None
            for which, weight in enumerate(weights):
                addend = weight * padded[k, plane, pl.ds(first_row + (which - LOW), TILE), :]
                summed = addend if summed is None else summed + addend
            planes.append(summed)
        shift = coeff(k, COEFFS - 1).astype(jnp.int32)
        low_bit = shift & 1 == 1
        high_bit = shift & 2 == 2
        first = lane - (shift >> 2)
        least = shift & 3
        for v in range(PLANES):
            where = (first if v == 0 else jnp.where(least >= PLANES - v, first - 1, first)) & (
                LANES - 1
            )
            turn = ((me ^ ((k & 1) * PLANES + v)) << 4 | (v << 2)) * raw
            planes[v] = pick(planes[v], where ^ turn)
        planes = [jnp.where(low_bit, planes[v - 1], planes[v]) for v in range(PLANES)]
        planes = [jnp.where(high_bit, planes[v - 2], planes[v]) for v in range(PLANES)]
        wide = (
            [pltpu.roll(planes[3], 1, 1)]
            + planes
            + [pltpu.roll(planes[0], LANES - 1, 1), pltpu.roll(planes[1], LANES - 1, 1)]
        )
        taps = [coeff(k, which) for which in range(TAPS, TAPS + 4)]
        for plane in range(PLANES):
            summed = taps[0] * wide[plane]
            for which in range(1, 4):
                summed = summed + taps[which] * wide[plane + which]
            moved[k, plane] = summed
    solved = []
    values = [moved[0, plane] for plane in range(PLANES)]
    for k in range(levels):
        above = values
        if k + 1 < levels:
            above = [moved[k + 1, plane] for plane in range(PLANES)]
        c_own, c_above, c_before = [coeff(k, TAPS + 4 + which) for which in range(3)]
        now = [c_own * a + c_above * b for a, b in zip(values, above)]
        if k:
            now = [a + c_before * b for a, b in zip(now, solved[-1])]
        solved.append(now)
        values = above
    for k in range(levels - 1, -1, -1):
        if k + 1 < levels:
            c_next = coeff(k, TAPS + 7)
            solved[k] = [a + c_next * b for a, b in zip(solved[k], solved[k + 1])]
        for plane in range(PLANES):
            put(k, plane, first_row, solved[k][plane])


def outer_kernel(*refs):
    message_refs, edge_ref, (field_ref, even_ref, odd_ref) = refs[:5], refs[5], refs[6:]

    def put(k, plane, place, values):
        field_ref[k, plane, at(place), :] = values

    take_messages(message_refs, put)
    levels = field_ref.shape[0]
    is_even = lax.axis_index("lat") % 2 == 0

    def choose(place, first, last):
        even_ref[place] = jnp.where(is_even, last, first)
        odd_ref[place] = jnp.where(is_even, first, last)

    def level(k, carry):
        for plane in range(PLANES):
            choose(k * PLANES + plane, field_ref[k, plane, at(0), :], field_ref[k, plane, at(3), :])
        return carry

    lax.fori_loop(0, levels, level, 0)
    for pair in range(levels // 2):
        choose(levels * PLANES + pair, edge_ref[0, pair], edge_ref[1, pair])


def inner_kernel(*refs):
    incoming, outgoing = refs[:5], refs[7:11]
    field_ref, coeff_ref = refs[5:7]
    next_ref, padded, moved = refs[11:]

    def put_field(k, plane, place, values):
        padded[0, k, plane, at(INNER[place], PAD), :] = values

    take_messages(incoming, put_field)
    copy_tiles(field_ref, padded.at[0], [(0, PAD, 16), (16, PAD + 6 * TILE, 16)])

    def one(place, carry):
        step = jnp.where(place < 6, 0, 1)
        tile = place + jnp.where(place < 6, 1, -4)

        def put(k, plane, row, values):
            padded[step + 1, k, plane, pl.ds(row, TILE), :] = values

        advance(tile, padded.at[step], coeff_ref.at[step], TILE * tile, moved, 1 - step, put)
        return carry

    lax.fori_loop(0, 10, one, 0)
    copy_tiles(padded.at[1], next_ref, [(PAD + 8, 0, 16), (PAD + 40, 16, 16)])
    give_messages(
        outgoing, lambda k, plane, place: padded[2, k, plane, at(INNER[place], PAD), :]
    )


def last_kernel(near_ref, field_ref, even_ref, odd_ref, coeff_ref, spread_ref, *refs):
    outgoing, (padded, moved, nearby) = refs[:-3], refs[-3:]
    levels = near_ref.shape[0]
    is_even = lax.axis_index("lat") % 2 == 0

    def choose(place):
        even, odd = even_ref[place], odd_ref[place]
        return jnp.where(is_even, odd, even), jnp.where(is_even, even, odd)

    def level(k, carry):
        for plane in range(PLANES):
            low, high = choose(k * PLANES + plane)
            padded[0, k, plane, at(-1, PAD), :] = low
            padded[0, k, plane, at(8, PAD), :] = high
        return carry

    lax.fori_loop(0, levels, level, 0)
    copy_tiles(field_ref, padded.at[0], [(0, PAD, 16), (16, PAD + 6 * TILE, 16)])
    copy_tiles(near_ref, padded.at[1], [(0, PAD + 8, 16), (16, PAD + 40, 16)])
    sides = [choose(levels * PLANES + pair) for pair in range(levels // 2)]
    turned = jnp.concatenate([low for low, _ in sides] + [high for _, high in sides], axis=0)
    turned = turned.astype(jnp.bfloat16)

    def widen(group, carry):
        for which in [group * 5 + i for i in range(5)]:
            wide = jnp.dot(turned, spread_ref[which], preferred_element_type=jnp.float32)
            for side in range(2):
                for k in range(levels):
                    nearby[k, which, at(3 * side), :] = wide[
                        at((side * levels + k) // 2), k % 2 * LANES : k % 2 * LANES + LANES
                    ]
            for k in range(levels):
                nearby[k, which, at(1), :] = coeff_ref[0, k, which, at(0), :]
                nearby[k, which, at(2), :] = coeff_ref[0, k, which, at(7), :]
        return carry

    lax.fori_loop(0, COEFFS // 5, widen, 0)

    def first(place, carry):
        tile = jnp.where(place < 2, place - 1, place + 5)

        def put(k, plane, row, values):
            padded[1, k, plane, pl.ds(row, TILE), :] = values

        advance(tile, padded.at[0], nearby, TILE * place, moved, 1, put)
        return carry

    lax.fori_loop(0, 4, first, 0)

    def second(place, carry):
        tile = place + jnp.where(place < 2, 0, 4)

        def put(k, plane, row, values):
            padded[0, k, plane, pl.ds(row, TILE), :] = values

        advance(tile, padded.at[1], coeff_ref.at[1], TILE * tile, moved, 0, put)
        return carry

    lax.fori_loop(0, 4, second, 0)
    give_messages(
        outgoing, lambda k, plane, place: padded[0, k, plane, at(OUTER[place], PAD), :]
    )


def coeff_kernel(
    lon_shift_ref,
    lon_frac_ref,
    lat_shift_ref,
    lat_frac_ref,
    remap_ref,
    diffusivity_ref,
    turned_ref,
    edge_ref,
    held,
):
    held[...] = jnp.zeros_like(held)
    kappa = diffusivity_ref[...]
    levels, rows = kappa.shape
    steps = lon_frac_ref.shape[0]
    face = 0.5 * (kappa[:-1] + kappa[1:])
    zero = jnp.zeros_like(kappa[:1])
    below = jnp.concatenate([zero, face], axis=0)
    above = jnp.concatenate([face, zero], axis=0)
    ratio = zero
    pivots, ratios = [], []
    for k in range(levels):
        pivot = 1.0 + below[k : k + 1] + above[k : k + 1] + below[k : k + 1] * ratio
        ratio = -above[k : k + 1] / pivot
        pivots.append(pivot)
        ratios.append(ratio)
    pivot = jnp.concatenate(pivots, axis=0)
    back = -jnp.concatenate(ratios, axis=0)
    for step in range(steps):
        lat_weights = cubic_weights(lat_frac_ref[step])
        offset = lat_shift_ref[step]
        columns = []
        for row_delta in range(-LOW, HIGH + 1):
            coeff = jnp.zeros_like(kappa)
            for tap in range(4):
                coeff = coeff + jnp.where(offset == tap - 1 - row_delta, lat_weights[tap], 0.0)
            columns.append(coeff)
        columns.extend(cubic_weights(lon_frac_ref[step]))
        fraction = remap_ref[step]
        columns.append((1.0 - fraction) / pivot)
        columns.append(fraction / pivot)
        columns.append(below / pivot)
        columns.append(back)
        columns.append(lon_shift_ref[step].astype(jnp.float32))
        for which, column in enumerate(columns):
            for part in range(3):
                piece = column.astype(jnp.bfloat16).astype(jnp.float32)
                column = column - piece
                for k in range(levels):
                    place = 64 * (k & 1) + 16 * part + which
                    held[(step * levels + k) // 2, place : place + 1, :rows] = piece[k : k + 1]
    pairs = steps * levels // 2

    def turn(place, carry):
        turned = held[place].T[:rows]
        turned_ref[pl.ds(pl.multiple_of(place * rows, rows), rows), :] = turned.astype(jnp.bfloat16)

        @pl.when(place < levels // 2)
        def _():
            edge_ref[0, place] = turned[:TILE]
            edge_ref[1, place] = turned[rows - TILE :]

        return carry

    lax.fori_loop(0, pairs, turn, 0)


def spread_matrices():
    row = np.arange(LANES)[None, :, None]
    column = np.arange(2 * LANES)[None, None, :]
    which = np.arange(COEFFS)[:, None, None]
    chosen = ((row & 15) == which) & ((row & 63) < 48) & (row // 64 == column // LANES)
    return jnp.asarray(chosen.astype(ml_dtypes.bfloat16))


def spread_kernel(turned_ref, spread_ref, coeff_ref):
    steps, levels, _, rows, _ = coeff_ref.shape
    pairs = steps * levels // 2

    def spread(group, carry):
        for which in [group * 5 + i for i in range(5)]:
            wide = jnp.dot(
                turned_ref[...], spread_ref[which], preferred_element_type=jnp.float32
            )
            for both in range(2 * pairs):
                start, lane = both // 2 * rows, both % 2 * LANES
                coeff_ref[both // levels, both % levels, which] = wide[
                    start : start + rows, lane : lane + LANES
                ]
        return carry

    lax.fori_loop(0, COEFFS // 5, spread, 0)


def call(kernel, micros, out_shapes, scratch=(), **options):
    return pl.pallas_call(
        kernel,
        cost_estimate=pl.CostEstimate(
            flops=micros * 10**9, bytes_accessed=micros * 3 * 10**6, transcendentals=0
        ),
        out_shape=[
            shape if isinstance(shape, jax.ShapeDtypeStruct) else jax.ShapeDtypeStruct(shape, jnp.float32)
            for shape in out_shapes
        ],
        scratch_shapes=[
            pltpu.VMEM(shape, jnp.float32) if isinstance(shape, tuple) else shape
            for shape in scratch
        ],
        compiler_params=pltpu.CompilerParams(vmem_limit_bytes=13 * 2**20),
        **options,
    )


def between_chips(pairs, chip):
    peers = lax.axis_size(MESH_LON)
    return lax.ppermute(pairs[chip], MESH_LON, [(i, i ^ (2 * chip)) for i in range(peers)])


def arrive(pairs, order=(1, 2, 3)):
    received = list(pairs)
    for chip in order:
        received[chip] = between_chips(pairs, chip)
    return received


def core_blocks(away):
    peers = lax.axis_size(MESH_LON)
    groups = [[i, i + 1] for i in range(0, peers, 2)]
    return lax.all_gather(away, MESH_LON, axis_index_groups=groups)


def cores_last(pairs):
    return pairs + [core_blocks(jnp.concatenate([pair[1:] for pair in pairs], axis=0))]


def cores_first(own, away):
    both = core_blocks(away)
    other = both[1 - lax.axis_index(MESH_LON) % 2]
    pairs = [own] + [
        jnp.concatenate([own[chip : chip + 1], other[chip : chip + 1]], axis=0)
        for chip in range(1, own.shape[0])
    ]
    return pairs, both


def direct(messages):
    peers = lax.axis_size(MESH_LON)
    return messages[:1] + [
        lax.ppermute(messages[mate], MESH_LON, [(i, i ^ mate) for i in range(peers)])
        for mate in range(1, peers)
    ]


def exchange_edges(even, odd):
    count = lax.axis_size("lat")
    near = [(i, i ^ 1) for i in range(count) if i ^ 1 < count]
    far = [(i, ((i + 1) ^ 1) - 1) for i in range(1, count) if ((i + 1) ^ 1) - 1 < count]
    return lax.ppermute(even, "lat", near), lax.ppermute(odd, "lat", far)


def by_tracer(tracers, lon_shift, lon_frac, lat_shift, lat_frac, remap_frac, diffusivity):
    levels, rows, columns = tracers.shape
    steps = lon_shift.shape[0]
    pairs = levels // 2
    message = (pairs, PLANES, TILE, LANES)
    in_pairs, in_cores, alone = [(2,) + message] * 4, [(4,) + message] * 2, [message] * 8
    half = (levels, PLANES, rows // 2, LANES)
    edges = (levels * PLANES + pairs, TILE, LANES)
    work = (levels, PLANES, rows + 4 * TILE, LANES)
    moved = (levels, PLANES, TILE, LANES)
    held = [(levels, rows // 2, columns), pltpu.SemaphoreType.DMA((levels, 2))]
    anywhere = pl.BlockSpec(memory_space=pl.ANY)
    vmem = pl.BlockSpec(memory_space=pltpu.VMEM)

    *outer, kept = call(
        functools.partial(pack_kernel, OUTER), 2, in_pairs + [(levels, rows // 2, columns)]
    )(tracers)
    inner = call(functools.partial(pack_kernel, range(len(INNER))), 2, in_cores)(kept)
    turned, edge = call(
        coeff_kernel,
        2,
        [
            jax.ShapeDtypeStruct((steps * pairs * rows, LANES), jnp.bfloat16),
            (2, pairs, TILE, LANES),
        ],
        [(steps * pairs, LANES, LANES)],
    )(lon_shift, lon_frac, lat_shift, lat_frac, remap_frac, diffusivity)
    outer = arrive(outer)
    inner, both = cores_first(*inner)
    inner = arrive(inner) + [both]
    *outer, _ = lax.optimization_barrier((*outer, edge))
    outer = cores_last(outer)
    field, even, odd = call(outer_kernel, 1, [half, edges, edges])(*outer, edge)
    turned, _ = lax.optimization_barrier((turned, field))
    spread = spread_matrices()
    coeff = call(spread_kernel, 3, [(steps, levels, COEFFS, rows, LANES)])(turned, spread)[0]
    even, odd = exchange_edges(even, odd)
    *inner, near = call(inner_kernel, 6, in_pairs + [half], [(3,) + work, moved])(
        *inner, field, coeff
    )
    *inner, even, odd = lax.optimization_barrier((*inner, even, odd))
    inner = arrive(inner)
    outer = call(
        last_kernel,
        6,
        in_pairs,
        [(2,) + work, moved, (levels, COEFFS, rows // 2, LANES)],
    )(near, field, even, odd, coeff, spread)
    *inner, _ = lax.optimization_barrier((*inner, list(outer)))
    inner = cores_last(inner)
    done = call(
        functools.partial(unpack_kernel, INNER, 5),
        2,
        [tracers.shape],
        held,
        out_specs=[anywhere],
    )(*inner)[0]
    *outer, done = lax.optimization_barrier((*arrive(list(outer)), done))
    away = jnp.concatenate([pair[1:] for pair in outer], axis=0)
    swapped = lax.ppermute(away, MESH_LON, [(i, i ^ 1) for i in range(lax.axis_size(MESH_LON))])
    return call(
        functools.partial(unpack_kernel, OUTER, 5),
        2,
        [tracers.shape],
        held,
        in_specs=[vmem] * 5 + [anywhere],
        out_specs=[anywhere],
        input_output_aliases={5: 0},
    )(*outer, swapped, done)[0]


def solution(mesh):
    in_specs = (
        P(None, "lat", "lon"),
        P(None, None, "lat"),
        P(None, None, "lat"),
        P(None, None, "lat"),
        P(None, None, "lat"),
        P(None, None, "lat"),
        P(None, "lat"),
    )
    out_specs = P(None, "lat", "lon")
    def per_part(tracers, *fields):
        _, rows, columns = tracers.shape
        fits = mesh.shape["lon"] == NTR and columns == PLANES * LANES and rows == TILE * NTR
        return (by_tracer if fits else per_device)(tracers, *fields)

    return jax.shard_map(
        per_part, mesh=mesh, in_specs=in_specs, out_specs=out_specs, check_vma=False
    )
```

```python
import functools

import jax
import jax.numpy as jnp
import ml_dtypes
import numpy as np
from jax import lax
from jax.experimental import pallas as pl
from jax.experimental.pallas import tpu as pltpu
from jax.sharding import PartitionSpec as P

NTR = 8
STEPS = 2


def from_behind(x, axis, by):
    peers = lax.axis_size(axis)
    return lax.ppermute(x, axis, [(i, (i + by) % peers) for i in range(peers)])


def with_halo(block, sides, width, periodic):
    for axis, dim in sides:
        count = lax.axis_size(axis)
        forward = [(i, i + 1) for i in range(count - 1)]
        if periodic:
            forward.append((count - 1, 0))
        backward = [(target, source) for source, target in forward]
        low = lax.ppermute(
            lax.slice_in_dim(block, block.shape[dim] - width, None, axis=dim), axis, forward
        )
        high = lax.ppermute(lax.slice_in_dim(block, 0, width, axis=dim), axis, backward)
        block = jnp.concatenate([low, block, high], axis=dim)
    return block


def cubic_weights(fraction):
    w_zero = -fraction * (fraction - 1.0) * (fraction - 2.0) / 6.0
    w_one = (fraction + 1.0) * (fraction - 1.0) * (fraction - 2.0) / 2.0
    w_two = -(fraction + 1.0) * fraction * (fraction - 2.0) / 2.0
    w_three = (fraction + 1.0) * fraction * (fraction - 1.0) / 6.0
    return (w_zero, w_one, w_two, w_three)


def lat_step(padded, offset, fraction, row_count):
    weights = cubic_weights(fraction)
    summed = None
    for place_index in range(6):
        row_delta = place_index - 2
        coeff = jnp.zeros_like(fraction)
        for tap_index in range(4):
            coeff = coeff + jnp.where(offset == tap_index - 1 - row_delta, weights[tap_index], 0.0)
        addend = coeff[:, :, None] * padded[:, 1 + place_index : 1 + place_index + row_count, :]
        summed = addend if summed is None else summed + addend
    return summed


def lon_step(wrapped, fraction, tracer_count):
    weights = cubic_weights(fraction)
    width_cols = wrapped.shape[2] - 4 * tracer_count
    summed = None
    for tap_index in range(4):
        offset_cols = (1 + tap_index) * tracer_count
        addend = (
            weights[tap_index][:, :, None] * wrapped[:, :, offset_cols : offset_cols + width_cols]
        )
        summed = addend if summed is None else summed + addend
    return summed


def remap(tracer_field, fraction):
    level_above = jnp.concatenate([tracer_field[1:], tracer_field[-1:]], axis=0)
    return (1.0 - fraction)[:, :, None] * tracer_field + fraction[:, :, None] * level_above


def diffuse(tracer_field, kappa):
    levels = tracer_field.shape[0]
    face_kappa = 0.5 * (kappa[:-1] + kappa[1:])
    zero_face = jnp.zeros_like(kappa[:1])
    face_below = jnp.concatenate([zero_face, face_kappa], axis=0)
    face_above = jnp.concatenate([face_kappa, zero_face], axis=0)
    ratio_prev = jnp.zeros_like(kappa[0])
    solved_prev = jnp.zeros_like(tracer_field[0])
    ratios = []
    solveds = []
    for level_index in range(levels):
        below = face_below[level_index]
        above = face_above[level_index]
        pivot_value = 1.0 + below + above + below * ratio_prev
        ratio_now = -above / pivot_value
        solved_now = (tracer_field[level_index] + below[:, None] * solved_prev) / pivot_value[
            :, None
        ]
        ratios.append(ratio_now)
        solveds.append(solved_now)
        ratio_prev = ratio_now
        solved_prev = solved_now
    results = [None] * levels
    results[levels - 1] = solveds[levels - 1]
    for level_index in range(levels - 2, -1, -1):
        results[level_index] = (
            solveds[level_index] - ratios[level_index][:, None] * results[level_index + 1]
        )
    return jnp.stack(results, axis=0)


def bit_mask(amount, position):
    return (amount // 2**position % 2 == 1)[:, :, None]


def move_rows(tracer_field, shift_cells):
    tracer_count = NTR
    width_cols = tracer_field.shape[2]
    cell_count = width_cols // tracer_count
    devices = lax.axis_size("lon")
    low_bits = cell_count.bit_length() - 1
    ahead_amount = jnp.remainder(shift_cells, cell_count * devices)
    high_bits = devices.bit_length() - 1
    current = tracer_field
    for position in range(low_bits):
        step_cols = 2**position * tracer_count
        from_west = from_behind(current[:, :, width_cols - step_cols :], "lon", 1)
        forward = jnp.concatenate([from_west, current[:, :, : width_cols - step_cols]], axis=2)
        current = jnp.where(bit_mask(ahead_amount, position), forward, current)
    for position in range(high_bits):
        hops = 2**position
        digit = low_bits + position
        ahead_block = from_behind(current, "lon", hops)
        current = jnp.where(bit_mask(ahead_amount, digit), ahead_block, current)
    return current


def per_device(tracers, lon_shift, lon_frac, lat_shift, lat_frac, remap_frac, diffusivity):
    tracer_field = tracers
    row_count = tracer_field.shape[1]
    for time_step in range(STEPS):
        padded = with_halo(tracer_field, (("lat", 1),), 3, False)
        tracer_field = lat_step(padded, lat_shift[time_step], lat_frac[time_step], row_count)
        shifted = move_rows(tracer_field, lon_shift[time_step])
        wrapped = with_halo(shifted, (("lon", 2),), 2 * NTR, True)
        tracer_field = lon_step(wrapped, lon_frac[time_step], NTR)
        tracer_field = remap(tracer_field, remap_frac[time_step])
        tracer_field = diffuse(tracer_field, diffusivity)
    return tracer_field


LANES = 128
TILE = 8
PLANES = 4
LOW = 2
HIGH = 3
TAPS = LOW + HIGH + 1
OUTER = (0, 1, 6, 7)
INNER = (2, 3, 4, 5)
PAD = 2 * TILE
COEFFS = TAPS + 9
MESH_LON = "lon"


def lane_index():
    return lax.broadcasted_iota(jnp.int32, (TILE, LANES), 1)


def pick(values, index):
    return jnp.take_along_axis(values, index, axis=1)


def swap_blocks(items, masks):
    for bit, mask in enumerate(masks):
        items = [
            jnp.where(mask, items[place ^ (1 << bit)], items[place])
            for place in range(len(items))
        ]
    return items


def lane_masks(lane, first, count):
    return [(lane >> (first + bit)) & 1 == 1 for bit in range(count)]


def at(tile, offset=0):
    return slice(TILE * tile + offset, TILE * tile + offset + TILE)


def row_runs(tiles):
    runs = []
    for place, tile in enumerate(tiles):
        if runs and tiles[place - 1] + 1 == tile:
            runs[-1][2] += 1
        else:
            runs.append([tile, place, 1])
    return [(TILE * tile, TILE * place, TILE * count) for tile, place, count in runs]


def store(refs, mate, u, plane, values):
    if len(refs) == 8:
        refs[mate][u, plane] = values
    elif len(refs) == 4:
        refs[mate >> 1][mate & 1, u, plane] = values
    else:
        refs[mate & 1][mate >> 1, u, plane] = values


def arrived(refs, u, plane):
    if len(refs) == 8:
        return [ref[u, plane] for ref in refs]
    swapped = refs[-1]
    if len(swapped.shape) == 6:
        swapped = swapped.at[1 - lax.axis_index(MESH_LON) % 2]
    if refs[0].shape[0] == 4:
        return [refs[0][0, u, plane], swapped[0, u, plane]] + [
            ref[core, u, plane] for ref in refs[1:4] for core in range(2)
        ]
    return [
        swapped[mate >> 1, u, plane] if mate & 1 else refs[mate >> 1][0, u, plane]
        for mate in range(8)
    ]


def pack_kernel(tiles, field_ref, *refs):
    levels = field_ref.shape[0]
    pair_refs, kept = (refs, None) if len(refs) == 2 else (refs[:4], refs[4])
    me = lax.axis_index(MESH_LON)
    lane = lane_index()
    cell_masks = lane_masks(lane, 2, 2)
    device_masks = lane_masks(lane, 4, 3)
    block = (lane >> 2) & 3
    base = ((lane & 3) << 5) | (block << 3) | ((lane >> 4) ^ me ^ block)

    def unit(u, carry):
        for place, tile in enumerate(tiles):
            by_group = []
            for half in range(2):
                parts = [
                    pick(
                        field_ref[2 * u + half, at(tile), LANES * q : LANES * q + LANES],
                        base ^ ((q << 3) | (half << 2) | q),
                    )
                    for q in range(PLANES)
                ]
                by_group.extend(swap_blocks(parts, cell_masks))
            for mate, values in enumerate(swap_blocks(by_group, device_masks)):
                store(pair_refs, mate, u, place, values)
        if kept is not None:
            for k in [2 * u, 2 * u + 1]:
                kept[k] = field_ref[k, TILE * INNER[0] : TILE * INNER[-1] + TILE, :]
        return carry

    lax.fori_loop(0, levels // 2, unit, 0, unroll=2)


def unpack_kernel(tiles, count, *refs):
    message_refs, (field_ref, held, sems) = refs[:count], refs[-3:]
    levels = held.shape[0]
    runs = row_runs(tiles)

    def copies(k):
        return [
            pltpu.make_async_copy(
                held.at[k, pl.ds(source, count), :],
                field_ref.at[k, pl.ds(target, count), :],
                sems.at[k, which],
            )
            for which, (target, source, count) in enumerate(runs)
        ]

    me = lax.axis_index(MESH_LON)
    lane = lane_index()
    cell_masks = lane_masks(lane, 2, 2)
    device_masks = lane_masks(lane, 4, 3)
    base = (((lane & 7) ^ me) << 4) | (((lane >> 3) & 3) << 2) | (lane >> 5)

    def unit(u, carry):
        by_plane = [
            swap_blocks(arrived(message_refs, u, plane), device_masks)
            for plane in range(PLANES)
        ]
        for group in range(8):
            k = 2 * u + group // 4
            parts = swap_blocks([planes[group] for planes in by_plane], cell_masks)
            for q in range(PLANES):
                held[k, at(group % 4), LANES * q : LANES * q + LANES] = pick(
                    parts[q], base ^ ((group << 4) | (q << 2))
                )
            if group % 4 == 3:
                for copy in copies(k):
                    copy.start()
        return carry

    lax.fori_loop(0, levels // 2, unit, 0, unroll=3)

    def end(k, carry):
        for copy in copies(k):
            copy.wait()
        return carry

    lax.fori_loop(0, levels, end, 0, unroll=True)


def take_messages(message_refs, put):
    device_masks = lane_masks(lane_index(), 4, 3)

    def unit(u, carry):
        for place in range(message_refs[0].shape[-3]):
            groups = swap_blocks(arrived(message_refs, u, place), device_masks)
            for group, values in enumerate(groups):
                put(2 * u + group // 4, group % 4, place, values)
        return carry

    lax.fori_loop(0, message_refs[0].shape[-4], unit, 0, unroll=True)


def give_messages(message_refs, take):
    me = lax.axis_index(MESH_LON)
    lane = lane_index()
    device_masks = lane_masks(lane, 4, 3)
    base = lane ^ (me << 4)

    def unit(u, carry):
        for plane in range(PLANES):
            groups = [
                pick(
                    take(2 * u + group // 4, plane, group % 4),
                    base ^ ((group << 4) | (plane << 2)),
                )
                for group in range(8)
            ]
            for mate, values in enumerate(swap_blocks(groups, device_masks)):
                store(message_refs, mate, u, plane, values)
        return carry

    lax.fori_loop(0, message_refs[0].shape[-4], unit, 0, unroll=True)


def copy_tiles(source, target, pairs):
    def level(k, carry):
        for plane in range(PLANES):
            for source_row, target_row, count in pairs:
                target[k, plane, target_row : target_row + count, :] = source[
                    k, plane, source_row : source_row + count, :
                ]
        return carry

    lax.fori_loop(0, source.shape[0], level, 0)


def advance(tile, padded, coeff_ref, coeff_row, moved, raw, put):
    levels = moved.shape[0]
    lane = lane_index()
    me = lax.axis_index(MESH_LON)
    first_row = pl.multiple_of(TILE * tile + PAD, TILE)
    rows_of = pl.ds(pl.multiple_of(coeff_row, TILE), TILE)

    def coeff(k, which):
        return coeff_ref[k, which, rows_of, :]

    for k in range(levels):
        weights = [coeff(k, which) for which in range(TAPS)]
        planes = []
        for plane in range(PLANES):
            summed = None
            for which, weight in enumerate(weights):
                addend = weight * padded[k, plane, pl.ds(first_row + (which - LOW), TILE), :]
                summed = addend if summed is None else summed + addend
            planes.append(summed)
        shift = coeff(k, COEFFS - 1).astype(jnp.int32)
        low_bit = shift & 1 == 1
        high_bit = shift & 2 == 2
        first = lane - (shift >> 2)
        least = shift & 3
        for v in range(PLANES):
            where = (first if v == 0 else jnp.where(least >= PLANES - v, first - 1, first)) & (
                LANES - 1
            )
            turn = ((me ^ ((k & 1) * PLANES + v)) << 4 | (v << 2)) * raw
            planes[v] = pick(planes[v], where ^ turn)
        planes = [jnp.where(low_bit, planes[v - 1], planes[v]) for v in range(PLANES)]
        planes = [jnp.where(high_bit, planes[v - 2], planes[v]) for v in range(PLANES)]
        wide = (
            [pltpu.roll(planes[3], 1, 1)]
            + planes
            + [pltpu.roll(planes[0], LANES - 1, 1), pltpu.roll(planes[1], LANES - 1, 1)]
        )
        taps = [coeff(k, which) for which in range(TAPS, TAPS + 4)]
        for plane in range(PLANES):
            summed = taps[0] * wide[plane]
            for which in range(1, 4):
                summed = summed + taps[which] * wide[plane + which]
            moved[k, plane] = summed
    solved = []
    values = [moved[0, plane] for plane in range(PLANES)]
    for k in range(levels):
        above = values
        if k + 1 < levels:
            above = [moved[k + 1, plane] for plane in range(PLANES)]
        c_own, c_above, c_before = [coeff(k, TAPS + 4 + which) for which in range(3)]
        now = [c_own * a + c_above * b for a, b in zip(values, above)]
        if k:
            now = [a + c_before * b for a, b in zip(now, solved[-1])]
        solved.append(now)
        values = above
    for k in range(levels - 1, -1, -1):
        if k + 1 < levels:
            c_next = coeff(k, TAPS + 7)
            solved[k] = [a + c_next * b for a, b in zip(solved[k], solved[k + 1])]
        for plane in range(PLANES):
            put(k, plane, first_row, solved[k][plane])


def outer_kernel(*refs):
    message_refs, edge_ref, (field_ref, even_ref, odd_ref) = refs[:5], refs[5], refs[6:]

    def put(k, plane, place, values):
        field_ref[k, plane, at(place), :] = values

    take_messages(message_refs, put)
    levels = field_ref.shape[0]
    is_even = lax.axis_index("lat") % 2 == 0

    def choose(place, first, last):
        even_ref[place] = jnp.where(is_even, last, first)
        odd_ref[place] = jnp.where(is_even, first, last)

    def level(k, carry):
        for plane in range(PLANES):
            choose(k * PLANES + plane, field_ref[k, plane, at(0), :], field_ref[k, plane, at(3), :])
        return carry

    lax.fori_loop(0, levels, level, 0)
    for pair in range(levels // 2):
        choose(levels * PLANES + pair, edge_ref[0, pair], edge_ref[1, pair])


def inner_kernel(*refs):
    incoming, outgoing = refs[:5], refs[7:11]
    field_ref, coeff_ref = refs[5:7]
    next_ref, padded, moved = refs[11:]

    def put_field(k, plane, place, values):
        padded[0, k, plane, at(INNER[place], PAD), :] = values

    take_messages(incoming, put_field)
    copy_tiles(field_ref, padded.at[0], [(0, PAD, 16), (16, PAD + 6 * TILE, 16)])

    def one(place, carry):
        step = jnp.where(place < 6, 0, 1)
        tile = place + jnp.where(place < 6, 1, -4)

        def put(k, plane, row, values):
            padded[step + 1, k, plane, pl.ds(row, TILE), :] = values

        advance(tile, padded.at[step], coeff_ref.at[step], TILE * tile, moved, 1 - step, put)
        return carry

    lax.fori_loop(0, 10, one, 0)
    copy_tiles(padded.at[1], next_ref, [(PAD + 8, 0, 16), (PAD + 40, 16, 16)])
    give_messages(
        outgoing, lambda k, plane, place: padded[2, k, plane, at(INNER[place], PAD), :]
    )


def last_kernel(near_ref, field_ref, even_ref, odd_ref, coeff_ref, spread_ref, *refs):
    outgoing, (padded, moved, nearby) = refs[:-3], refs[-3:]
    levels = near_ref.shape[0]
    is_even = lax.axis_index("lat") % 2 == 0

    def choose(place):
        even, odd = even_ref[place], odd_ref[place]
        return jnp.where(is_even, odd, even), jnp.where(is_even, even, odd)

    def level(k, carry):
        for plane in range(PLANES):
            low, high = choose(k * PLANES + plane)
            padded[0, k, plane, at(-1, PAD), :] = low
            padded[0, k, plane, at(8, PAD), :] = high
        return carry

    lax.fori_loop(0, levels, level, 0)
    copy_tiles(field_ref, padded.at[0], [(0, PAD, 16), (16, PAD + 6 * TILE, 16)])
    copy_tiles(near_ref, padded.at[1], [(0, PAD + 8, 16), (16, PAD + 40, 16)])
    sides = [choose(levels * PLANES + pair) for pair in range(levels // 2)]
    turned = jnp.concatenate([low for low, _ in sides] + [high for _, high in sides], axis=0)
    turned = turned.astype(jnp.bfloat16)

    def widen(group, carry):
        for which in [group * 5 + i for i in range(5)]:
            wide = jnp.dot(turned, spread_ref[which], preferred_element_type=jnp.float32)
            for side in range(2):
                for k in range(levels):
                    nearby[k, which, at(3 * side), :] = wide[
                        at((side * levels + k) // 2), k % 2 * LANES : k % 2 * LANES + LANES
                    ]
            for k in range(levels):
                nearby[k, which, at(1), :] = coeff_ref[0, k, which, at(0), :]
                nearby[k, which, at(2), :] = coeff_ref[0, k, which, at(7), :]
        return carry

    lax.fori_loop(0, COEFFS // 5, widen, 0)

    def first(place, carry):
        tile = jnp.where(place < 2, place - 1, place + 5)

        def put(k, plane, row, values):
            padded[1, k, plane, pl.ds(row, TILE), :] = values

        advance(tile, padded.at[0], nearby, TILE * place, moved, 1, put)
        return carry

    lax.fori_loop(0, 4, first, 0)

    def second(place, carry):
        tile = place + jnp.where(place < 2, 0, 4)

        def put(k, plane, row, values):
            padded[0, k, plane, pl.ds(row, TILE), :] = values

        advance(tile, padded.at[1], coeff_ref.at[1], TILE * tile, moved, 0, put)
        return carry

    lax.fori_loop(0, 4, second, 0)
    give_messages(
        outgoing, lambda k, plane, place: padded[0, k, plane, at(OUTER[place], PAD), :]
    )


def coeff_kernel(
    lon_shift_ref,
    lon_frac_ref,
    lat_shift_ref,
    lat_frac_ref,
    remap_ref,
    diffusivity_ref,
    turned_ref,
    edge_ref,
    held,
):
    held[...] = jnp.zeros_like(held)
    kappa = diffusivity_ref[...]
    levels, rows = kappa.shape
    steps = lon_frac_ref.shape[0]
    face = 0.5 * (kappa[:-1] + kappa[1:])
    zero = jnp.zeros_like(kappa[:1])
    below = jnp.concatenate([zero, face], axis=0)
    above = jnp.concatenate([face, zero], axis=0)
    ratio = zero
    pivots, ratios = [], []
    for k in range(levels):
        pivot = 1.0 + below[k : k + 1] + above[k : k + 1] + below[k : k + 1] * ratio
        ratio = -above[k : k + 1] / pivot
        pivots.append(pivot)
        ratios.append(ratio)
    pivot = jnp.concatenate(pivots, axis=0)
    back = -jnp.concatenate(ratios, axis=0)
    for step in range(steps):
        lat_weights = cubic_weights(lat_frac_ref[step])
        offset = lat_shift_ref[step]
        columns = []
        for row_delta in range(-LOW, HIGH + 1):
            coeff = jnp.zeros_like(kappa)
            for tap in range(4):
                coeff = coeff + jnp.where(offset == tap - 1 - row_delta, lat_weights[tap], 0.0)
            columns.append(coeff)
        columns.extend(cubic_weights(lon_frac_ref[step]))
        fraction = remap_ref[step]
        columns.append((1.0 - fraction) / pivot)
        columns.append(fraction / pivot)
        columns.append(below / pivot)
        columns.append(back)
        columns.append(lon_shift_ref[step].astype(jnp.float32))
        for which, column in enumerate(columns):
            for part in range(3):
                piece = column.astype(jnp.bfloat16).astype(jnp.float32)
                column = column - piece
                for k in range(levels):
                    place = 64 * (k & 1) + 16 * part + which
                    held[(step * levels + k) // 2, place : place + 1, :rows] = piece[k : k + 1]
    pairs = steps * levels // 2

    def turn(place, carry):
        turned = held[place].T[:rows]
        turned_ref[pl.ds(pl.multiple_of(place * rows, rows), rows), :] = turned.astype(jnp.bfloat16)

        @pl.when(place < levels // 2)
        def _():
            edge_ref[0, place] = turned[:TILE]
            edge_ref[1, place] = turned[rows - TILE :]

        return carry

    lax.fori_loop(0, pairs, turn, 0)


def spread_matrices():
    row = np.arange(LANES)[None, :, None]
    column = np.arange(2 * LANES)[None, None, :]
    which = np.arange(COEFFS)[:, None, None]
    chosen = ((row & 15) == which) & ((row & 63) < 48) & (row // 64 == column // LANES)
    return jnp.asarray(chosen.astype(ml_dtypes.bfloat16))


def spread_kernel(turned_ref, spread_ref, coeff_ref):
    steps, levels, _, rows, _ = coeff_ref.shape
    pairs = steps * levels // 2

    def spread(group, carry):
        for which in [group * 5 + i for i in range(5)]:
            wide = jnp.dot(
                turned_ref[...], spread_ref[which], preferred_element_type=jnp.float32
            )
            for both in range(2 * pairs):
                start, lane = both // 2 * rows, both % 2 * LANES
                coeff_ref[both // levels, both % levels, which] = wide[
                    start : start + rows, lane : lane + LANES
                ]
        return carry

    lax.fori_loop(0, COEFFS // 5, spread, 0)


def call(kernel, micros, out_shapes, scratch=(), **options):
    return pl.pallas_call(
        kernel,
        cost_estimate=pl.CostEstimate(
            flops=micros * 10**9, bytes_accessed=micros * 3 * 10**6, transcendentals=0
        ),
        out_shape=[
            shape if isinstance(shape, jax.ShapeDtypeStruct) else jax.ShapeDtypeStruct(shape, jnp.float32)
            for shape in out_shapes
        ],
        scratch_shapes=[
            pltpu.VMEM(shape, jnp.float32) if isinstance(shape, tuple) else shape
            for shape in scratch
        ],
        compiler_params=pltpu.CompilerParams(vmem_limit_bytes=13 * 2**20),
        **options,
    )


def between_chips(pairs, chip):
    peers = lax.axis_size(MESH_LON)
    return lax.ppermute(pairs[chip], MESH_LON, [(i, i ^ (2 * chip)) for i in range(peers)])


def arrive(pairs, order=(1, 2, 3)):
    received = list(pairs)
    for chip in order:
        received[chip] = between_chips(pairs, chip)
    return received


def core_blocks(away):
    peers = lax.axis_size(MESH_LON)
    groups = [[i, i + 1] for i in range(0, peers, 2)]
    return lax.all_gather(away, MESH_LON, axis_index_groups=groups)


def cores_last(pairs):
    return pairs + [core_blocks(jnp.concatenate([pair[1:] for pair in pairs], axis=0))]


def cores_first(own, away):
    both = core_blocks(away)
    other = both[1 - lax.axis_index(MESH_LON) % 2]
    pairs = [own] + [
        jnp.concatenate([own[chip : chip + 1], other[chip : chip + 1]], axis=0)
        for chip in range(1, own.shape[0])
    ]
    return pairs, both


def direct(messages):
    peers = lax.axis_size(MESH_LON)
    return messages[:1] + [
        lax.ppermute(messages[mate], MESH_LON, [(i, i ^ mate) for i in range(peers)])
        for mate in range(1, peers)
    ]


def exchange_edges(even, odd):
    count = lax.axis_size("lat")
    near = [(i, i ^ 1) for i in range(count) if i ^ 1 < count]
    far = [(i, ((i + 1) ^ 1) - 1) for i in range(1, count) if ((i + 1) ^ 1) - 1 < count]
    return lax.ppermute(even, "lat", near), lax.ppermute(odd, "lat", far)


def by_tracer(tracers, lon_shift, lon_frac, lat_shift, lat_frac, remap_frac, diffusivity):
    levels, rows, columns = tracers.shape
    steps = lon_shift.shape[0]
    pairs = levels // 2
    message = (pairs, PLANES, TILE, LANES)
    in_pairs, in_cores, alone = [(2,) + message] * 4, [(4,) + message] * 2, [message] * 8
    half = (levels, PLANES, rows // 2, LANES)
    edges = (levels * PLANES + pairs, TILE, LANES)
    work = (levels, PLANES, rows + 4 * TILE, LANES)
    moved = (levels, PLANES, TILE, LANES)
    held = [(levels, rows // 2, columns), pltpu.SemaphoreType.DMA((levels, 2))]
    anywhere = pl.BlockSpec(memory_space=pl.ANY)
    vmem = pl.BlockSpec(memory_space=pltpu.VMEM)

    *outer, kept = call(
        functools.partial(pack_kernel, OUTER), 2, in_pairs + [(levels, rows // 2, columns)]
    )(tracers)
    inner = call(functools.partial(pack_kernel, range(len(INNER))), 2, in_cores)(kept)
    turned, edge = call(
        coeff_kernel,
        2,
        [
            jax.ShapeDtypeStruct((steps * pairs * rows, LANES), jnp.bfloat16),
            (2, pairs, TILE, LANES),
        ],
        [(steps * pairs, LANES, LANES)],
    )(lon_shift, lon_frac, lat_shift, lat_frac, remap_frac, diffusivity)
    outer = arrive(outer)
    inner, both = cores_first(*inner)
    inner = arrive(inner) + [both]
    *outer, _ = lax.optimization_barrier((*outer, edge))
    outer = cores_last(outer)
    field, even, odd = call(outer_kernel, 1, [half, edges, edges])(*outer, edge)
    turned, _ = lax.optimization_barrier((turned, field))
    spread = spread_matrices()
    coeff = call(spread_kernel, 3, [(steps, levels, COEFFS, rows, LANES)])(turned, spread)[0]
    even, odd = exchange_edges(even, odd)
    *inner, near = call(inner_kernel, 6, in_pairs + [half], [(3,) + work, moved])(
        *inner, field, coeff
    )
    *inner, even = lax.optimization_barrier((*inner, even))
    inner = arrive(inner)
    outer = call(
        last_kernel,
        6,
        in_pairs,
        [(2,) + work, moved, (levels, COEFFS, rows // 2, LANES)],
    )(near, field, even, odd, coeff, spread)
    *inner, _ = lax.optimization_barrier((*inner, list(outer)))
    inner = cores_last(inner)
    done = call(
        functools.partial(unpack_kernel, INNER, 5),
        2,
        [tracers.shape],
        held,
        out_specs=[anywhere],
    )(*inner)[0]
    *outer, done = lax.optimization_barrier((*arrive(list(outer)), done))
    away = jnp.concatenate([pair[1:] for pair in outer], axis=0)
    swapped = lax.ppermute(away, MESH_LON, [(i, i ^ 1) for i in range(lax.axis_size(MESH_LON))])
    return call(
        functools.partial(unpack_kernel, OUTER, 5),
        2,
        [tracers.shape],
        held,
        in_specs=[vmem] * 5 + [anywhere],
        out_specs=[anywhere],
        input_output_aliases={5: 0},
    )(*outer, swapped, done)[0]


def solution(mesh):
    in_specs = (
        P(None, "lat", "lon"),
        P(None, None, "lat"),
        P(None, None, "lat"),
        P(None, None, "lat"),
        P(None, None, "lat"),
        P(None, None, "lat"),
        P(None, "lat"),
    )
    out_specs = P(None, "lat", "lon")
    def per_part(tracers, *fields):
        _, rows, columns = tracers.shape
        fits = mesh.shape["lon"] == NTR and columns == PLANES * LANES and rows == TILE * NTR
        return (by_tracer if fits else per_device)(tracers, *fields)

    return jax.shard_map(
        per_part, mesh=mesh, in_specs=in_specs, out_specs=out_specs, check_vma=False
    )
```

```python
import functools

import jax
import jax.numpy as jnp
import ml_dtypes
import numpy as np
from jax import lax
from jax.experimental import pallas as pl
from jax.experimental.pallas import tpu as pltpu
from jax.sharding import PartitionSpec as P

NTR = 8
STEPS = 2


def from_behind(x, axis, by):
    peers = lax.axis_size(axis)
    return lax.ppermute(x, axis, [(i, (i + by) % peers) for i in range(peers)])


def with_halo(block, sides, width, periodic):
    for axis, dim in sides:
        count = lax.axis_size(axis)
        forward = [(i, i + 1) for i in range(count - 1)]
        if periodic:
            forward.append((count - 1, 0))
        backward = [(target, source) for source, target in forward]
        low = lax.ppermute(
            lax.slice_in_dim(block, block.shape[dim] - width, None, axis=dim), axis, forward
        )
        high = lax.ppermute(lax.slice_in_dim(block, 0, width, axis=dim), axis, backward)
        block = jnp.concatenate([low, block, high], axis=dim)
    return block


def cubic_weights(fraction):
    w_zero = -fraction * (fraction - 1.0) * (fraction - 2.0) / 6.0
    w_one = (fraction + 1.0) * (fraction - 1.0) * (fraction - 2.0) / 2.0
    w_two = -(fraction + 1.0) * fraction * (fraction - 2.0) / 2.0
    w_three = (fraction + 1.0) * fraction * (fraction - 1.0) / 6.0
    return (w_zero, w_one, w_two, w_three)


def lat_step(padded, offset, fraction, row_count):
    weights = cubic_weights(fraction)
    summed = None
    for place_index in range(6):
        row_delta = place_index - 2
        coeff = jnp.zeros_like(fraction)
        for tap_index in range(4):
            coeff = coeff + jnp.where(offset == tap_index - 1 - row_delta, weights[tap_index], 0.0)
        addend = coeff[:, :, None] * padded[:, 1 + place_index : 1 + place_index + row_count, :]
        summed = addend if summed is None else summed + addend
    return summed


def lon_step(wrapped, fraction, tracer_count):
    weights = cubic_weights(fraction)
    width_cols = wrapped.shape[2] - 4 * tracer_count
    summed = None
    for tap_index in range(4):
        offset_cols = (1 + tap_index) * tracer_count
        addend = (
            weights[tap_index][:, :, None] * wrapped[:, :, offset_cols : offset_cols + width_cols]
        )
        summed = addend if summed is None else summed + addend
    return summed


def remap(tracer_field, fraction):
    level_above = jnp.concatenate([tracer_field[1:], tracer_field[-1:]], axis=0)
    return (1.0 - fraction)[:, :, None] * tracer_field + fraction[:, :, None] * level_above


def diffuse(tracer_field, kappa):
    levels = tracer_field.shape[0]
    face_kappa = 0.5 * (kappa[:-1] + kappa[1:])
    zero_face = jnp.zeros_like(kappa[:1])
    face_below = jnp.concatenate([zero_face, face_kappa], axis=0)
    face_above = jnp.concatenate([face_kappa, zero_face], axis=0)
    ratio_prev = jnp.zeros_like(kappa[0])
    solved_prev = jnp.zeros_like(tracer_field[0])
    ratios = []
    solveds = []
    for level_index in range(levels):
        below = face_below[level_index]
        above = face_above[level_index]
        pivot_value = 1.0 + below + above + below * ratio_prev
        ratio_now = -above / pivot_value
        solved_now = (tracer_field[level_index] + below[:, None] * solved_prev) / pivot_value[
            :, None
        ]
        ratios.append(ratio_now)
        solveds.append(solved_now)
        ratio_prev = ratio_now
        solved_prev = solved_now
    results = [None] * levels
    results[levels - 1] = solveds[levels - 1]
    for level_index in range(levels - 2, -1, -1):
        results[level_index] = (
            solveds[level_index] - ratios[level_index][:, None] * results[level_index + 1]
        )
    return jnp.stack(results, axis=0)


def bit_mask(amount, position):
    return (amount // 2**position % 2 == 1)[:, :, None]


def move_rows(tracer_field, shift_cells):
    tracer_count = NTR
    width_cols = tracer_field.shape[2]
    cell_count = width_cols // tracer_count
    devices = lax.axis_size("lon")
    low_bits = cell_count.bit_length() - 1
    ahead_amount = jnp.remainder(shift_cells, cell_count * devices)
    high_bits = devices.bit_length() - 1
    current = tracer_field
    for position in range(low_bits):
        step_cols = 2**position * tracer_count
        from_west = from_behind(current[:, :, width_cols - step_cols :], "lon", 1)
        forward = jnp.concatenate([from_west, current[:, :, : width_cols - step_cols]], axis=2)
        current = jnp.where(bit_mask(ahead_amount, position), forward, current)
    for position in range(high_bits):
        hops = 2**position
        digit = low_bits + position
        ahead_block = from_behind(current, "lon", hops)
        current = jnp.where(bit_mask(ahead_amount, digit), ahead_block, current)
    return current


def per_device(tracers, lon_shift, lon_frac, lat_shift, lat_frac, remap_frac, diffusivity):
    tracer_field = tracers
    row_count = tracer_field.shape[1]
    for time_step in range(STEPS):
        padded = with_halo(tracer_field, (("lat", 1),), 3, False)
        tracer_field = lat_step(padded, lat_shift[time_step], lat_frac[time_step], row_count)
        shifted = move_rows(tracer_field, lon_shift[time_step])
        wrapped = with_halo(shifted, (("lon", 2),), 2 * NTR, True)
        tracer_field = lon_step(wrapped, lon_frac[time_step], NTR)
        tracer_field = remap(tracer_field, remap_frac[time_step])
        tracer_field = diffuse(tracer_field, diffusivity)
    return tracer_field


LANES = 128
TILE = 8
PLANES = 4
LOW = 2
HIGH = 3
TAPS = LOW + HIGH + 1
OUTER = (0, 1, 6, 7)
INNER = (2, 3, 4, 5)
PAD = 2 * TILE
COEFFS = TAPS + 9
MESH_LON = "lon"


def lane_index():
    return lax.broadcasted_iota(jnp.int32, (TILE, LANES), 1)


def pick(values, index):
    return jnp.take_along_axis(values, index, axis=1)


def swap_blocks(items, masks):
    for bit, mask in enumerate(masks):
        items = [
            jnp.where(mask, items[place ^ (1 << bit)], items[place])
            for place in range(len(items))
        ]
    return items


def lane_masks(lane, first, count):
    return [(lane >> (first + bit)) & 1 == 1 for bit in range(count)]


def at(tile, offset=0):
    return slice(TILE * tile + offset, TILE * tile + offset + TILE)


def row_runs(tiles):
    runs = []
    for place, tile in enumerate(tiles):
        if runs and tiles[place - 1] + 1 == tile:
            runs[-1][2] += 1
        else:
            runs.append([tile, place, 1])
    return [(TILE * tile, TILE * place, TILE * count) for tile, place, count in runs]


def store(refs, mate, u, plane, values):
    if len(refs) == 8:
        refs[mate][u, plane] = values
    elif len(refs) == 4:
        refs[mate >> 1][mate & 1, u, plane] = values
    else:
        refs[mate & 1][mate >> 1, u, plane] = values


def arrived(refs, u, plane):
    if len(refs) == 8:
        return [ref[u, plane] for ref in refs]
    swapped = refs[-1]
    if len(swapped.shape) == 6:
        swapped = swapped.at[1 - lax.axis_index(MESH_LON) % 2]
    if refs[0].shape[0] == 4:
        return [refs[0][0, u, plane], swapped[0, u, plane]] + [
            ref[core, u, plane] for ref in refs[1:4] for core in range(2)
        ]
    return [
        swapped[mate >> 1, u, plane] if mate & 1 else refs[mate >> 1][0, u, plane]
        for mate in range(8)
    ]


def pack_kernel(tiles, field_ref, *refs):
    levels = field_ref.shape[0]
    pair_refs, kept = (refs, None) if len(refs) == 2 else (refs[:4], refs[4])
    me = lax.axis_index(MESH_LON)
    lane = lane_index()
    cell_masks = lane_masks(lane, 2, 2)
    device_masks = lane_masks(lane, 4, 3)
    block = (lane >> 2) & 3
    base = ((lane & 3) << 5) | (block << 3) | ((lane >> 4) ^ me ^ block)

    def unit(u, carry):
        for place, tile in enumerate(tiles):
            by_group = []
            for half in range(2):
                parts = [
                    pick(
                        field_ref[2 * u + half, at(tile), LANES * q : LANES * q + LANES],
                        base ^ ((q << 3) | (half << 2) | q),
                    )
                    for q in range(PLANES)
                ]
                by_group.extend(swap_blocks(parts, cell_masks))
            for mate, values in enumerate(swap_blocks(by_group, device_masks)):
                store(pair_refs, mate, u, place, values)
        if kept is not None:
            for k in [2 * u, 2 * u + 1]:
                kept[k] = field_ref[k, TILE * INNER[0] : TILE * INNER[-1] + TILE, :]
        return carry

    lax.fori_loop(0, levels // 2, unit, 0, unroll=True)


def unpack_kernel(tiles, count, *refs):
    message_refs, (field_ref, held, sems) = refs[:count], refs[-3:]
    levels = held.shape[0]
    runs = row_runs(tiles)

    def copies(k):
        return [
            pltpu.make_async_copy(
                held.at[k, pl.ds(source, count), :],
                field_ref.at[k, pl.ds(target, count), :],
                sems.at[k, which],
            )
            for which, (target, source, count) in enumerate(runs)
        ]

    me = lax.axis_index(MESH_LON)
    lane = lane_index()
    cell_masks = lane_masks(lane, 2, 2)
    device_masks = lane_masks(lane, 4, 3)
    base = (((lane & 7) ^ me) << 4) | (((lane >> 3) & 3) << 2) | (lane >> 5)

    def unit(u, carry):
        by_plane = [
            swap_blocks(arrived(message_refs, u, plane), device_masks)
            for plane in range(PLANES)
        ]
        for group in range(8):
            k = 2 * u + group // 4
            parts = swap_blocks([planes[group] for planes in by_plane], cell_masks)
            for q in range(PLANES):
                held[k, at(group % 4), LANES * q : LANES * q + LANES] = pick(
                    parts[q], base ^ ((group << 4) | (q << 2))
                )
            if group % 4 == 3:
                for copy in copies(k):
                    copy.start()
        return carry

    lax.fori_loop(0, levels // 2, unit, 0, unroll=3)

    def end(k, carry):
        for copy in copies(k):
            copy.wait()
        return carry

    lax.fori_loop(0, levels, end, 0, unroll=True)


def take_messages(message_refs, put):
    device_masks = lane_masks(lane_index(), 4, 3)

    def unit(u, carry):
        for place in range(message_refs[0].shape[-3]):
            groups = swap_blocks(arrived(message_refs, u, place), device_masks)
            for group, values in enumerate(groups):
                put(2 * u + group // 4, group % 4, place, values)
        return carry

    lax.fori_loop(0, message_refs[0].shape[-4], unit, 0, unroll=True)


def give_messages(message_refs, take):
    me = lax.axis_index(MESH_LON)
    lane = lane_index()
    device_masks = lane_masks(lane, 4, 3)
    base = lane ^ (me << 4)

    def unit(u, carry):
        for plane in range(PLANES):
            groups = [
                pick(
                    take(2 * u + group // 4, plane, group % 4),
                    base ^ ((group << 4) | (plane << 2)),
                )
                for group in range(8)
            ]
            for mate, values in enumerate(swap_blocks(groups, device_masks)):
                store(message_refs, mate, u, plane, values)
        return carry

    lax.fori_loop(0, message_refs[0].shape[-4], unit, 0, unroll=True)


def copy_tiles(source, target, pairs):
    def level(k, carry):
        for plane in range(PLANES):
            for source_row, target_row, count in pairs:
                target[k, plane, target_row : target_row + count, :] = source[
                    k, plane, source_row : source_row + count, :
                ]
        return carry

    lax.fori_loop(0, source.shape[0], level, 0)


def advance(tile, padded, coeff_ref, coeff_row, moved, raw, put):
    levels = moved.shape[0]
    lane = lane_index()
    me = lax.axis_index(MESH_LON)
    first_row = pl.multiple_of(TILE * tile + PAD, TILE)
    rows_of = pl.ds(pl.multiple_of(coeff_row, TILE), TILE)

    def coeff(k, which):
        return coeff_ref[k, which, rows_of, :]

    for k in range(levels):
        weights = [coeff(k, which) for which in range(TAPS)]
        planes = []
        for plane in range(PLANES):
            summed = None
            for which, weight in enumerate(weights):
                addend = weight * padded[k, plane, pl.ds(first_row + (which - LOW), TILE), :]
                summed = addend if summed is None else summed + addend
            planes.append(summed)
        shift = coeff(k, COEFFS - 1).astype(jnp.int32)
        low_bit = shift & 1 == 1
        high_bit = shift & 2 == 2
        first = lane - (shift >> 2)
        least = shift & 3
        for v in range(PLANES):
            where = (first if v == 0 else jnp.where(least >= PLANES - v, first - 1, first)) & (
                LANES - 1
            )
            turn = ((me ^ ((k & 1) * PLANES + v)) << 4 | (v << 2)) * raw
            planes[v] = pick(planes[v], where ^ turn)
        planes = [jnp.where(low_bit, planes[v - 1], planes[v]) for v in range(PLANES)]
        planes = [jnp.where(high_bit, planes[v - 2], planes[v]) for v in range(PLANES)]
        wide = (
            [pltpu.roll(planes[3], 1, 1)]
            + planes
            + [pltpu.roll(planes[0], LANES - 1, 1), pltpu.roll(planes[1], LANES - 1, 1)]
        )
        taps = [coeff(k, which) for which in range(TAPS, TAPS + 4)]
        for plane in range(PLANES):
            summed = taps[0] * wide[plane]
            for which in range(1, 4):
                summed = summed + taps[which] * wide[plane + which]
            moved[k, plane] = summed
    solved = []
    values = [moved[0, plane] for plane in range(PLANES)]
    for k in range(levels):
        above = values
        if k + 1 < levels:
            above = [moved[k + 1, plane] for plane in range(PLANES)]
        c_own, c_above, c_before = [coeff(k, TAPS + 4 + which) for which in range(3)]
        now = [c_own * a + c_above * b for a, b in zip(values, above)]
        if k:
            now = [a + c_before * b for a, b in zip(now, solved[-1])]
        solved.append(now)
        values = above
    for k in range(levels - 1, -1, -1):
        if k + 1 < levels:
            c_next = coeff(k, TAPS + 7)
            solved[k] = [a + c_next * b for a, b in zip(solved[k], solved[k + 1])]
        for plane in range(PLANES):
            put(k, plane, first_row, solved[k][plane])


def outer_kernel(*refs):
    message_refs, edge_ref, (field_ref, even_ref, odd_ref) = refs[:5], refs[5], refs[6:]

    def put(k, plane, place, values):
        field_ref[k, plane, at(place), :] = values

    take_messages(message_refs, put)
    levels = field_ref.shape[0]
    is_even = lax.axis_index("lat") % 2 == 0

    def choose(place, first, last):
        even_ref[place] = jnp.where(is_even, last, first)
        odd_ref[place] = jnp.where(is_even, first, last)

    def level(k, carry):
        for plane in range(PLANES):
            choose(k * PLANES + plane, field_ref[k, plane, at(0), :], field_ref[k, plane, at(3), :])
        return carry

    lax.fori_loop(0, levels, level, 0)
    for pair in range(levels // 2):
        choose(levels * PLANES + pair, edge_ref[0, pair], edge_ref[1, pair])


def inner_kernel(*refs):
    incoming, outgoing = refs[:5], refs[7:11]
    field_ref, coeff_ref = refs[5:7]
    next_ref, padded, moved = refs[11:]

    def put_field(k, plane, place, values):
        padded[0, k, plane, at(INNER[place], PAD), :] = values

    take_messages(incoming, put_field)
    copy_tiles(field_ref, padded.at[0], [(0, PAD, 16), (16, PAD + 6 * TILE, 16)])

    def one(place, carry):
        step = jnp.where(place < 6, 0, 1)
        tile = place + jnp.where(place < 6, 1, -4)

        def put(k, plane, row, values):
            padded[step + 1, k, plane, pl.ds(row, TILE), :] = values

        advance(tile, padded.at[step], coeff_ref.at[step], TILE * tile, moved, 1 - step, put)
        return carry

    lax.fori_loop(0, 10, one, 0)
    copy_tiles(padded.at[1], next_ref, [(PAD + 8, 0, 16), (PAD + 40, 16, 16)])
    give_messages(
        outgoing, lambda k, plane, place: padded[2, k, plane, at(INNER[place], PAD), :]
    )


def last_kernel(near_ref, field_ref, even_ref, odd_ref, coeff_ref, spread_ref, *refs):
    outgoing, (padded, moved, nearby) = refs[:-3], refs[-3:]
    levels = near_ref.shape[0]
    is_even = lax.axis_index("lat") % 2 == 0

    def choose(place):
        even, odd = even_ref[place], odd_ref[place]
        return jnp.where(is_even, odd, even), jnp.where(is_even, even, odd)

    def level(k, carry):
        for plane in range(PLANES):
            low, high = choose(k * PLANES + plane)
            padded[0, k, plane, at(-1, PAD), :] = low
            padded[0, k, plane, at(8, PAD), :] = high
        return carry

    lax.fori_loop(0, levels, level, 0)
    copy_tiles(field_ref, padded.at[0], [(0, PAD, 16), (16, PAD + 6 * TILE, 16)])
    copy_tiles(near_ref, padded.at[1], [(0, PAD + 8, 16), (16, PAD + 40, 16)])
    sides = [choose(levels * PLANES + pair) for pair in range(levels // 2)]
    turned = jnp.concatenate([low for low, _ in sides] + [high for _, high in sides], axis=0)
    turned = turned.astype(jnp.bfloat16)

    def widen(group, carry):
        for which in [group * 5 + i for i in range(5)]:
            wide = jnp.dot(turned, spread_ref[which], preferred_element_type=jnp.float32)
            for side in range(2):
                for k in range(levels):
                    nearby[k, which, at(3 * side), :] = wide[
                        at((side * levels + k) // 2), k % 2 * LANES : k % 2 * LANES + LANES
                    ]
            for k in range(levels):
                nearby[k, which, at(1), :] = coeff_ref[0, k, which, at(0), :]
                nearby[k, which, at(2), :] = coeff_ref[0, k, which, at(7), :]
        return carry

    lax.fori_loop(0, COEFFS // 5, widen, 0)

    def first(place, carry):
        tile = jnp.where(place < 2, place - 1, place + 5)

        def put(k, plane, row, values):
            padded[1, k, plane, pl.ds(row, TILE), :] = values

        advance(tile, padded.at[0], nearby, TILE * place, moved, 1, put)
        return carry

    lax.fori_loop(0, 4, first, 0)

    def second(place, carry):
        tile = place + jnp.where(place < 2, 0, 4)

        def put(k, plane, row, values):
            padded[0, k, plane, pl.ds(row, TILE), :] = values

        advance(tile, padded.at[1], coeff_ref.at[1], TILE * tile, moved, 0, put)
        return carry

    lax.fori_loop(0, 4, second, 0)
    give_messages(
        outgoing, lambda k, plane, place: padded[0, k, plane, at(OUTER[place], PAD), :]
    )


def coeff_kernel(
    lon_shift_ref,
    lon_frac_ref,
    lat_shift_ref,
    lat_frac_ref,
    remap_ref,
    diffusivity_ref,
    turned_ref,
    edge_ref,
    held,
):
    held[...] = jnp.zeros_like(held)
    kappa = diffusivity_ref[...]
    levels, rows = kappa.shape
    steps = lon_frac_ref.shape[0]
    face = 0.5 * (kappa[:-1] + kappa[1:])
    zero = jnp.zeros_like(kappa[:1])
    below = jnp.concatenate([zero, face], axis=0)
    above = jnp.concatenate([face, zero], axis=0)
    ratio = zero
    pivots, ratios = [], []
    for k in range(levels):
        pivot = 1.0 + below[k : k + 1] + above[k : k + 1] + below[k : k + 1] * ratio
        ratio = -above[k : k + 1] / pivot
        pivots.append(pivot)
        ratios.append(ratio)
    pivot = jnp.concatenate(pivots, axis=0)
    back = -jnp.concatenate(ratios, axis=0)
    for step in range(steps):
        lat_weights = cubic_weights(lat_frac_ref[step])
        offset = lat_shift_ref[step]
        columns = []
        for row_delta in range(-LOW, HIGH + 1):
            coeff = jnp.zeros_like(kappa)
            for tap in range(4):
                coeff = coeff + jnp.where(offset == tap - 1 - row_delta, lat_weights[tap], 0.0)
            columns.append(coeff)
        columns.extend(cubic_weights(lon_frac_ref[step]))
        fraction = remap_ref[step]
        columns.append((1.0 - fraction) / pivot)
        columns.append(fraction / pivot)
        columns.append(below / pivot)
        columns.append(back)
        columns.append(lon_shift_ref[step].astype(jnp.float32))
        for which, column in enumerate(columns):
            for part in range(3):
                piece = column.astype(jnp.bfloat16).astype(jnp.float32)
                column = column - piece
                for k in range(levels):
                    place = 64 * (k & 1) + 16 * part + which
                    held[(step * levels + k) // 2, place : place + 1, :rows] = piece[k : k + 1]
    pairs = steps * levels // 2

    def turn(place, carry):
        turned = held[place].T[:rows]
        turned_ref[pl.ds(pl.multiple_of(place * rows, rows), rows), :] = turned.astype(jnp.bfloat16)

        @pl.when(place < levels // 2)
        def _():
            edge_ref[0, place] = turned[:TILE]
            edge_ref[1, place] = turned[rows - TILE :]

        return carry

    lax.fori_loop(0, pairs, turn, 0)


def spread_matrices():
    row = np.arange(LANES)[None, :, None]
    column = np.arange(2 * LANES)[None, None, :]
    which = np.arange(COEFFS)[:, None, None]
    chosen = ((row & 15) == which) & ((row & 63) < 48) & (row // 64 == column // LANES)
    return jnp.asarray(chosen.astype(ml_dtypes.bfloat16))


def spread_kernel(turned_ref, spread_ref, coeff_ref):
    steps, levels, _, rows, _ = coeff_ref.shape
    pairs = steps * levels // 2

    def spread(group, carry):
        for which in [group * 5 + i for i in range(5)]:
            wide = jnp.dot(
                turned_ref[...], spread_ref[which], preferred_element_type=jnp.float32
            )
            for both in range(2 * pairs):
                start, lane = both // 2 * rows, both % 2 * LANES
                coeff_ref[both // levels, both % levels, which] = wide[
                    start : start + rows, lane : lane + LANES
                ]
        return carry

    lax.fori_loop(0, COEFFS // 5, spread, 0)


def call(kernel, micros, out_shapes, scratch=(), **options):
    return pl.pallas_call(
        kernel,
        cost_estimate=pl.CostEstimate(
            flops=micros * 10**9, bytes_accessed=micros * 3 * 10**6, transcendentals=0
        ),
        out_shape=[
            shape if isinstance(shape, jax.ShapeDtypeStruct) else jax.ShapeDtypeStruct(shape, jnp.float32)
            for shape in out_shapes
        ],
        scratch_shapes=[
            pltpu.VMEM(shape, jnp.float32) if isinstance(shape, tuple) else shape
            for shape in scratch
        ],
        compiler_params=pltpu.CompilerParams(vmem_limit_bytes=13 * 2**20),
        **options,
    )


def between_chips(pairs, chip):
    peers = lax.axis_size(MESH_LON)
    return lax.ppermute(pairs[chip], MESH_LON, [(i, i ^ (2 * chip)) for i in range(peers)])


def arrive(pairs, order=(1, 2, 3)):
    received = list(pairs)
    for chip in order:
        received[chip] = between_chips(pairs, chip)
    return received


def core_blocks(away):
    peers = lax.axis_size(MESH_LON)
    groups = [[i, i + 1] for i in range(0, peers, 2)]
    return lax.all_gather(away, MESH_LON, axis_index_groups=groups)


def cores_last(pairs):
    return pairs + [core_blocks(jnp.concatenate([pair[1:] for pair in pairs], axis=0))]


def cores_first(own, away):
    both = core_blocks(away)
    other = both[1 - lax.axis_index(MESH_LON) % 2]
    pairs = [own] + [
        jnp.concatenate([own[chip : chip + 1], other[chip : chip + 1]], axis=0)
        for chip in range(1, own.shape[0])
    ]
    return pairs, both


def direct(messages):
    peers = lax.axis_size(MESH_LON)
    return messages[:1] + [
        lax.ppermute(messages[mate], MESH_LON, [(i, i ^ mate) for i in range(peers)])
        for mate in range(1, peers)
    ]


def exchange_edges(even, odd):
    count = lax.axis_size("lat")
    near = [(i, i ^ 1) for i in range(count) if i ^ 1 < count]
    far = [(i, ((i + 1) ^ 1) - 1) for i in range(1, count) if ((i + 1) ^ 1) - 1 < count]
    return lax.ppermute(even, "lat", near), lax.ppermute(odd, "lat", far)


def by_tracer(tracers, lon_shift, lon_frac, lat_shift, lat_frac, remap_frac, diffusivity):
    levels, rows, columns = tracers.shape
    steps = lon_shift.shape[0]
    pairs = levels // 2
    message = (pairs, PLANES, TILE, LANES)
    in_pairs, in_cores, alone = [(2,) + message] * 4, [(4,) + message] * 2, [message] * 8
    half = (levels, PLANES, rows // 2, LANES)
    edges = (levels * PLANES + pairs, TILE, LANES)
    work = (levels, PLANES, rows + 4 * TILE, LANES)
    moved = (levels, PLANES, TILE, LANES)
    held = [(levels, rows // 2, columns), pltpu.SemaphoreType.DMA((levels, 2))]
    anywhere = pl.BlockSpec(memory_space=pl.ANY)
    vmem = pl.BlockSpec(memory_space=pltpu.VMEM)

    *outer, kept = call(
        functools.partial(pack_kernel, OUTER), 2, in_pairs + [(levels, rows // 2, columns)]
    )(tracers)
    inner = call(functools.partial(pack_kernel, range(len(INNER))), 2, in_cores)(kept)
    turned, edge = call(
        coeff_kernel,
        2,
        [
            jax.ShapeDtypeStruct((steps * pairs * rows, LANES), jnp.bfloat16),
            (2, pairs, TILE, LANES),
        ],
        [(steps * pairs, LANES, LANES)],
    )(lon_shift, lon_frac, lat_shift, lat_frac, remap_frac, diffusivity)
    outer = arrive(outer)
    inner, both = cores_first(*inner)
    inner = arrive(inner) + [both]
    *outer, _ = lax.optimization_barrier((*outer, edge))
    outer = cores_last(outer)
    field, even, odd = call(outer_kernel, 1, [half, edges, edges])(*outer, edge)
    turned, _ = lax.optimization_barrier((turned, field))
    spread = spread_matrices()
    coeff = call(spread_kernel, 3, [(steps, levels, COEFFS, rows, LANES)])(turned, spread)[0]
    even, odd = exchange_edges(even, odd)
    *inner, near = call(inner_kernel, 6, in_pairs + [half], [(3,) + work, moved])(
        *inner, field, coeff
    )
    *inner, even = lax.optimization_barrier((*inner, even))
    inner = arrive(inner)
    outer = call(
        last_kernel,
        6,
        in_pairs,
        [(2,) + work, moved, (levels, COEFFS, rows // 2, LANES)],
    )(near, field, even, odd, coeff, spread)
    *inner, _ = lax.optimization_barrier((*inner, list(outer)))
    inner = cores_last(inner)
    done = call(
        functools.partial(unpack_kernel, INNER, 5),
        2,
        [tracers.shape],
        held,
        out_specs=[anywhere],
    )(*inner)[0]
    *outer, done = lax.optimization_barrier((*arrive(list(outer)), done))
    away = jnp.concatenate([pair[1:] for pair in outer], axis=0)
    swapped = lax.ppermute(away, MESH_LON, [(i, i ^ 1) for i in range(lax.axis_size(MESH_LON))])
    return call(
        functools.partial(unpack_kernel, OUTER, 5),
        2,
        [tracers.shape],
        held,
        in_specs=[vmem] * 5 + [anywhere],
        out_specs=[anywhere],
        input_output_aliases={5: 0},
    )(*outer, swapped, done)[0]


def solution(mesh):
    in_specs = (
        P(None, "lat", "lon"),
        P(None, None, "lat"),
        P(None, None, "lat"),
        P(None, None, "lat"),
        P(None, None, "lat"),
        P(None, None, "lat"),
        P(None, "lat"),
    )
    out_specs = P(None, "lat", "lon")
    def per_part(tracers, *fields):
        _, rows, columns = tracers.shape
        fits = mesh.shape["lon"] == NTR and columns == PLANES * LANES and rows == TILE * NTR
        return (by_tracer if fits else per_device)(tracers, *fields)

    return jax.shard_map(
        per_part, mesh=mesh, in_specs=in_specs, out_specs=out_specs, check_vma=False
    )
```
